32 devices in a mesh: dp: 8 (over z, core), tensor: 4 (over y, x).
Axes of the slice: x: 2, y: 2, z: 4, core: 2. Of those that a mesh axis runs over, the one named last changes fastest.
Arguments:
- tokens: bfloat16 [8192, 1024], P('dp'), may hold values from -6 to 6
- segment: int32 [8, 1024], P('dp'), may hold values from 0 to 3, never falling along the last dimension, each value on 1 to 512 neighbouring positions
- attn_gain: float32 [1024], replicated, may hold values from 0.5 to 1.5
- attn_shift: float32 [1024], replicated, may hold values from -1.5 to 1.5
- mlp_gain: float32 [1024], replicated, may hold values from 0.5 to 1.5
- mlp_shift: float32 [1024], replicated, may hold values from -1.5 to 1.5
- w_qkv: bfloat16 [1024, 3072], P(None, 'tensor'), may hold values from -0.1875 to 0.1875
- b_qkv: float32 [3072], P('tensor'), may hold values from -1.5 to 1.5
- w_out: bfloat16 [1024, 1024], P('tensor'), may hold values from -1.5 to 1.5
- w_up: bfloat16 [1024, 4096], P(None, 'tensor'), may hold values from -0.1875 to 0.1875
- b_up: float32 [4096], P('tensor'), may hold values from -1.5 to 1.5
- w_down: bfloat16 [4096, 1024], P('tensor'), may hold values from -0.09375 to 0.09375
- b_branch: float32 [1024], replicated, may hold values from -1.5 to 1.5
- cotangent: bfloat16 [8192, 1024], P('dp'), may hold values from -6 to 6
Outputs:
- result: bfloat16 [8192, 1024], P('dp')
- d_tokens: float32 [8192, 1024], P('dp')
- d_w_qkv: float32 [1024, 3072], P(None, 'tensor')
- d_b_qkv: float32 [3072], P('tensor')
- d_w_out: float32 [1024, 1024], P('tensor')
- d_w_up: float32 [1024, 4096], P(None, 'tensor')
- d_b_up: float32 [4096], P('tensor')
- d_w_down: float32 [4096, 1024], P('tensor')
- d_b_branch: float32 [1024], replicated
- d_attn_gain: float32 [1024], replicated
- d_attn_shift: float32 [1024], replicated
- d_mlp_gain: float32 [1024], replicated
- d_mlp_shift: float32 [1024], replicated
The draws below stay inside these ranges and needn't reach their ends.
Inputs may be any that keep to these rules, and one draw needn't show every extreme that they name: Within each sequence segment numbers never fall; each document holds 1 to 512 tokens.
All inputs are finite; a program needn't handle non-finite values.
Results may differ from the reference program's by a relative error of at most 0.012.
Values sent between devices are 32-bit elements; how exact they have to be, the bound alone decides.
No kernel may reach another device: no remote copies, remote signals or barrier semaphores. Data moves between devices by JAX's collectives and lax.ppermute only.
A program may use at most 128 MiB of HBM per device.

```python
import math
import jax
import jax.numpy as jnp
import numpy as np
from jax import lax

D = 1024
HEADS = 16
HD = 64
ROT = 16
FF = 4096
SEQ = 1024
NSEQ = 8
TOKENS = 8192


def levels(key, extent, pieces, least, top_value):
    gain = 1.0
    for dim, blocks in pieces:
        heights = jax.random.uniform(jax.random.fold_in(jax.random.fold_in(key, 6), dim), (blocks,), jnp.float32, least / len(pieces), top_value / len(pieces))
        gain = gain * jnp.repeat(jnp.exp(heights), extent[dim] // blocks).reshape((-1,) + (1,) * (len(extent) - 1 - dim))
    return gain


def split_up(number_of, total, limit, lean):
    loads = [(1 << 20) // math.isqrt(standing ** lean) + 1 for standing in range(2, number_of + 1)]
    surplus, counts = total - limit - (number_of - 1), [1] * (number_of - 1)
    while surplus > 0:
        candidates = [i for i in range(number_of - 1) if counts[i] < limit]
        whole, left = sum([loads[i] for i in candidates]), surplus
        for i in candidates:
            more = min(limit - counts[i], max(1, left * loads[i] // whole), surplus)
            counts[i] = counts[i] + more
            surplus = surplus - more
    return np.array([limit] + counts)


def uneven_parts(key, number_of, total, bound, lean):
    if number_of == 2:
        one = jax.random.randint(key, (), max(1, total - bound), min(bound, total - 1) + 1)
        return jnp.stack([one, total - one])
    tallies = jnp.asarray(split_up(number_of, total, bound, lean), jnp.int32)
    twos = (number_of - 1) // 2
    source_of, receiver = tallies[1:1 + 2 * twos:2], tallies[2:2 + 2 * twos:2]
    margin = jnp.minimum(source_of - 1, bound - receiver)
    passed = jax.random.randint(jax.random.fold_in(key, 1), (twos,), 0, 1 << 20) % (margin + 1)
    tallies = tallies.at[1:1 + 2 * twos:2].set(source_of - passed).at[2:2 + 2 * twos:2].set(receiver + passed)
    return tallies[jax.random.permutation(jax.random.fold_in(key, 2), number_of)]


def bell_draw(rng, extent, width, most, pieces=(), kind=jnp.bfloat16):
    drawn = width * jax.random.normal(rng, extent, jnp.float32)
    if pieces:
        drawn = drawn * levels(rng, extent, pieces, -0.22, 0.18)
    return jnp.clip(drawn, -most, most).astype(kind)


def setup_inputs(seed: int = 0) -> dict:
    splits = jax.random.split(jax.random.key(seed), 15)
    return {
        "tokens": bell_draw(splits[0], (TOKENS, D), 1.0, 6.0, ((0, 8),)),
        "segment": jax.vmap(lambda own: jnp.searchsorted(jnp.cumsum(uneven_parts(own, 4, SEQ, SEQ // 2, 0)), jnp.arange(SEQ), side="right"))(jax.random.split(splits[1], NSEQ)).reshape((NSEQ, SEQ)).astype(jnp.int32),
        "attn_gain": jnp.clip(1.0 + 0.1 * jax.random.normal(splits[2], (D,), jnp.float32), 0.5, 1.5),
        "attn_shift": bell_draw(splits[3], (D,), 0.3, 1.5, (), jnp.float32),
        "mlp_gain": jnp.clip(1.0 + 0.1 * jax.random.normal(splits[4], (D,), jnp.float32), 0.5, 1.5),
        "mlp_shift": bell_draw(splits[5], (D,), 0.3, 1.5, (), jnp.float32),
        "w_qkv": bell_draw(splits[6], (D, HEADS * 3 * HD), D ** -0.5, 0.1875, ((1, 4),)),
        "b_qkv": bell_draw(splits[7], (HEADS * 3 * HD,), 0.3, 1.5, ((0, 4),), jnp.float32),
        "w_out": bell_draw(splits[8], (HEADS * HD, D), (HEADS * HD // 64) ** -0.5, 1.5, ((0, 4),)),
        "w_up": bell_draw(splits[9], (D, FF), D ** -0.5, 0.1875, ((1, 4),)),
        "b_up": bell_draw(splits[10], (FF,), 0.3, 1.5, ((0, 4),), jnp.float32),
        "w_down": bell_draw(splits[11], (FF, D), FF ** -0.5, 0.09375, ((0, 4),)),
        "b_branch": bell_draw(splits[12], (D,), 0.3, 1.5, (), jnp.float32),
        "cotangent": bell_draw(splits[13], (TOKENS, D), 1.0, 6.0, ((0, 8),)),
    }


EPS = 1e-05
NEG = -1e+30

@jax.custom_vjp
def low(v):
    return lax.optimization_barrier(v.astype(jnp.bfloat16)).astype(jnp.float32)

@jax.custom_vjp
def low_back(v):
    return v

def low_keep(v):
    return (low(v), None)

def low_pass(kept, grad):
    return (grad,)

def back_keep(v):
    return (v, None)

def back_low(kept, grad):
    return (low(grad),)
low.defvjp(low_keep, low_pass)
low_back.defvjp(back_keep, back_low)

def matmul(first_mat, second_mat):
    return jnp.dot(first_mat, second_mat, precision=lax.Precision.HIGHEST)

def layer_norm(token_rows, ln_gain, ln_shift):
    row_mean = lax.optimization_barrier(jnp.mean(token_rows, axis=-1, keepdims=True))
    centred = token_rows - row_mean
    spread = lax.optimization_barrier(jnp.mean(centred * centred, axis=-1, keepdims=True))
    return centred * lax.rsqrt(spread + EPS) * ln_gain + ln_shift

def rotary_tables(segment):
    spots = lax.broadcasted_iota(jnp.int32, segment.shape, 1)
    opening = jnp.concatenate([jnp.ones((segment.shape[0], 1), jnp.bool_), segment[:, 1:] != segment[:, :-1]], axis=1)
    starts = lax.cummax(jnp.where(opening, spots, 0), axis=1)
    offsets = (spots - starts).astype(jnp.float32)
    frequency = 10000.0 ** (-2.0 * jnp.arange(ROT // 2, dtype=jnp.float32) / ROT)
    angles = offsets[:, :, None, None] * frequency
    return (jnp.cos(angles), jnp.sin(angles))

def rotate_pair(vectors, cosine, sine):
    half_rot = cosine.shape[-1]
    first = vectors[..., :half_rot]
    second = vectors[..., half_rot:2 * half_rot]
    remain = vectors[..., 2 * half_rot:]
    return jnp.concatenate([first * cosine - second * sine, second * cosine + first * sine, remain], axis=-1)

def attend_one(query_seq, key_seq, value_seq, segment_row):
    raw = jnp.einsum('qhd,khd->hqk', query_seq, key_seq, precision=lax.Precision.HIGHEST) * HD ** (-0.5)
    raw = low_back(raw)
    spots = jnp.arange(SEQ)
    allowed = (spots[None, :] <= spots[:, None]) & (segment_row[:, None] == segment_row[None, :])
    masked = jnp.where(allowed[None], raw, NEG)
    row_max = lax.optimization_barrier(jnp.max(masked, axis=-1, keepdims=True))
    exponent = jnp.exp(masked - row_max)
    attn_probs = low(exponent / lax.optimization_barrier(jnp.sum(exponent, axis=-1, keepdims=True)))
    return jnp.einsum('hqk,khd->qhd', attn_probs, value_seq, precision=lax.Precision.HIGHEST)

def forward(token_rows, segment, attn_gain, attn_shift, mlp_gain, mlp_shift, w_qkv, b_qkv, w_out, w_up, b_up, w_down, b_branch):
    count_seq = segment.shape[0]
    attn_low = low(layer_norm(token_rows, attn_gain, attn_shift))
    mlp_low = low(layer_norm(token_rows, mlp_gain, mlp_shift))
    projected = low_back(matmul(attn_low, w_qkv) + b_qkv)
    grouped = projected.reshape(count_seq, SEQ, HEADS, 3, HD)
    cosine, sine = rotary_tables(segment)
    queries = low(rotate_pair(grouped[:, :, :, 0], cosine, sine))
    keys_rot = low(rotate_pair(grouped[:, :, :, 1], cosine, sine))
    values = low(grouped[:, :, :, 2])
    attended = lax.map(jax.checkpoint(lambda packed: attend_one(*packed)), (queries, keys_rot, values, segment))
    attended = low(low_back(attended)).reshape(count_seq * SEQ, HEADS * HD)
    attn_part = matmul(attended, w_out)
    pre_act = low_back(matmul(mlp_low, w_up) + b_up)
    hidden = low(jax.nn.gelu(pre_act, approximate=False))
    mlp_part = matmul(hidden, w_down)
    return token_rows + attn_part + mlp_part + b_branch

def reference(tokens, segment, attn_gain, attn_shift, mlp_gain, mlp_shift, w_qkv, b_qkv, w_out, w_up, b_up, w_down, b_branch, cotangent):
    primal = (tokens.astype(jnp.float32), attn_gain.astype(jnp.float32), attn_shift.astype(jnp.float32), mlp_gain.astype(jnp.float32), mlp_shift.astype(jnp.float32), w_qkv.astype(jnp.float32), b_qkv.astype(jnp.float32), w_out.astype(jnp.float32), w_up.astype(jnp.float32), b_up.astype(jnp.float32), w_down.astype(jnp.float32), b_branch.astype(jnp.float32))

    def closed(*params):
        return forward(params[0], segment, *params[1:])
    result, pull_back = jax.vjp(closed, *primal)
    gradients = pull_back(cotangent.astype(jnp.float32))
    return (result.astype(jnp.bfloat16), gradients[0], gradients[5], gradients[6], gradients[7], gradients[8], gradients[9], gradients[10], gradients[11], gradients[1], gradients[2], gradients[3], gradients[4])
```

```python
import math

import jax
import jax.numpy as jnp
from jax import lax
from jax.sharding import PartitionSpec as P

HD = 64
ROT = 16

EPS = 1e-05
NEG = -1e30


def inner_rows(first_mat, second_mat):
    return lax.dot_general(
        first_mat, second_mat, (((0,), (0,)), ((), ())), preferred_element_type=jnp.float32
    )


def times_trans(first_mat, second_mat):
    return lax.dot_general(
        first_mat, second_mat, (((1,), (1,)), ((), ())), preferred_element_type=jnp.float32
    )


def rotary_tables(segment):
    spots = lax.broadcasted_iota(jnp.int32, segment.shape, 1)
    smaller = segment[:, :, None] > segment[:, None, :]
    starts = jnp.sum(smaller.astype(jnp.int32), axis=2)
    offsets = (spots - starts).astype(jnp.float32)
    frequency = 10000.0 ** (-2.0 * jnp.arange(ROT // 2, dtype=jnp.float32) / ROT)
    angles = offsets[:, :, None, None] * frequency
    return (jnp.cos(angles), jnp.sin(angles))


def rotate_pair(vectors, cosine, sine, inverse):
    half_rot = cosine.shape[-1]
    first = vectors[..., :half_rot]
    second = vectors[..., half_rot : 2 * half_rot]
    remain = vectors[..., 2 * half_rot :]
    turn = -sine if inverse else sine
    return jnp.concatenate(
        [first * cosine - second * turn, second * cosine + first * turn, remain], axis=-1
    )


def swap(array, axis, size, bit):
    return lax.ppermute(array, axis, [(i, i ^ bit) for i in range(size)])


def bits_of(size):
    return [1 << k for k in range(size.bit_length() - 1)]


def scatter_sum(array, size, order):
    where_am_i = lax.axis_index("tensor")
    first = 0
    for bit in order:
        half = array.shape[0] // 2
        mine = (where_am_i // bit) % 2
        away = lax.dynamic_slice_in_dim(array, (1 - mine) * half, half, 0)
        keep = lax.dynamic_slice_in_dim(array, mine * half, half, 0)
        array = keep + swap(away, "tensor", size, bit)
        first = first + mine * half
    return array, first


def gather_back(array, size, order):
    where_am_i = lax.axis_index("tensor")
    pieces = [(array, 0)]
    for bit in reversed(order):
        pieces = pieces + [(swap(piece, "tensor", size, bit), mask | bit) for piece, mask in pieces]
    placed = []
    for piece, mask in pieces:
        rows = array.shape[0] << len(order)
        first = 0
        for bit in order:
            rows = rows // 2
            first = first + (((where_am_i ^ mask) // bit) % 2) * rows
        placed.append((piece, first))
    return placed


def line_sum(array, size):
    chips = size // 2
    place = lax.axis_index("dp") // 2

    def send(what, pairs):
        return lax.ppermute(
            what, "dp", [(2 * a + c, 2 * b + c) for a, b in pairs for c in range(2)]
        )

    if chips == 1:
        return array
    steps = range(chips // 2 - 1)
    for s in steps:
        array = array + send(array, [(s, s + 1), (chips - 1 - s, chips - 2 - s)])
    middle = chips // 2
    array = array + send(array, [(middle - 1, middle), (middle, middle - 1)])
    for s in reversed(steps):
        got = send(array, [(s + 1, s), (chips - 2 - s, chips - 1 - s)])
        array = jnp.where((place == s) | (place == chips - 1 - s), got, array)
    return array


def dp_sum(array, size, chunks):
    core = lax.axis_index("dp") % 2
    half = array.shape[0] // 2
    rows = half // chunks
    total = array
    for c in range(chunks):
        away = lax.dynamic_slice_in_dim(array, (1 - core) * half + c * rows, rows, 0)
        keep = lax.dynamic_slice_in_dim(array, core * half + c * rows, rows, 0)
        mine = line_sum(keep + swap(away, "dp", size, 1), size)
        other = swap(mine, "dp", size, 1)
        total = lax.dynamic_update_slice_in_dim(total, mine, core * half + c * rows, 0)
        total = lax.dynamic_update_slice_in_dim(total, other, (1 - core) * half + c * rows, 0)
    return total


def small_sum(array, size, axis):
    if axis == "dp":
        return line_sum(array + swap(array, "dp", size, 1), size)
    for bit in bits_of(size):
        array = array + swap(array, axis, size, bit)
    return array


def shards(
    dp_size,
    tensor_size,
    tokens,
    segment,
    attn_gain,
    attn_shift,
    mlp_gain,
    mlp_shift,
    w_qkv,
    b_qkv,
    w_out,
    w_up,
    b_up,
    w_down,
    b_branch,
    cotangent,
):
    token_rows = tokens.astype(jnp.float32)
    count_seq = segment.shape[0]
    seq_len = segment.shape[1]
    rows_here, width = tokens.shape
    local_heads = w_qkv.shape[1] // (3 * HD)
    score_scale = HD ** (-0.5)
    block = min(512, seq_len)
    up_order = bits_of(tensor_size)
    orders = (up_order, up_order[::-1])

    row_mean = jnp.mean(token_rows, axis=-1, keepdims=True)
    centred = token_rows - row_mean
    scale_inv = lax.rsqrt(jnp.mean(centred * centred, axis=-1, keepdims=True) + EPS)
    normed = centred * scale_inv
    attn_low = (normed * attn_gain + attn_shift).astype(jnp.bfloat16)
    mlp_low = (normed * mlp_gain + mlp_shift).astype(jnp.bfloat16)

    cosine, sine = rotary_tables(segment)
    projected = jnp.dot(attn_low, w_qkv, preferred_element_type=jnp.float32) + b_qkv
    grouped = projected.reshape(count_seq, seq_len, local_heads, 3, HD)
    queries = rotate_pair(grouped[:, :, :, 0], cosine, sine, False).astype(jnp.bfloat16)
    keys_rot = rotate_pair(grouped[:, :, :, 1], cosine, sine, False).astype(jnp.bfloat16)
    values = grouped[:, :, :, 2].astype(jnp.bfloat16)
    key_spots = lax.broadcasted_iota(jnp.int32, (block, seq_len), 1)
    query_base = lax.broadcasted_iota(jnp.int32, (block, seq_len), 0)

    def block_scores(start, query_block):
        raw = (
            jnp.einsum("nqhd,nkhd->nhqk", query_block, keys_rot, preferred_element_type=jnp.float32)
            * score_scale
        )
        same_doc = segment[:, start : start + block, None] == segment[:, None, :]
        allowed = same_doc & (key_spots <= query_base + start)
        return jnp.where(allowed[:, None], raw, NEG)

    outputs = []
    lse_parts = []
    for start in range(0, seq_len, block):
        masked = block_scores(start, queries[:, start : start + block])
        row_max = jnp.max(masked, axis=-1, keepdims=True)
        exponent = jnp.exp(masked - row_max)
        totals = jnp.sum(exponent, axis=-1, keepdims=True)
        attn_probs = exponent / totals
        outputs.append(
            jnp.einsum(
                "nhqk,nkhd->nqhd",
                attn_probs.astype(jnp.bfloat16),
                values,
                preferred_element_type=jnp.float32,
            )
        )
        lse_parts.append(row_max + jnp.log(totals))
    attended = (
        jnp.concatenate(outputs, axis=1).astype(jnp.bfloat16).reshape(rows_here, local_heads * HD)
    )

    pre_act = jnp.dot(mlp_low, w_up, preferred_element_type=jnp.float32) + b_up
    phi_sum = 0.5 * (1.0 + lax.erf(pre_act * (0.5**0.5)))
    hidden = (pre_act * phi_sum).astype(jnp.bfloat16)
    slope = phi_sum + pre_act * jnp.exp(-0.5 * pre_act * pre_act) * ((2.0 * math.pi) ** -0.5)

    split = rows_here // 2
    result = jnp.zeros((rows_here, width), jnp.bfloat16)
    for part, order in enumerate(orders):
        rows = slice(part * split, (part + 1) * split)
        partial = jnp.dot(attended[rows], w_out, preferred_element_type=jnp.float32) + jnp.dot(
            hidden[rows], w_down, preferred_element_type=jnp.float32
        )
        mine, _ = scatter_sum(partial, tensor_size, order)
        for piece, first in gather_back(mine, tensor_size, order):
            at = first + part * split
            its_tokens = lax.dynamic_slice_in_dim(tokens, at, piece.shape[0], 0)
            done = (its_tokens.astype(jnp.float32) + piece + b_branch).astype(jnp.bfloat16)
            result = lax.dynamic_update_slice_in_dim(result, done, at, 0)

    grad_down = dp_sum(inner_rows(hidden, cotangent), dp_size, 2)
    d_pre_wide = times_trans(cotangent, w_down) * slope
    d_pre = d_pre_wide.astype(jnp.bfloat16)
    grad_up = dp_sum(inner_rows(mlp_low, d_pre), dp_size, 2)
    grad_up_bias = jnp.sum(d_pre.astype(jnp.float32), axis=0)
    branch_grad = jnp.sum(cotangent.astype(jnp.float32), axis=0)
    d_mlp_in = times_trans(d_pre, w_up)
    grad_out = dp_sum(inner_rows(attended, cotangent), dp_size, 1)

    d_attended = (
        times_trans(cotangent, w_out)
        .astype(jnp.bfloat16)
        .reshape(count_seq, seq_len, local_heads, HD)
    )
    d_queries = []
    d_keys = jnp.zeros((count_seq, seq_len, local_heads, HD), jnp.float32)
    d_values = jnp.zeros((count_seq, seq_len, local_heads, HD), jnp.float32)
    for start in range(0, seq_len, block):
        query_block = queries[:, start : start + block]
        masked = block_scores(start, query_block)
        attn_probs = jnp.exp(masked - lse_parts[start // block])
        grad_block = d_attended[:, start : start + block]
        d_probs = jnp.einsum(
            "nqhd,nkhd->nhqk", grad_block, values, preferred_element_type=jnp.float32
        )
        row_dot = jnp.sum(attn_probs * d_probs, axis=-1, keepdims=True)
        d_scores = (attn_probs * (d_probs - row_dot)).astype(jnp.bfloat16)
        d_queries.append(
            jnp.einsum("nhqk,nkhd->nqhd", d_scores, keys_rot, preferred_element_type=jnp.float32)
            * score_scale
        )
        d_keys = (
            d_keys
            + jnp.einsum(
                "nhqk,nqhd->nkhd", d_scores, query_block, preferred_element_type=jnp.float32
            )
            * score_scale
        )
        d_values = d_values + jnp.einsum(
            "nhqk,nqhd->nkhd",
            attn_probs.astype(jnp.bfloat16),
            grad_block,
            preferred_element_type=jnp.float32,
        )
    d_query_all = rotate_pair(jnp.concatenate(d_queries, axis=1), cosine, sine, True)
    d_key_all = rotate_pair(d_keys, cosine, sine, True)
    d_projected = (
        jnp.stack([d_query_all, d_key_all, d_values], axis=3)
        .reshape(rows_here, local_heads * 3 * HD)
        .astype(jnp.bfloat16)
    )
    d_attn_in = times_trans(d_projected, w_qkv)

    scaled = d_attn_in * attn_gain + d_mlp_in * mlp_gain
    d_tokens = jnp.zeros((rows_here, width), jnp.float32)
    for part, order in enumerate(orders):
        rows = slice(part * split, (part + 1) * split)
        mine, first = scatter_sum(scaled[rows], tensor_size, order)
        at = first + part * split

        def here(whole, at=at, count=mine.shape[0]):
            return lax.dynamic_slice_in_dim(whole, at, count, 0)

        normed_here = here(normed)
        back = here(cotangent).astype(jnp.float32) + here(scale_inv) * (
            mine
            - jnp.mean(mine, axis=-1, keepdims=True)
            - normed_here * jnp.mean(mine * normed_here, axis=-1, keepdims=True)
        )
        for piece, its_first in gather_back(back, tensor_size, order):
            d_tokens = lax.dynamic_update_slice_in_dim(
                d_tokens, piece, its_first + part * split, 0
            )
    grad_qkv = inner_rows(attn_low, d_projected)
    grad_qkv_bias = jnp.sum(d_projected.astype(jnp.float32), axis=0)
    grad_qkv = dp_sum(grad_qkv, dp_size, 2)

    stats = jnp.stack(
        [
            jnp.sum(d_attn_in * normed, axis=0),
            jnp.sum(d_attn_in, axis=0),
            jnp.sum(d_mlp_in * normed, axis=0),
            jnp.sum(d_mlp_in, axis=0),
        ]
    )
    stats = small_sum(stats, tensor_size, "tensor")
    vectors = jnp.concatenate(
        [stats.reshape(-1), grad_qkv_bias, grad_up_bias, branch_grad]
    )
    vectors = small_sum(vectors, dp_size, "dp")
    sizes = (width,) * 4 + (grad_qkv_bias.shape[0], grad_up_bias.shape[0], width)
    ends = [sum(sizes[: k + 1]) for k in range(len(sizes))]
    a_gain, a_shift, m_gain, m_shift, qkv_bias, up_bias, branch = (
        vectors[end - size : end] for end, size in zip(ends, sizes, strict=True)
    )
    return (
        result,
        d_tokens,
        grad_qkv,
        qkv_bias,
        grad_out,
        grad_up,
        up_bias,
        grad_down,
        branch,
        a_gain,
        a_shift,
        m_gain,
        m_shift,
    )


def solution(mesh):
    placed = (
        P("dp", None),
        P("dp", None),
        P(),
        P(),
        P(),
        P(),
        P(None, "tensor"),
        P("tensor"),
        P("tensor", None),
        P(None, "tensor"),
        P("tensor"),
        P("tensor", None),
        P(),
        P("dp", None),
    )

    def body(*arrays):
        return shards(mesh.shape["dp"], mesh.shape["tensor"], *arrays)

    return jax.shard_map(
        body,
        mesh=mesh,
        in_specs=placed,
        out_specs=(
            P("dp", None),
            P("dp", None),
            P(None, "tensor"),
            P("tensor"),
            P("tensor", None),
            P(None, "tensor"),
            P("tensor"),
            P("tensor", None),
            P(),
            P(),
            P(),
            P(),
            P(),
        ),
        check_vma=False,
    )
```

```python
import functools
import math

import jax
import jax.numpy as jnp
from jax import lax
from jax.experimental import pallas as pl
from jax.experimental.pallas import tpu as pltpu
from jax.sharding import PartitionSpec as P

HD = 64
ROT = 16
MOST = 512

EPS = 1e-05
NEG = -1e30


def inner_rows(first_mat, second_mat):
    return lax.dot_general(
        first_mat, second_mat, (((0,), (0,)), ((), ())), preferred_element_type=jnp.float32
    )


def times_trans(first_mat, second_mat):
    return lax.dot_general(
        first_mat, second_mat, (((1,), (1,)), ((), ())), preferred_element_type=jnp.float32
    )


def product(first_mat, second_mat):
    return jnp.dot(first_mat, second_mat, preferred_element_type=jnp.float32)


def turn_angles(segment):
    spots = lax.broadcasted_iota(jnp.int32, segment.shape, 0)
    starts = jnp.zeros_like(segment)
    for number in range(3):
        count = jnp.sum((segment == number).astype(jnp.int32))
        starts = starts + jnp.where(segment > number, count, 0)
    offsets = (spots - starts).astype(jnp.float32)
    frequency = 10000.0 ** (-2.0 * jnp.arange(ROT // 2, dtype=jnp.float32) / ROT)
    angles = frequency[:, None] * offsets[None, :]
    number = jnp.broadcast_to(segment.astype(jnp.float32), (8, segment.shape[0]))
    return jnp.concatenate([jnp.cos(angles), jnp.sin(angles), number], axis=0)


def spread(angles, rows, take):
    return lax.dot_general(
        angles[0 : take.shape[0], rows],
        take,
        (((0,), (0,)), ((), ())),
        precision=lax.Precision.HIGHEST,
        preferred_element_type=jnp.float32,
    )


def turn_tables(angles, rows):
    tile, half = 2 * HD, ROT // 2
    source = lax.broadcasted_iota(jnp.int32, (ROT, tile), 0)
    column = lax.broadcasted_iota(jnp.int32, (ROT, tile), 1) % HD
    take_cos = ((source == column % half) & (column < ROT)).astype(jnp.float32)
    take_sin = source == column % half + half
    take_low = -(take_sin & (column < half)).astype(jnp.float32)
    take_high = (take_sin & (column >= half) & (column < ROT)).astype(jnp.float32)
    lane = lax.broadcasted_iota(jnp.int32, (rows.stop - rows.start, tile), 1)
    still = (lane % HD >= ROT).astype(jnp.float32)
    return (
        spread(angles, rows, take_cos) + still,
        spread(angles, rows, take_low),
        spread(angles, rows, take_high),
    )


def turn(wide, number, turned, low, high):
    tile, half = 2 * HD, ROT // 2
    lane = lax.broadcasted_iota(jnp.int32, wide.shape, 1)
    moved = (
        wide * turned
        + pltpu.roll(wide, tile - half, 1) * low
        + pltpu.roll(wide, half, 1) * high
    )
    if 2 * number % 3 == 2:
        return jnp.where(lane < HD, wide, moved)
    if (2 * number + 1) % 3 == 2:
        return jnp.where(lane >= HD, wide, moved)
    return moved


def key_range(start, block):
    return max(0, start - -(-MOST // block) * block), start + block


def fill_bias(bias, angles, start, block):
    first, until = key_range(start, block)
    count = until - first
    source = lax.broadcasted_iota(jnp.int32, (ROT + 8, 2 * HD), 0)
    own = spread(angles, slice(start, until), (source == ROT).astype(jnp.float32))[:, :1]
    other = angles[ROT : ROT + 1, first:until]
    query_spot = lax.broadcasted_iota(jnp.int32, (block, count), 0) + start
    key_spot = lax.broadcasted_iota(jnp.int32, (block, count), 1) + first
    bias[:, :count] = jnp.where((own == other) & (key_spot <= query_spot), 0.0, NEG)


def attend_kernel(heads, angles, projected, attended, sums, q_s, k_s, v_s, bias):
    seq_len, lanes = projected.shape
    block = min(256, seq_len)
    tile = 2 * HD
    for start in range(0, seq_len, block):
        rows = slice(start, start + block)
        turned, low, high = turn_tables(angles, rows)
        for number in range(lanes // tile):
            wide = turn(
                projected[rows, number * tile : (number + 1) * tile], number, turned, low, high
            )
            for side in range(2):
                head, kind = divmod(2 * number + side, 3)
                if head < heads:
                    part = wide[:, side * HD : (side + 1) * HD].astype(jnp.bfloat16)
                    (q_s, k_s, v_s)[kind][head, rows, :] = (
                        part * HD ** (-0.5) if kind == 0 else part
                    )
    for start in range(0, seq_len, block):
        first, until = key_range(start, block)
        count = until - first
        rows, keys = slice(start, until), slice(first, until)
        fill_bias(bias, angles, start, block)
        outs = []
        for h in range(heads):
            scores = times_trans(q_s[h, rows, :], k_s[h, keys, :]) + bias[:, :count]
            most = jnp.max(scores, axis=-1, keepdims=True)
            exponent = jnp.exp(scores - most)
            total = jnp.sum(exponent, axis=-1, keepdims=True)
            probs = (exponent * (1.0 / total)).astype(jnp.bfloat16)
            sums[rows, h : h + 1] = most + jnp.log(total)
            outs.append(product(probs, v_s[h, keys, :]))
        attended[rows, :] = jnp.concatenate(outs, axis=1).astype(jnp.bfloat16)


def attend_back_kernel(
    begin, heads, angles, q_s, k_s, v_s, sums, attended, d_attended, d_projected, dq_s, dk_s, dv_s, bias
):
    seq_len, lanes = d_projected.shape
    block = min(256, seq_len)
    tile = 2 * HD
    for start in range(0, seq_len, block):
        first, until = key_range(start, block)
        count = until - first
        rows, keys = slice(start, until), slice(first, until)
        fill_bias(bias, angles, start, block)
        for h in range(heads):
            g = begin + h
            q, k, v = q_s[g, rows, :], k_s[g, keys, :], v_s[g, keys, :]
            d_out = d_attended[rows, g * HD : (g + 1) * HD]
            out = attended[rows, g * HD : (g + 1) * HD]
            probs = jnp.exp(times_trans(q, k) + (bias[:, :count] - sums[rows, g : g + 1]))
            row_dot = jnp.sum(
                out.astype(jnp.float32) * d_out.astype(jnp.float32), axis=-1, keepdims=True
            )
            d_scores = (probs * (times_trans(d_out, v) - row_dot)).astype(jnp.bfloat16)
            dq_s[h, rows, :] = product(d_scores, k) * HD ** (-0.5)
            d_k = inner_rows(q, d_scores)
            d_v = inner_rows(d_out, probs.astype(jnp.bfloat16))
            old = count - block
            if old:
                dk_s[h, :, first:start] += d_k[:, :old]
                dv_s[h, :, first:start] += d_v[:, :old]
            dk_s[h, :, rows] = d_k[:, old:]
            dv_s[h, :, rows] = d_v[:, old:]
    for start in range(0, seq_len, block):
        rows = slice(start, start + block)
        turned, low, high = turn_tables(angles, rows)

        def section(at, rows=rows):
            head, kind = divmod(at, 3)
            if head >= heads:
                return jnp.zeros((block, HD), jnp.float32)
            return dq_s[head, rows, :] if kind == 0 else (dk_s, dv_s)[kind - 1][head, :, rows].T

        for number in range(lanes // tile):
            wide = jnp.concatenate([section(2 * number), section(2 * number + 1)], axis=1)
            d_projected[rows, number * tile : (number + 1) * tile] = turn(
                wide, number, turned, -low, -high
            ).astype(jnp.bfloat16)


VMEM = pl.BlockSpec(memory_space=pltpu.VMEM)


def bias_held(block):
    return pltpu.VMEM((block, -(-MOST // block) * block + block), jnp.float32)


def attend(angles, projected, heads):
    seq_len = projected.shape[0]
    pairs = heads * seq_len * seq_len // 2
    shape = jax.ShapeDtypeStruct
    return pl.pallas_call(
        functools.partial(attend_kernel, heads),
        out_shape=(
            shape((seq_len, heads * HD), jnp.bfloat16),
            shape((seq_len, 2 * HD), jnp.float32),
        )
        + (shape((heads, seq_len, HD), jnp.bfloat16),) * 3,
        in_specs=[VMEM] * 2,
        out_specs=(VMEM,) * 5,
        scratch_shapes=[bias_held(min(256, seq_len))],
        compiler_params=pltpu.CompilerParams(vmem_limit_bytes=24 * 2**20),
        cost_estimate=pl.CostEstimate(
            flops=80 * pairs * HD, bytes_accessed=seq_len * seq_len * 8, transcendentals=pairs
        ),
    )(angles, projected)


def attend_back(angles, kept, d_attended, begin, heads, lanes):
    attended, sums, queries, keys, values = kept
    seq_len = attended.shape[0]
    pairs = heads * seq_len * seq_len // 2
    cross = pltpu.VMEM((heads, HD, seq_len), jnp.float32)
    return pl.pallas_call(
        functools.partial(attend_back_kernel, begin, heads),
        out_shape=jax.ShapeDtypeStruct((seq_len, lanes), jnp.bfloat16),
        in_specs=[VMEM] * 7,
        out_specs=VMEM,
        scratch_shapes=[
            pltpu.VMEM((heads, seq_len, HD), jnp.float32),
            cross,
            cross,
            bias_held(min(256, seq_len)),
        ],
        compiler_params=pltpu.CompilerParams(vmem_limit_bytes=24 * 2**20),
        cost_estimate=pl.CostEstimate(
            flops=160 * pairs * HD, bytes_accessed=seq_len * seq_len * 8, transcendentals=pairs
        ),
    )(angles, queries, keys, values, sums, attended, d_attended)


class Order:
    def __init__(self, token):
        self.token = token

    def tie(self, *arrays):
        tied = lax.optimization_barrier((self.token, *arrays))
        self.token = tied[0]
        return tied[1] if len(arrays) == 1 else tied[1:]

    def run(self, step, *arrays):
        tied = lax.optimization_barrier((self.token, *arrays))
        out = step(*tied[1:])
        if isinstance(out, tuple):
            return self.tie(*out)
        return self.tie(out)


class Chain:
    def __init__(self, order, steps):
        self.order, self.steps, self.out, self.held = order, steps, None, None
        self._go(None)

    def _go(self, arrived):
        try:
            array, axis, pairs = self.steps.send(arrived)
        except StopIteration as stop:
            self.held, self.out = None, stop.value
            return
        array = self.order.tie(array)
        self.held = lax.ppermute(array, axis, pairs)

    def on(self):
        if self.held is not None:
            self._go(self.order.tie(self.held))
        return self

    def end(self):
        while self.held is not None:
            self.on()
        return self.out


def swap_pairs(size, bit):
    return [(i, i ^ bit) for i in range(size)]


def tensor_steps(array, size, order, between):
    place = lax.axis_index("tensor")
    first = 0
    for bit in order:
        half = array.shape[0] // 2
        mine = (place // bit) % 2
        away = lax.dynamic_slice_in_dim(array, (1 - mine) * half, half, 0)
        got = yield away, "tensor", swap_pairs(size, bit)
        array = lax.dynamic_slice_in_dim(array, mine * half, half, 0) + got
        first = first + mine * half
    array = between(array, first)
    for bit in reversed(order):
        got = yield array, "tensor", swap_pairs(size, bit)
        mine = (place // bit) % 2
        array = jnp.where(
            mine == 0,
            jnp.concatenate([array, got], axis=0),
            jnp.concatenate([got, array], axis=0),
        )
    return array


def core_steps(array, size):
    core = lax.axis_index("dp") % 2
    half = array.shape[0] // 2
    away = lax.dynamic_slice_in_dim(array, (1 - core) * half, half, 0)
    got = yield away, "dp", swap_pairs(size, 1)
    return lax.dynamic_slice_in_dim(array, core * half, half, 0) + got


def line_steps(array, size, back=True):
    chips = size // 2
    place = lax.axis_index("dp") // 2

    def pairs(moves):
        return [(2 * a + c, 2 * b + c) for a, b in moves for c in range(2)]

    if chips > 1:
        steps = range(chips // 2 - 1)
        for s in steps:
            got = yield array, "dp", pairs([(s, s + 1), (chips - 1 - s, chips - 2 - s)])
            array = array + got
        middle = chips // 2
        got = yield array, "dp", pairs([(middle - 1, middle), (middle, middle - 1)])
        array = array + got
        for s in reversed(steps):
            got = yield array, "dp", pairs([(s + 1, s), (chips - 2 - s, chips - 1 - s)])
            array = jnp.where((place == s) | (place == chips - 1 - s), got, array)
    if not back:
        return array
    got = yield array, "dp", swap_pairs(size, 1)
    return array, got


def small_steps(stats, rest, tensor_size, dp_size):
    for bit in (1 << k for k in range(tensor_size.bit_length() - 1)):
        got = yield stats, "tensor", swap_pairs(tensor_size, bit)
        stats = stats + got
    vectors = jnp.concatenate([stats.reshape(-1), *rest])
    got = yield vectors, "dp", swap_pairs(dp_size, 1)
    return (yield from line_steps(vectors + got, dp_size, back=False))


def assemble(core, parts):
    low = [jnp.where(core == 0, mine, other) for mine, other in parts]
    high = [jnp.where(core == 0, other, mine) for mine, other in parts]
    return jnp.concatenate(low + high, axis=0)


def halves(array, chunks):
    rows = array.shape[0] // chunks
    return [array[c * rows : (c + 1) * rows] for c in range(chunks)]


def shards(
    dp_size,
    tensor_size,
    tokens,
    segment,
    attn_gain,
    attn_shift,
    mlp_gain,
    mlp_shift,
    w_qkv,
    b_qkv,
    w_out,
    w_up,
    b_up,
    w_down,
    b_branch,
    cotangent,
):
    rows_here, width = tokens.shape
    heads = w_qkv.shape[1] // (3 * HD)
    group = 2 if heads % 2 == 0 else heads
    lanes = -(-3 * HD * group // 128) * 128
    bits = [1 << k for k in range(tensor_size.bit_length() - 1)]
    orders = (bits, bits[::-1])
    split = rows_here // 2
    order = Order(lax.axis_index("dp") % 2)
    run = order.run

    def chain(steps):
        return Chain(order, steps)

    def norm(tokens):
        rows = tokens.astype(jnp.float32)
        centred = rows - jnp.mean(rows, axis=-1, keepdims=True)
        scale_inv = lax.rsqrt(jnp.mean(centred * centred, axis=-1, keepdims=True) + EPS)
        normed = centred * scale_inv
        return (
            (normed * attn_gain + attn_shift).astype(jnp.bfloat16),
            (normed * mlp_gain + mlp_shift).astype(jnp.bfloat16),
            normed,
            scale_inv,
        )

    def feed(mlp_low, w_up):
        pre_act = product(mlp_low, w_up) + b_up
        below = 0.5 * (1.0 + lax.erf(pre_act * (0.5**0.5)))
        bell = jnp.exp(-0.5 * pre_act * pre_act) * ((2.0 * math.pi) ** -0.5)
        return (pre_act * below).astype(jnp.bfloat16), below + pre_act * bell

    def project(attn_low, w_qkv):
        projected = product(attn_low, w_qkv) + b_qkv
        if group * 3 * HD != lanes:
            projected = jnp.pad(projected, ((0, 0), (0, lanes - group * 3 * HD)))
        return projected

    attn_low, mlp_low, normed, scale_inv = run(norm, tokens)
    hidden, slope = run(feed, mlp_low, w_up)
    core_down = chain(core_steps(run(inner_rows, hidden, cotangent), dp_size))
    projected = run(project, attn_low, w_qkv)
    angles = run(turn_angles, segment[0])
    d_attended = run(
        lambda dy, w: times_trans(dy, w).astype(jnp.bfloat16), cotangent, w_out
    )
    down = [line_steps(part, dp_size) for part in halves(core_down.end(), 2)]
    down[0] = chain(down[0])
    kept = run(functools.partial(attend, heads=heads), angles, projected)
    attended = kept[0]

    def branches(attended, hidden):
        return tuple(
            product(attended[rows], w_out) + product(hidden[rows], w_down)
            for rows in (slice(0, split), slice(split, None))
        )

    partial = run(branches, attended, hidden)
    result = [
        chain(tensor_steps(part, tensor_size, its, lambda rows, first: rows))
        for part, its in zip(partial, orders, strict=True)
    ]
    d_pre = run(
        lambda dy, w, slope: (times_trans(dy, w) * slope).astype(jnp.bfloat16),
        cotangent,
        w_down,
        slope,
    )
    core_up = chain(core_steps(run(inner_rows, mlp_low, d_pre), dp_size))
    down[0].on()
    down[1] = chain(down[1])
    d_mlp_in = run(times_trans, d_pre, w_up)
    up = [line_steps(part, dp_size) for part in halves(core_up.end(), 2)]
    result[0].on()
    result[1].on()

    back = []
    for begin in range(0, heads, group):
        def step(angles, d_attended, *kept, begin=begin):
            return attend_back(angles, kept, d_attended, begin, group, lanes)

        back.append(run(step, angles, d_attended, *kept)[:, : group * 3 * HD])
        result[0].on()
        result[1].on()
        if begin == 0:
            down[0].on()
            down[1].on()
            up[0] = chain(up[0])

    def backward(w_qkv, d_mlp_in, *back):
        d_projected = jnp.concatenate(back, axis=1)
        d_attn_in = times_trans(d_projected, w_qkv)
        return d_projected, d_attn_in, d_attn_in * attn_gain + d_mlp_in * mlp_gain

    d_projected, d_attn_in, scaled = run(backward, w_qkv, d_mlp_in, *back)

    def norm_back(part):
        def between(rows, first):
            at = first + part * split

            def here(whole):
                return lax.dynamic_slice_in_dim(whole, at, rows.shape[0], 0)

            normed_here = here(normed)
            return here(cotangent).astype(jnp.float32) + here(scale_inv) * (
                rows
                - jnp.mean(rows, axis=-1, keepdims=True)
                - normed_here * jnp.mean(rows * normed_here, axis=-1, keepdims=True)
            )

        return between

    d_tokens = [
        chain(tensor_steps(scaled[p * split : (p + 1) * split], tensor_size, its, norm_back(p)))
        for p, its in enumerate(orders)
    ]
    core_qkv = chain(core_steps(run(inner_rows, attn_low, d_projected), dp_size))
    down[0].on()
    down[1].on()
    up[0].on()
    up[1] = chain(up[1])
    core_out = chain(core_steps(run(inner_rows, attended, cotangent), dp_size))

    def sums(d_attn_in, d_mlp_in, normed):
        return jnp.stack(
            [
                jnp.sum(d_attn_in * normed, axis=0),
                jnp.sum(d_attn_in, axis=0),
                jnp.sum(d_mlp_in * normed, axis=0),
                jnp.sum(d_mlp_in, axis=0),
            ]
        )

    def columns(*arrays):
        return tuple(jnp.sum(array.astype(jnp.float32), axis=0) for array in arrays)

    stats = run(sums, d_attn_in, d_mlp_in, normed)
    rest = run(columns, d_projected, d_pre, cotangent)
    small = chain(small_steps(stats, rest, tensor_size, dp_size))
    qkv = [line_steps(part, dp_size) for part in halves(core_qkv.end(), 2)]
    out = line_steps(core_out.end(), dp_size)
    small.on()

    def finish(tokens, *parts):
        summed = jnp.concatenate(parts, axis=0)
        return (tokens.astype(jnp.float32) + summed + b_branch).astype(jnp.bfloat16)

    result = run(finish, tokens, *(part.end() for part in result))
    small.on()
    for part in d_tokens:
        part.on()
    for part in (down[0], down[1], up[0], up[1]):
        part.on()
    qkv[0] = chain(qkv[0])
    small.on()
    for part in d_tokens:
        part.on()
    small.on()
    for part in (down[1], up[0], up[1], qkv[0]):
        part.on()
    qkv[1] = chain(qkv[1])
    small.on()
    for part in d_tokens:
        part.on()
    grad_down = run(lambda *p: assemble(p[0], (p[1:3], p[3:5])), order.token, *down[0].end(), *down[1].end())
    for part in (up[0], up[1], qkv[0], qkv[1]):
        part.on()
    out = chain(out)
    for part in d_tokens:
        part.on()
    for part in (up[1], qkv[0], qkv[1], out):
        part.on()
    d_tokens = run(lambda *p: jnp.concatenate(p, axis=0), *(part.end() for part in d_tokens))
    grad_up = run(lambda *p: assemble(p[0], (p[1:3], p[3:5])), order.token, *up[0].end(), *up[1].end())
    vectors = small.end()
    for part in (qkv[0], qkv[1], out):
        part.on()
    qkv[0].end(), qkv[1].end()
    out.on()
    grad_qkv = run(lambda *p: assemble(p[0], (p[1:3], p[3:5])), order.token, *qkv[0].end(), *qkv[1].end())
    grad_out = out.end()
    grad_out = assemble(order.token, (grad_out,))

    sizes = (width,) * 4 + (w_qkv.shape[1], w_up.shape[1], width)
    ends = [sum(sizes[: k + 1]) for k in range(len(sizes))]
    a_gain, a_shift, m_gain, m_shift, qkv_bias, up_bias, branch = (
        vectors[end - size : end] for end, size in zip(ends, sizes, strict=True)
    )
    return (
        result,
        d_tokens,
        grad_qkv,
        qkv_bias,
        grad_out,
        grad_up,
        up_bias,
        grad_down,
        branch,
        a_gain,
        a_shift,
        m_gain,
        m_shift,
    )


def solution(mesh):
    placed = (
        P("dp", None),
        P("dp", None),
        P(),
        P(),
        P(),
        P(),
        P(None, "tensor"),
        P("tensor"),
        P("tensor", None),
        P(None, "tensor"),
        P("tensor"),
        P("tensor", None),
        P(),
        P("dp", None),
    )

    def body(*arrays):
        return shards(mesh.shape["dp"], mesh.shape["tensor"], *arrays)

    return jax.shard_map(
        body,
        mesh=mesh,
        in_specs=placed,
        out_specs=(
            P("dp", None),
            P("dp", None),
            P(None, "tensor"),
            P("tensor"),
            P("tensor", None),
            P(None, "tensor"),
            P("tensor"),
            P("tensor", None),
            P(),
            P(),
            P(),
            P(),
            P(),
        ),
        check_vma=False,
    )
```

```python
import functools
import math

import jax
import jax.numpy as jnp
from jax import lax
from jax.experimental import pallas as pl
from jax.experimental.pallas import tpu as pltpu
from jax.sharding import PartitionSpec as P

HD = 64
ROT = 16
MOST = 512

EPS = 1e-05
NEG = -1e30


def inner_rows(first_mat, second_mat):
    return lax.dot_general(
        first_mat, second_mat, (((0,), (0,)), ((), ())), preferred_element_type=jnp.float32
    )


def times_trans(first_mat, second_mat):
    return lax.dot_general(
        first_mat, second_mat, (((1,), (1,)), ((), ())), preferred_element_type=jnp.float32
    )


def product(first_mat, second_mat):
    return jnp.dot(first_mat, second_mat, preferred_element_type=jnp.float32)


def turn_angles(segment):
    spots = lax.broadcasted_iota(jnp.int32, segment.shape, 0)
    starts = jnp.zeros_like(segment)
    for number in range(3):
        count = jnp.sum((segment == number).astype(jnp.int32))
        starts = starts + jnp.where(segment > number, count, 0)
    offsets = (spots - starts).astype(jnp.float32)
    frequency = 10000.0 ** (-2.0 * jnp.arange(ROT // 2, dtype=jnp.float32) / ROT)
    angles = frequency[:, None] * offsets[None, :]
    number = jnp.broadcast_to(segment.astype(jnp.float32), (8, segment.shape[0]))
    return jnp.concatenate([jnp.cos(angles), jnp.sin(angles), number], axis=0)


def spread(angles, rows, take):
    return lax.dot_general(
        angles[0 : take.shape[0], rows],
        take,
        (((0,), (0,)), ((), ())),
        precision=lax.Precision.HIGHEST,
        preferred_element_type=jnp.float32,
    )


def turn_tables(angles, rows):
    tile, half = 2 * HD, ROT // 2
    source = lax.broadcasted_iota(jnp.int32, (ROT, tile), 0)
    column = lax.broadcasted_iota(jnp.int32, (ROT, tile), 1) % HD
    take_cos = ((source == column % half) & (column < ROT)).astype(jnp.float32)
    take_sin = source == column % half + half
    take_low = -(take_sin & (column < half)).astype(jnp.float32)
    take_high = (take_sin & (column >= half) & (column < ROT)).astype(jnp.float32)
    lane = lax.broadcasted_iota(jnp.int32, (rows.stop - rows.start, tile), 1)
    still = (lane % HD >= ROT).astype(jnp.float32)
    return (
        spread(angles, rows, take_cos) + still,
        spread(angles, rows, take_low),
        spread(angles, rows, take_high),
    )


def turn(wide, number, turned, low, high):
    tile, half = 2 * HD, ROT // 2
    lane = lax.broadcasted_iota(jnp.int32, wide.shape, 1)
    moved = (
        wide * turned
        + pltpu.roll(wide, tile - half, 1) * low
        + pltpu.roll(wide, half, 1) * high
    )
    if 2 * number % 3 == 2:
        return jnp.where(lane < HD, wide, moved)
    if (2 * number + 1) % 3 == 2:
        return jnp.where(lane >= HD, wide, moved)
    return moved


def key_range(start, block):
    return max(0, start - -(-MOST // block) * block), start + block


def fill_bias(bias, angles, start, block):
    first, until = key_range(start, block)
    count = until - first
    source = lax.broadcasted_iota(jnp.int32, (ROT + 8, 2 * HD), 0)
    own = spread(angles, slice(start, until), (source == ROT).astype(jnp.float32))[:, :1]
    other = angles[ROT : ROT + 1, first:until]
    query_spot = lax.broadcasted_iota(jnp.int32, (block, count), 0) + start
    key_spot = lax.broadcasted_iota(jnp.int32, (block, count), 1) + first
    bias[:, :count] = jnp.where((own == other) & (key_spot <= query_spot), 0.0, NEG)


def attend_kernel(heads, angles, projected, attended, sums, q_s, k_s, v_s, bias):
    seq_len, lanes = projected.shape
    block = min(256, seq_len)
    tile = 2 * HD
    for start in range(0, seq_len, block):
        rows = slice(start, start + block)
        turned, low, high = turn_tables(angles, rows)
        for number in range(lanes // tile):
            wide = turn(
                projected[rows, number * tile : (number + 1) * tile], number, turned, low, high
            )
            for side in range(2):
                head, kind = divmod(2 * number + side, 3)
                if head < heads:
                    part = wide[:, side * HD : (side + 1) * HD].astype(jnp.bfloat16)
                    (q_s, k_s, v_s)[kind][head, rows, :] = (
                        part * HD ** (-0.5) if kind == 0 else part
                    )
    for start in range(0, seq_len, block):
        first, until = key_range(start, block)
        count = until - first
        rows, keys = slice(start, until), slice(first, until)
        fill_bias(bias, angles, start, block)
        outs = []
        for h in range(heads):
            scores = times_trans(q_s[h, rows, :], k_s[h, keys, :]) + bias[:, :count]
            most = jnp.max(scores, axis=-1, keepdims=True)
            exponent = jnp.exp(scores - most)
            total = jnp.sum(exponent, axis=-1, keepdims=True)
            probs = (exponent * (1.0 / total)).astype(jnp.bfloat16)
            sums[rows, h : h + 1] = most + jnp.log(total)
            outs.append(product(probs, v_s[h, keys, :]))
        attended[rows, :] = jnp.concatenate(outs, axis=1).astype(jnp.bfloat16)


def attend_back_kernel(
    begin, heads, angles, q_s, k_s, v_s, sums, attended, d_attended, d_projected, dq_s, dk_s, dv_s, bias
):
    seq_len, lanes = d_projected.shape
    block = min(256, seq_len)
    tile = 2 * HD
    for start in range(0, seq_len, block):
        first, until = key_range(start, block)
        count = until - first
        rows, keys = slice(start, until), slice(first, until)
        fill_bias(bias, angles, start, block)
        for h in range(heads):
            g = begin + h
            q, k, v = q_s[g, rows, :], k_s[g, keys, :], v_s[g, keys, :]
            d_out = d_attended[rows, g * HD : (g + 1) * HD]
            out = attended[rows, g * HD : (g + 1) * HD]
            probs = jnp.exp(times_trans(q, k) + (bias[:, :count] - sums[rows, g : g + 1]))
            row_dot = jnp.sum(
                out.astype(jnp.float32) * d_out.astype(jnp.float32), axis=-1, keepdims=True
            )
            d_scores = (probs * (times_trans(d_out, v) - row_dot)).astype(jnp.bfloat16)
            dq_s[h, rows, :] = product(d_scores, k) * HD ** (-0.5)
            d_k = inner_rows(q, d_scores)
            d_v = inner_rows(d_out, probs.astype(jnp.bfloat16))
            old = count - block
            if old:
                dk_s[h, :, first:start] += d_k[:, :old]
                dv_s[h, :, first:start] += d_v[:, :old]
            dk_s[h, :, rows] = d_k[:, old:]
            dv_s[h, :, rows] = d_v[:, old:]
    for start in range(0, seq_len, block):
        rows = slice(start, start + block)
        turned, low, high = turn_tables(angles, rows)

        def section(at, rows=rows):
            head, kind = divmod(at, 3)
            if head >= heads:
                return jnp.zeros((block, HD), jnp.float32)
            return dq_s[head, rows, :] if kind == 0 else (dk_s, dv_s)[kind - 1][head, :, rows].T

        for number in range(lanes // tile):
            wide = jnp.concatenate([section(2 * number), section(2 * number + 1)], axis=1)
            d_projected[rows, number * tile : (number + 1) * tile] = turn(
                wide, number, turned, -low, -high
            ).astype(jnp.bfloat16)


VMEM = pl.BlockSpec(memory_space=pltpu.VMEM)


def bias_held(block):
    return pltpu.VMEM((block, -(-MOST // block) * block + block), jnp.float32)


def attend(angles, projected, heads):
    seq_len = projected.shape[0]
    shape = jax.ShapeDtypeStruct
    return pl.pallas_call(
        functools.partial(attend_kernel, heads),
        out_shape=(
            shape((seq_len, heads * HD), jnp.bfloat16),
            shape((seq_len, 2 * HD), jnp.float32),
        )
        + (shape((heads, seq_len, HD), jnp.bfloat16),) * 3,
        in_specs=[VMEM] * 2,
        out_specs=(VMEM,) * 5,
        scratch_shapes=[bias_held(min(256, seq_len))],
        compiler_params=pltpu.CompilerParams(vmem_limit_bytes=24 * 2**20),
    )(angles, projected)


def attend_back(angles, kept, d_attended, begin, heads, lanes):
    attended, sums, queries, keys, values = kept
    seq_len = attended.shape[0]
    cross = pltpu.VMEM((heads, HD, seq_len), jnp.float32)
    return pl.pallas_call(
        functools.partial(attend_back_kernel, begin, heads),
        out_shape=jax.ShapeDtypeStruct((seq_len, lanes), jnp.bfloat16),
        in_specs=[VMEM] * 7,
        out_specs=VMEM,
        scratch_shapes=[
            pltpu.VMEM((heads, seq_len, HD), jnp.float32),
            cross,
            cross,
            bias_held(min(256, seq_len)),
        ],
        compiler_params=pltpu.CompilerParams(vmem_limit_bytes=24 * 2**20),
    )(angles, queries, keys, values, sums, attended, d_attended)


def normed_rows(tokens):
    rows = tokens.astype(jnp.float32)
    centred = rows - jnp.mean(rows, axis=-1, keepdims=True)
    scale_inv = lax.rsqrt(jnp.mean(centred * centred, axis=-1, keepdims=True) + EPS)
    return centred * scale_inv, scale_inv


def tiled(width, tile, at=lambda i, *order: i):
    return pl.BlockSpec((tile, width), lambda i, *order: (at(i, *order), 0))


def whole(array):
    return pl.BlockSpec(array.shape, lambda i, *order: (0,) * array.ndim)


PARAMS = pltpu.CompilerParams(vmem_limit_bytes=40 * 2**20)


def forward_kernel(
    tokens,
    cotangent,
    attn_gain,
    attn_shift,
    mlp_gain,
    mlp_shift,
    w_qkv,
    b_qkv,
    w_out,
    w_up,
    b_up,
    attn_low,
    mlp_low,
    projected,
    d_attended,
    hidden,
    slope,
):
    normed, _ = normed_rows(tokens[...])
    attn_in = (normed * attn_gain[...] + attn_shift[...]).astype(jnp.bfloat16)
    mlp_in = (normed * mlp_gain[...] + mlp_shift[...]).astype(jnp.bfloat16)
    attn_low[...] = attn_in
    mlp_low[...] = mlp_in
    count, lanes = w_qkv.shape[1], projected.shape[1]
    if lanes > count:
        projected[...] = jnp.zeros(projected.shape, jnp.float32)
    projected[:, :count] = product(attn_in, w_qkv[...]) + b_qkv[...]
    d_attended[...] = times_trans(cotangent[...], w_out[...]).astype(jnp.bfloat16)
    pre_act = product(mlp_in, w_up[...]) + b_up[...]
    below = 0.5 * (1.0 + lax.erf(pre_act * (0.5**0.5)))
    bell = jnp.exp(-0.5 * pre_act * pre_act) * ((2.0 * math.pi) ** -0.5)
    hidden[...] = (pre_act * below).astype(jnp.bfloat16)
    slope[...] = (below + pre_act * bell).astype(slope.dtype)


def forward(tokens, cotangent, vectors, w_qkv, b_qkv, w_out, w_up, b_up, lanes):
    rows, width = tokens.shape
    tile = rows // 4
    fixed = (*vectors, w_qkv, b_qkv, w_out, w_up, b_up)
    outs = (
        (width, jnp.bfloat16),
        (width, jnp.bfloat16),
        (lanes, jnp.float32),
        (w_out.shape[0], jnp.bfloat16),
        (w_up.shape[1], jnp.bfloat16),
        (w_up.shape[1], jnp.float32),
    )
    return pl.pallas_call(
        forward_kernel,
        grid=(4,),
        in_specs=[tiled(width, tile)] * 2 + [whole(array) for array in fixed],
        out_specs=tuple(tiled(wide, tile) for wide, _ in outs),
        out_shape=tuple(jax.ShapeDtypeStruct((rows, wide), kind) for wide, kind in outs),
        compiler_params=PARAMS,
    )(tokens, cotangent, *fixed)


def feed_back_kernel(
    tokens, cotangent, slope, w_down, w_up, mlp_gain, d_pre, scaled, sums, bias_sum
):
    @pl.when(pl.program_id(0) == 0)
    def _():
        sums[...] = jnp.zeros(sums.shape, jnp.float32)
        bias_sum[...] = jnp.zeros(bias_sum.shape, jnp.float32)

    d_low = (times_trans(cotangent[...], w_down[...]) * slope[...]).astype(jnp.bfloat16)
    d_pre[...] = d_low
    d_in = times_trans(d_low, w_up[...])
    scaled[...] = d_in * mlp_gain[...]
    normed, _ = normed_rows(tokens[...])
    sums[0:1, :] += jnp.sum(d_in * normed, axis=0, keepdims=True)
    sums[1:2, :] += jnp.sum(d_in, axis=0, keepdims=True)
    bias_sum[...] += jnp.sum(d_low.astype(jnp.float32), axis=0, keepdims=True)


def feed_back(tokens, cotangent, slope, w_down, w_up, mlp_gain):
    rows, width = tokens.shape
    inner = w_up.shape[1]
    tile = rows // 4
    fixed = (w_down, w_up, mlp_gain)
    shape = jax.ShapeDtypeStruct
    out_shape = (
        shape((rows, inner), jnp.bfloat16),
        shape((rows, width), jnp.float32),
        shape((2, width), jnp.float32),
        shape((1, inner), jnp.float32),
    )
    return pl.pallas_call(
        feed_back_kernel,
        grid=(4,),
        in_specs=[tiled(width, tile)] * 2 + [tiled(inner, tile)] + [whole(a) for a in fixed],
        out_specs=(tiled(inner, tile), tiled(width, tile)) + tuple(whole(a) for a in out_shape[2:]),
        out_shape=out_shape,
        compiler_params=PARAMS,
    )(tokens, cotangent, slope, *fixed)


def quarter_outs(rows, width):
    shape = jax.ShapeDtypeStruct((rows // 4, width), jnp.float32)
    return (shape,) * 4


def branches_kernel(tiles, attended, hidden, w_out, w_down, *outs):
    total = product(attended[...], w_out[...]) + product(hidden[...], w_down[...])
    for number, out in enumerate(outs):

        @pl.when(pl.program_id(0) == number)
        def _(out=out):
            out[...] = total


def picked(i, tiles):
    return tiles[i]


def branches(tiles, attended, hidden, w_out, w_down):
    rows, width = hidden.shape[0], w_down.shape[1]
    outs = quarter_outs(rows, width)
    return pl.pallas_call(
        branches_kernel,
        grid_spec=pltpu.PrefetchScalarGridSpec(
            num_scalar_prefetch=1,
            grid=(4,),
            in_specs=[
                tiled(attended.shape[1], rows // 4, picked),
                tiled(hidden.shape[1], rows // 4, picked),
                whole(w_out),
                whole(w_down),
            ],
            out_specs=tuple(whole(out) for out in outs),
        ),
        out_shape=outs,
        compiler_params=PARAMS,
    )(tiles, attended, hidden, w_out, w_down)


def input_back_kernel(count, heads_wide, tiles, *refs):
    d_heads, rest = refs[:count], refs[count:]
    tokens, cotangent, before, w_qkv, attn_gain = rest[:5]
    outs, (sums, bias_sum, branch_sum) = rest[5:9], rest[9:]

    @pl.when(pl.program_id(0) == 0)
    def _():
        for held in (sums, bias_sum, branch_sum):
            held[...] = jnp.zeros(held.shape, jnp.float32)

    d_in = None
    for number, part in enumerate(d_heads):
        columns = slice(number * heads_wide, (number + 1) * heads_wide)
        low = part[:, :heads_wide]
        term = times_trans(low, w_qkv[:, columns])
        d_in = term if d_in is None else d_in + term
        bias_sum[:, columns] += jnp.sum(low.astype(jnp.float32), axis=0, keepdims=True)
    normed, _ = normed_rows(tokens[...])
    sums[0:1, :] += jnp.sum(d_in * normed, axis=0, keepdims=True)
    sums[1:2, :] += jnp.sum(d_in, axis=0, keepdims=True)
    branch_sum[...] += jnp.sum(cotangent[...].astype(jnp.float32), axis=0, keepdims=True)
    total = d_in * attn_gain[...] + before[...]
    for number, out in enumerate(outs):

        @pl.when(pl.program_id(0) == number)
        def _(out=out):
            out[...] = total


def input_back(tiles, d_heads, heads_wide, tokens, cotangent, before, w_qkv, attn_gain):
    rows, width = tokens.shape
    tile = rows // 4
    shape = jax.ShapeDtypeStruct
    outs = quarter_outs(rows, width) + (
        shape((2, width), jnp.float32),
        shape((1, w_qkv.shape[1]), jnp.float32),
        shape((1, width), jnp.float32),
    )
    return pl.pallas_call(
        functools.partial(input_back_kernel, len(d_heads), heads_wide),
        grid_spec=pltpu.PrefetchScalarGridSpec(
            num_scalar_prefetch=1,
            grid=(4,),
            in_specs=[tiled(part.shape[1], tile, picked) for part in d_heads]
            + [tiled(width, tile, picked)] * 3
            + [whole(w_qkv), whole(attn_gain)],
            out_specs=tuple(whole(out) for out in outs),
        ),
        out_shape=outs,
        compiler_params=PARAMS,
    )(tiles, *d_heads, tokens, cotangent, before, w_qkv, attn_gain)


def gradient_kernel(wide, tiles, first_mat, *refs):
    parts, (away, keep) = refs[:-2], refs[-2:]
    for number, part in enumerate(parts):
        block = inner_rows(first_mat[...], part[:, :wide])
        columns = slice(number * wide, (number + 1) * wide)

        @pl.when(pl.program_id(0) < pl.num_programs(0) // 2)
        def _(block=block, columns=columns):
            away[:, columns] = block

        @pl.when(pl.program_id(0) >= pl.num_programs(0) // 2)
        def _(block=block, columns=columns):
            keep[:, columns] = block


def gradient(core, first_mat, parts, wide):
    count, rows = first_mat.shape
    steps = 4 if rows >= 1024 else 2
    tile = rows // steps
    if tile % 128:
        full = inner_rows(
            first_mat, jnp.concatenate([part[:, :wide] for part in parts], axis=1)
        )
        return tuple(
            lax.dynamic_slice_in_dim(full, side * (rows // 2), rows // 2, 0)
            for side in (1 - core, core)
        )
    half = steps // 2
    tiles = (jnp.arange(steps, dtype=jnp.int32) + (1 - core) * half) % steps
    out = jax.ShapeDtypeStruct((rows // 2, wide * len(parts)), jnp.float32)
    columns = wide * len(parts)
    return pl.pallas_call(
        functools.partial(gradient_kernel, wide),
        grid_spec=pltpu.PrefetchScalarGridSpec(
            num_scalar_prefetch=1,
            grid=(steps,),
            in_specs=[pl.BlockSpec((count, tile), lambda i, tiles: (0, tiles[i]))]
            + [whole(part) for part in parts],
            out_specs=(
                tiled(columns, tile, lambda i, tiles: jnp.minimum(i, half - 1)),
                tiled(columns, tile, lambda i, tiles: jnp.maximum(i - half, 0)),
            ),
        ),
        out_shape=(out, out),
        compiler_params=PARAMS,
    )(tiles, first_mat, *parts)


class Order:
    def __init__(self, token):
        self.token = token

    def tie(self, *arrays):
        tied = lax.optimization_barrier((self.token, *arrays))
        self.token = tied[0]
        return tied[1] if len(arrays) == 1 else tied[1:]

    def run(self, step, *arrays):
        tied = lax.optimization_barrier((self.token, *arrays))
        out = step(*tied[1:])
        if isinstance(out, tuple):
            return self.tie(*out)
        return self.tie(out)


class Chain:
    def __init__(self, order, steps):
        self.order, self.steps, self.out, self.held = order, steps, None, None
        self._go(None)

    def _go(self, arrived):
        try:
            array, axis, pairs = self.steps.send(arrived)
        except StopIteration as stop:
            self.held, self.out = None, stop.value
            return
        array = self.order.tie(array)
        self.held = lax.ppermute(array, axis, pairs)

    def on(self):
        if self.held is not None:
            self._go(self.order.tie(self.held))
        return self

    def end(self):
        while self.held is not None:
            self.on()
        return self.out


def swap_pairs(size, bit):
    return [(i, i ^ bit) for i in range(size)]


def tensor_steps(away, keep, size, order, between):
    place = lax.axis_index("tensor")
    first = 0
    rows = away.shape[0]
    for number, bit in enumerate(order):
        mine = (place // bit) % 2
        if number:
            rows = rows // 2
            away = lax.dynamic_slice_in_dim(array, (1 - mine) * rows, rows, 0)
            keep = lax.dynamic_slice_in_dim(array, mine * rows, rows, 0)
        array = keep + (yield away, "tensor", swap_pairs(size, bit))
        first = first + mine * rows
    array = between(array, first)
    for bit in reversed(order):
        got = yield array, "tensor", swap_pairs(size, bit)
        mine = (place // bit) % 2
        array = jnp.where(
            mine == 0,
            jnp.concatenate([array, got], axis=0),
            jnp.concatenate([got, array], axis=0),
        )
    return array


def core_steps(parts, size, chunks):
    away, keep = parts
    got = yield away, "dp", swap_pairs(size, 1)
    rows = keep.shape[0] // chunks
    return [
        keep[c * rows : (c + 1) * rows] + got[c * rows : (c + 1) * rows] for c in range(chunks)
    ]


def line_steps(array, size, back=True):
    chips = size // 2
    place = lax.axis_index("dp") // 2

    def pairs(moves):
        return [(2 * a + c, 2 * b + c) for a, b in moves for c in range(2)]

    if chips > 1:
        steps = range(chips // 2 - 1)
        for s in steps:
            got = yield array, "dp", pairs([(s, s + 1), (chips - 1 - s, chips - 2 - s)])
            array = array + got
        middle = chips // 2
        got = yield array, "dp", pairs([(middle - 1, middle), (middle, middle - 1)])
        array = array + got
        for s in reversed(steps):
            got = yield array, "dp", pairs([(s + 1, s), (chips - 2 - s, chips - 1 - s)])
            array = jnp.where((place == s) | (place == chips - 1 - s), got, array)
    if not back:
        return array
    got = yield array, "dp", swap_pairs(size, 1)
    return array, got


def small_steps(stats, rest, tensor_size, dp_size):
    for bit in (1 << k for k in range(tensor_size.bit_length() - 1)):
        got = yield stats, "tensor", swap_pairs(tensor_size, bit)
        stats = stats + got
    vectors = jnp.concatenate([stats.reshape(-1), *rest])
    got = yield vectors, "dp", swap_pairs(dp_size, 1)
    return (yield from line_steps(vectors + got, dp_size, back=False))


def assemble(core, parts):
    low = [jnp.where(core == 0, mine, other) for mine, other in parts]
    high = [jnp.where(core == 0, other, mine) for mine, other in parts]
    return jnp.concatenate(low + high, axis=0)


def shards(
    dp_size,
    tensor_size,
    tokens,
    segment,
    attn_gain,
    attn_shift,
    mlp_gain,
    mlp_shift,
    w_qkv,
    b_qkv,
    w_out,
    w_up,
    b_up,
    w_down,
    b_branch,
    cotangent,
):
    rows_here, width = tokens.shape
    heads = w_qkv.shape[1] // (3 * HD)
    group = 2 if heads % 2 == 0 else heads
    wide = 3 * HD * group
    lanes = -(-wide // 128) * 128
    groups = heads // group
    bits = [1 << k for k in range(tensor_size.bit_length() - 1)]
    orders = (bits, bits[::-1])
    split = rows_here // 2
    core = lax.axis_index("dp") % 2
    place = lax.axis_index("tensor")
    order = Order(core)
    run = order.run
    mine = [(place // its[0]) % 2 for its in orders]
    tiles = jnp.stack([1 - mine[0], 3 - mine[1], mine[0], 2 + mine[1]]).astype(jnp.int32)

    def chain(steps):
        return Chain(order, steps)

    def lines(core_chain):
        return [line_steps(part, dp_size) for part in core_chain.end()]

    def grads(chunks, first_mat, *parts, wide=None):
        def step(first_mat, *parts):
            return gradient(core, first_mat, parts, wide or parts[0].shape[1])

        return chain(core_steps(run(step, first_mat, *parts), dp_size, chunks))

    vectors = [v[None, :] for v in (attn_gain, attn_shift, mlp_gain, mlp_shift)]
    attn_low, mlp_low, projected, d_attended, hidden, slope = run(
        lambda *a: forward(a[0], a[1], vectors, *a[2:], lanes=lanes * groups),
        tokens,
        cotangent,
        w_qkv,
        b_qkv[None, :],
        w_out,
        w_up,
        b_up[None, :],
    )
    core_down = grads(2, hidden, cotangent)
    d_pre, scaled_mlp, sums_mlp, up_bias = run(
        feed_back, tokens, cotangent, slope, w_down, w_up, mlp_gain[None, :]
    )
    down = lines(core_down)
    down[0] = chain(down[0])
    core_up = grads(2, mlp_low, d_pre)
    angles = run(turn_angles, segment[0])
    kept = run(functools.partial(attend, heads=heads), angles, projected)
    attended = kept[0]
    partial = run(branches, tiles, attended, hidden, w_out, w_down)
    result = [
        chain(tensor_steps(partial[p], partial[2 + p], tensor_size, orders[p], lambda rows, first: rows))
        for p in range(2)
    ]
    up = lines(core_up)
    down[0].on()
    down[1] = chain(down[1])

    back = []
    for begin in range(0, heads, group):
        def step(angles, d_attended, *kept, begin=begin):
            return attend_back(angles, kept, d_attended, begin, group, lanes)

        back.append(run(step, angles, d_attended, *kept))
    *scaled, sums_attn, qkv_bias, branch_sum = run(
        lambda tiles, *a: input_back(tiles, a[:-5], wide, *a[-5:]),
        tiles,
        *back,
        tokens,
        cotangent,
        scaled_mlp,
        w_qkv,
        attn_gain[None, :],
    )
    for part in result:
        part.on()
    core_qkv = grads(2, attn_low, *back, wide=wide)
    down[0].on()
    down[1].on()
    up[0] = chain(up[0])
    core_out = grads(1, attended, cotangent)
    qkv = lines(core_qkv)
    for part in result:
        part.on()
    out = lines(core_out)[0]

    def norm_back(part):
        def between(rows, first):
            at = first + part * split

            def here(whole):
                return lax.dynamic_slice_in_dim(whole, at, rows.shape[0], 0)

            normed, scale_inv = normed_rows(here(tokens))
            return here(cotangent).astype(jnp.float32) + scale_inv * (
                rows
                - jnp.mean(rows, axis=-1, keepdims=True)
                - normed * jnp.mean(rows * normed, axis=-1, keepdims=True)
            )

        return between

    for part in result:
        part.on()
    for part in (down[0], down[1], up[0]):
        part.on()
    up[1] = chain(up[1])
    small = chain(
        small_steps(
            jnp.concatenate([sums_attn, sums_mlp], axis=0),
            [v[0] for v in (qkv_bias, up_bias, branch_sum)],
            tensor_size,
            dp_size,
        )
    )
    down[0].end()
    small.on()

    def finish(tokens, *parts):
        summed = jnp.concatenate(parts, axis=0)
        return (tokens.astype(jnp.float32) + summed + b_branch).astype(jnp.bfloat16)

    ended = [part.end() for part in result]
    d_tokens = [
        chain(tensor_steps(scaled[p], scaled[2 + p], tensor_size, orders[p], norm_back(p)))
        for p in range(2)
    ]
    result = run(finish, tokens, *ended)
    for part in (down[1], up[0], up[1]):
        part.on()
    qkv[0] = chain(qkv[0])
    small.on()
    small.on()
    for part in d_tokens:
        part.on()
    down[1].end()
    grad_down = run(lambda *p: assemble(p[0], (p[1:3], p[3:5])), core, *down[0].end(), *down[1].end())
    for part in (up[0], up[1], qkv[0]):
        part.on()
    qkv[1] = chain(qkv[1])
    for part in d_tokens:
        part.on()
    small.on()
    up[0].end()
    for part in (up[1], qkv[0], qkv[1]):
        part.on()
    out = chain(out)
    for part in d_tokens:
        part.on()
    up[1].end()
    grad_up = run(lambda *p: assemble(p[0], (p[1:3], p[3:5])), core, *up[0].end(), *up[1].end())
    for part in (out, qkv[0], qkv[1]):
        part.on()
    vectors = small.end()
    qkv[0].end()
    for part in (out, qkv[1]):
        part.on()
    d_tokens = run(lambda *p: jnp.concatenate(p, axis=0), *(part.end() for part in d_tokens))
    qkv[1].end()
    grad_qkv = run(lambda *p: assemble(p[0], (p[1:3], p[3:5])), core, *qkv[0].end(), *qkv[1].end())
    grad_out = assemble(order.token, (out.end(),))

    sizes = (width,) * 4 + (w_qkv.shape[1], w_up.shape[1], width)
    ends = [sum(sizes[: k + 1]) for k in range(len(sizes))]
    a_gain, a_shift, m_gain, m_shift, qkv_bias, up_bias, branch = (
        vectors[end - size : end] for end, size in zip(ends, sizes, strict=True)
    )
    return (
        result,
        d_tokens,
        grad_qkv,
        qkv_bias,
        grad_out,
        grad_up,
        up_bias,
        grad_down,
        branch,
        a_gain,
        a_shift,
        m_gain,
        m_shift,
    )


def solution(mesh):
    placed = (
        P("dp", None),
        P("dp", None),
        P(),
        P(),
        P(),
        P(),
        P(None, "tensor"),
        P("tensor"),
        P("tensor", None),
        P(None, "tensor"),
        P("tensor"),
        P("tensor", None),
        P(),
        P("dp", None),
    )

    def body(*arrays):
        return shards(mesh.shape["dp"], mesh.shape["tensor"], *arrays)

    return jax.shard_map(
        body,
        mesh=mesh,
        in_specs=placed,
        out_specs=(
            P("dp", None),
            P("dp", None),
            P(None, "tensor"),
            P("tensor"),
            P("tensor", None),
            P(None, "tensor"),
            P("tensor"),
            P("tensor", None),
            P(),
            P(),
            P(),
            P(),
            P(),
        ),
        check_vma=False,
    )
```

```python
import functools
import math

import jax
import jax.numpy as jnp
from jax import lax
from jax.experimental import pallas as pl
from jax.experimental.pallas import tpu as pltpu
from jax.sharding import PartitionSpec as P

HD = 64
ROT = 16
MOST = 512

EPS = 1e-05
NEG = -1e30


def inner_rows(first_mat, second_mat):
    return lax.dot_general(
        first_mat, second_mat, (((0,), (0,)), ((), ())), preferred_element_type=jnp.float32
    )


def times_trans(first_mat, second_mat):
    return lax.dot_general(
        first_mat, second_mat, (((1,), (1,)), ((), ())), preferred_element_type=jnp.float32
    )


def product(first_mat, second_mat):
    return jnp.dot(first_mat, second_mat, preferred_element_type=jnp.float32)


def turn_angles(segment):
    spots = lax.broadcasted_iota(jnp.int32, segment.shape, 0)
    starts = jnp.zeros_like(segment)
    for number in range(3):
        count = jnp.sum((segment == number).astype(jnp.int32))
        starts = starts + jnp.where(segment > number, count, 0)
    offsets = (spots - starts).astype(jnp.float32)
    frequency = 10000.0 ** (-2.0 * jnp.arange(ROT // 2, dtype=jnp.float32) / ROT)
    angles = frequency[:, None] * offsets[None, :]
    number = jnp.broadcast_to(segment.astype(jnp.float32), (8, segment.shape[0]))
    return jnp.concatenate([jnp.cos(angles), jnp.sin(angles), number], axis=0)


def spread(angles, rows, take):
    return lax.dot_general(
        angles[0 : take.shape[0], rows],
        take,
        (((0,), (0,)), ((), ())),
        precision=lax.Precision.HIGHEST,
        preferred_element_type=jnp.float32,
    )


def turn_tables(angles, rows):
    tile, half = 2 * HD, ROT // 2
    source = lax.broadcasted_iota(jnp.int32, (ROT, tile), 0)
    column = lax.broadcasted_iota(jnp.int32, (ROT, tile), 1) % HD
    take_cos = ((source == column % half) & (column < ROT)).astype(jnp.float32)
    take_sin = source == column % half + half
    take_low = -(take_sin & (column < half)).astype(jnp.float32)
    take_high = (take_sin & (column >= half) & (column < ROT)).astype(jnp.float32)
    lane = lax.broadcasted_iota(jnp.int32, (rows.stop - rows.start, tile), 1)
    still = (lane % HD >= ROT).astype(jnp.float32)
    return (
        spread(angles, rows, take_cos) + still,
        spread(angles, rows, take_low),
        spread(angles, rows, take_high),
    )


def turn(wide, number, turned, low, high):
    tile, half = 2 * HD, ROT // 2
    lane = lax.broadcasted_iota(jnp.int32, wide.shape, 1)
    moved = (
        wide * turned
        + pltpu.roll(wide, tile - half, 1) * low
        + pltpu.roll(wide, half, 1) * high
    )
    if 2 * number % 3 == 2:
        return jnp.where(lane < HD, wide, moved)
    if (2 * number + 1) % 3 == 2:
        return jnp.where(lane >= HD, wide, moved)
    return moved


def key_range(start, block):
    return max(0, start - -(-MOST // block) * block), start + block


def fill_bias(bias, angles, start, block):
    first, until = key_range(start, block)
    count = until - first
    source = lax.broadcasted_iota(jnp.int32, (ROT + 8, 2 * HD), 0)
    own = spread(angles, slice(start, until), (source == ROT).astype(jnp.float32))[:, :1]
    other = angles[ROT : ROT + 1, first:until]
    query_spot = lax.broadcasted_iota(jnp.int32, (block, count), 0) + start
    key_spot = lax.broadcasted_iota(jnp.int32, (block, count), 1) + first
    bias[:, :count] = jnp.where((own == other) & (key_spot <= query_spot), 0.0, NEG)


def attend_kernel(heads, angles, projected, attended, sums, q_s, k_s, v_s, bias):
    seq_len, lanes = projected.shape
    block = min(256, seq_len)
    tile = 2 * HD
    for start in range(0, seq_len, block):
        rows = slice(start, start + block)
        turned, low, high = turn_tables(angles, rows)
        for number in range(lanes // tile):
            wide = turn(
                projected[rows, number * tile : (number + 1) * tile], number, turned, low, high
            )
            for side in range(2):
                head, kind = divmod(2 * number + side, 3)
                if head < heads:
                    part = wide[:, side * HD : (side + 1) * HD].astype(jnp.bfloat16)
                    (q_s, k_s, v_s)[kind][head, rows, :] = (
                        part * HD ** (-0.5) if kind == 0 else part
                    )
    for start in range(0, seq_len, block):
        first, until = key_range(start, block)
        count = until - first
        rows, keys = slice(start, until), slice(first, until)
        fill_bias(bias, angles, start, block)
        outs = []
        for h in range(heads):
            scores = times_trans(q_s[h, rows, :], k_s[h, keys, :]) + bias[:, :count]
            most = jnp.max(scores, axis=-1, keepdims=True)
            exponent = jnp.exp(scores - most)
            total = jnp.sum(exponent, axis=-1, keepdims=True)
            probs = (exponent * (1.0 / total)).astype(jnp.bfloat16)
            sums[rows, h : h + 1] = most + jnp.log(total)
            outs.append(product(probs, v_s[h, keys, :]))
        attended[rows, :] = jnp.concatenate(outs, axis=1).astype(jnp.bfloat16)


def attend_back_kernel(
    begin, heads, angles, q_s, k_s, v_s, sums, attended, d_attended, d_projected, dq_s, dk_s, dv_s, bias
):
    seq_len, lanes = d_projected.shape
    block = min(256, seq_len)
    tile = 2 * HD
    for start in range(0, seq_len, block):
        first, until = key_range(start, block)
        count = until - first
        rows, keys = slice(start, until), slice(first, until)
        fill_bias(bias, angles, start, block)
        for h in range(heads):
            g = begin + h
            q, k, v = q_s[g, rows, :], k_s[g, keys, :], v_s[g, keys, :]
            d_out = d_attended[rows, g * HD : (g + 1) * HD]
            out = attended[rows, g * HD : (g + 1) * HD]
            probs = jnp.exp(times_trans(q, k) + (bias[:, :count] - sums[rows, g : g + 1]))
            row_dot = jnp.sum(
                out.astype(jnp.float32) * d_out.astype(jnp.float32), axis=-1, keepdims=True
            )
            d_scores = (probs * (times_trans(d_out, v) - row_dot)).astype(jnp.bfloat16)
            dq_s[h, rows, :] = product(d_scores, k) * HD ** (-0.5)
            d_k = inner_rows(q, d_scores)
            d_v = inner_rows(d_out, probs.astype(jnp.bfloat16))
            old = count - block
            if old:
                dk_s[h, :, first:start] += d_k[:, :old]
                dv_s[h, :, first:start] += d_v[:, :old]
            dk_s[h, :, rows] = d_k[:, old:]
            dv_s[h, :, rows] = d_v[:, old:]
    for start in range(0, seq_len, block):
        rows = slice(start, start + block)
        turned, low, high = turn_tables(angles, rows)

        def section(at, rows=rows):
            head, kind = divmod(at, 3)
            if head >= heads:
                return jnp.zeros((block, HD), jnp.float32)
            return dq_s[head, rows, :] if kind == 0 else (dk_s, dv_s)[kind - 1][head, :, rows].T

        for number in range(lanes // tile):
            wide = jnp.concatenate([section(2 * number), section(2 * number + 1)], axis=1)
            d_projected[rows, number * tile : (number + 1) * tile] = turn(
                wide, number, turned, -low, -high
            ).astype(jnp.bfloat16)


VMEM = pl.BlockSpec(memory_space=pltpu.VMEM)


def bias_held(block):
    return pltpu.VMEM((block, -(-MOST // block) * block + block), jnp.float32)


def attend(angles, projected, heads):
    seq_len = projected.shape[0]
    shape = jax.ShapeDtypeStruct
    return pl.pallas_call(
        functools.partial(attend_kernel, heads),
        out_shape=(
            shape((seq_len, heads * HD), jnp.bfloat16),
            shape((seq_len, 2 * HD), jnp.float32),
        )
        + (shape((heads, seq_len, HD), jnp.bfloat16),) * 3,
        in_specs=[VMEM] * 2,
        out_specs=(VMEM,) * 5,
        scratch_shapes=[bias_held(min(256, seq_len))],
        compiler_params=pltpu.CompilerParams(vmem_limit_bytes=56 * 2**20),
    )(angles, projected)


def attend_back(angles, kept, d_attended, begin, heads, lanes):
    attended, sums, queries, keys, values = kept
    seq_len = attended.shape[0]
    cross = pltpu.VMEM((heads, HD, seq_len), jnp.float32)
    return pl.pallas_call(
        functools.partial(attend_back_kernel, begin, heads),
        out_shape=jax.ShapeDtypeStruct((seq_len, lanes), jnp.bfloat16),
        in_specs=[VMEM] * 7,
        out_specs=VMEM,
        scratch_shapes=[
            pltpu.VMEM((heads, seq_len, HD), jnp.float32),
            cross,
            cross,
            bias_held(min(256, seq_len)),
        ],
        compiler_params=pltpu.CompilerParams(vmem_limit_bytes=56 * 2**20),
    )(angles, queries, keys, values, sums, attended, d_attended)


def normed_rows(tokens):
    rows = tokens.astype(jnp.float32)
    centred = rows - jnp.mean(rows, axis=-1, keepdims=True)
    scale_inv = lax.rsqrt(jnp.mean(centred * centred, axis=-1, keepdims=True) + EPS)
    return centred * scale_inv, scale_inv


def tiled(width, tile, at=lambda i, *order: i):
    return pl.BlockSpec((tile, width), lambda i, *order: (at(i, *order), 0))


def whole(array):
    return pl.BlockSpec(array.shape, lambda i, *order: (0,) * array.ndim)


PARAMS = pltpu.CompilerParams(vmem_limit_bytes=56 * 2**20)


def forward_kernel(
    tokens,
    cotangent,
    attn_gain,
    attn_shift,
    mlp_gain,
    mlp_shift,
    w_qkv,
    b_qkv,
    w_out,
    w_up,
    b_up,
    attn_low,
    mlp_low,
    projected,
    d_attended,
    hidden,
    slope,
):
    normed, _ = normed_rows(tokens[...])
    attn_in = (normed * attn_gain[...] + attn_shift[...]).astype(jnp.bfloat16)
    mlp_in = (normed * mlp_gain[...] + mlp_shift[...]).astype(jnp.bfloat16)
    attn_low[...] = attn_in
    mlp_low[...] = mlp_in
    count, lanes = w_qkv.shape[1], projected.shape[1]
    if lanes > count:
        projected[...] = jnp.zeros(projected.shape, jnp.float32)
    projected[:, :count] = product(attn_in, w_qkv[...]) + b_qkv[...]
    d_attended[...] = times_trans(cotangent[...], w_out[...]).astype(jnp.bfloat16)
    pre_act = product(mlp_in, w_up[...]) + b_up[...]
    below = 0.5 * (1.0 + lax.erf(pre_act * (0.5**0.5)))
    bell = jnp.exp(-0.5 * pre_act * pre_act) * ((2.0 * math.pi) ** -0.5)
    hidden[...] = (pre_act * below).astype(jnp.bfloat16)
    slope[...] = (below + pre_act * bell).astype(slope.dtype)


def forward(tokens, cotangent, vectors, w_qkv, b_qkv, w_out, w_up, b_up, lanes):
    rows, width = tokens.shape
    tile = rows // 4
    fixed = (*vectors, w_qkv, b_qkv, w_out, w_up, b_up)
    outs = (
        (width, jnp.bfloat16),
        (width, jnp.bfloat16),
        (lanes, jnp.float32),
        (w_out.shape[0], jnp.bfloat16),
        (w_up.shape[1], jnp.bfloat16),
        (w_up.shape[1], jnp.float32),
    )
    return pl.pallas_call(
        forward_kernel,
        grid=(4,),
        in_specs=[tiled(width, tile)] * 2 + [whole(array) for array in fixed],
        out_specs=tuple(tiled(wide, tile) for wide, _ in outs),
        out_shape=tuple(jax.ShapeDtypeStruct((rows, wide), kind) for wide, kind in outs),
        compiler_params=PARAMS,
    )(tokens, cotangent, *fixed)


def feed_back_kernel(
    tokens, cotangent, slope, w_down, w_up, mlp_gain, d_pre, scaled, sums, bias_sum
):
    @pl.when(pl.program_id(0) == 0)
    def _():
        sums[...] = jnp.zeros(sums.shape, jnp.float32)
        bias_sum[...] = jnp.zeros(bias_sum.shape, jnp.float32)

    d_low = (times_trans(cotangent[...], w_down[...]) * slope[...]).astype(jnp.bfloat16)
    d_pre[...] = d_low
    d_in = times_trans(d_low, w_up[...])
    scaled[...] = d_in * mlp_gain[...]
    normed, _ = normed_rows(tokens[...])
    sums[0:1, :] += jnp.sum(d_in * normed, axis=0, keepdims=True)
    sums[1:2, :] += jnp.sum(d_in, axis=0, keepdims=True)
    bias_sum[...] += jnp.sum(d_low.astype(jnp.float32), axis=0, keepdims=True)


def feed_back(tokens, cotangent, slope, w_down, w_up, mlp_gain):
    rows, width = tokens.shape
    inner = w_up.shape[1]
    tile = rows // 4
    fixed = (w_down, w_up, mlp_gain)
    shape = jax.ShapeDtypeStruct
    out_shape = (
        shape((rows, inner), jnp.bfloat16),
        shape((rows, width), jnp.float32),
        shape((2, width), jnp.float32),
        shape((1, inner), jnp.float32),
    )
    return pl.pallas_call(
        feed_back_kernel,
        grid=(4,),
        in_specs=[tiled(width, tile)] * 2 + [tiled(inner, tile)] + [whole(a) for a in fixed],
        out_specs=(tiled(inner, tile), tiled(width, tile)) + tuple(whole(a) for a in out_shape[2:]),
        out_shape=out_shape,
        compiler_params=PARAMS,
    )(tokens, cotangent, slope, *fixed)


def quarter_outs(rows, width):
    shape = jax.ShapeDtypeStruct((rows // 4, width), jnp.float32)
    return (shape,) * 4


def branches_kernel(tiles, attended, hidden, w_out, w_down, *outs):
    total = product(attended[...], w_out[...]) + product(hidden[...], w_down[...])
    for number, out in enumerate(outs):

        @pl.when(pl.program_id(0) == number)
        def _(out=out):
            out[...] = total


def picked(i, tiles):
    return tiles[i]


def branches(tiles, attended, hidden, w_out, w_down):
    rows, width = hidden.shape[0], w_down.shape[1]
    outs = quarter_outs(rows, width)
    return pl.pallas_call(
        branches_kernel,
        grid_spec=pltpu.PrefetchScalarGridSpec(
            num_scalar_prefetch=1,
            grid=(4,),
            in_specs=[
                tiled(attended.shape[1], rows // 4, picked),
                tiled(hidden.shape[1], rows // 4, picked),
                whole(w_out),
                whole(w_down),
            ],
            out_specs=tuple(whole(out) for out in outs),
        ),
        out_shape=outs,
        compiler_params=PARAMS,
    )(tiles, attended, hidden, w_out, w_down)


def input_back_kernel(count, heads_wide, tiles, *refs):
    d_heads, rest = refs[:count], refs[count:]
    tokens, cotangent, before, w_qkv, attn_gain = rest[:5]
    outs, (sums, bias_sum, branch_sum) = rest[5:9], rest[9:]

    @pl.when(pl.program_id(0) == 0)
    def _():
        for held in (sums, bias_sum, branch_sum):
            held[...] = jnp.zeros(held.shape, jnp.float32)

    d_in = None
    for number, part in enumerate(d_heads):
        columns = slice(number * heads_wide, (number + 1) * heads_wide)
        low = part[:, :heads_wide]
        term = times_trans(low, w_qkv[:, columns])
        d_in = term if d_in is None else d_in + term
        bias_sum[:, columns] += jnp.sum(low.astype(jnp.float32), axis=0, keepdims=True)
    normed, _ = normed_rows(tokens[...])
    sums[0:1, :] += jnp.sum(d_in * normed, axis=0, keepdims=True)
    sums[1:2, :] += jnp.sum(d_in, axis=0, keepdims=True)
    branch_sum[...] += jnp.sum(cotangent[...].astype(jnp.float32), axis=0, keepdims=True)
    total = d_in * attn_gain[...] + before[...]
    for number, out in enumerate(outs):

        @pl.when(pl.program_id(0) == number)
        def _(out=out):
            out[...] = total


def input_back(tiles, d_heads, heads_wide, tokens, cotangent, before, w_qkv, attn_gain):
    rows, width = tokens.shape
    tile = rows // 4
    shape = jax.ShapeDtypeStruct
    outs = quarter_outs(rows, width) + (
        shape((2, width), jnp.float32),
        shape((1, w_qkv.shape[1]), jnp.float32),
        shape((1, width), jnp.float32),
    )
    return pl.pallas_call(
        functools.partial(input_back_kernel, len(d_heads), heads_wide),
        grid_spec=pltpu.PrefetchScalarGridSpec(
            num_scalar_prefetch=1,
            grid=(4,),
            in_specs=[tiled(part.shape[1], tile, picked) for part in d_heads]
            + [tiled(width, tile, picked)] * 3
            + [whole(w_qkv), whole(attn_gain)],
            out_specs=tuple(whole(out) for out in outs),
        ),
        out_shape=outs,
        compiler_params=PARAMS,
    )(tiles, *d_heads, tokens, cotangent, before, w_qkv, attn_gain)


def gradient_kernel(wide, tiles, first_mat, *refs):
    parts, outs = refs[:-2], refs[-2:]
    for number, part in enumerate(parts):
        block = inner_rows(first_mat[...], part[:, :wide])
        columns = slice(number * wide, (number + 1) * wide)
        for side, out in enumerate(outs):

            @pl.when(pl.program_id(0) // (pl.num_programs(0) // 2) == side)
            def _(out=out, block=block, columns=columns):
                out[:, columns] = block


def gradient(swapped, first_mat, parts, wide, begin=0, rows=None):
    count = first_mat.shape[0]
    rows = rows or first_mat.shape[1]
    steps = 4 if rows >= 1024 else 2
    tile = rows // steps
    half = steps // 2
    columns = wide * len(parts)
    if tile % 128:
        full = inner_rows(
            first_mat[:, begin : begin + rows],
            jnp.concatenate([part[:, :wide] for part in parts], axis=1),
        )
        return tuple(
            lax.dynamic_slice_in_dim(full, side * (rows // 2), rows // 2, 0)
            for side in (swapped, 1 - swapped)
        )
    tiles = (jnp.arange(steps, dtype=jnp.int32) + swapped * half) % steps + begin // tile
    out = jax.ShapeDtypeStruct((rows // 2, columns), jnp.float32)
    return pl.pallas_call(
        functools.partial(gradient_kernel, wide),
        grid_spec=pltpu.PrefetchScalarGridSpec(
            num_scalar_prefetch=1,
            grid=(steps,),
            in_specs=[pl.BlockSpec((count, tile), lambda i, tiles: (0, tiles[i]))]
            + [whole(part) for part in parts],
            out_specs=(
                tiled(columns, tile, lambda i, tiles: jnp.minimum(i, half - 1)),
                tiled(columns, tile, lambda i, tiles: jnp.maximum(i - half, 0)),
            ),
        ),
        out_shape=(out, out),
        compiler_params=PARAMS,
    )(tiles, first_mat, *parts)


def float_shape(rows, width):
    return jax.ShapeDtypeStruct((rows, width), jnp.float32)


def steps_for(rows):
    return 2 if rows % 16 == 0 else 1


def scalars(*values):
    return jnp.stack([jnp.asarray(value, jnp.int32) for value in values])


def add_kernel(first, second, out):
    out[...] = first[...] + second[...]


def add(first, second):
    rows, width = first.shape
    steps = steps_for(rows)
    spec = tiled(width, rows // steps)
    return pl.pallas_call(
        add_kernel,
        grid=(steps,),
        in_specs=[spec] * 2,
        out_specs=spec,
        out_shape=float_shape(rows, width),
        compiler_params=PARAMS,
    )(first, second)


def choose_kernel(flag, first, second, out):
    @pl.when(flag[0] == 1)
    def _():
        out[...] = first[...]

    @pl.when(flag[0] == 0)
    def _():
        out[...] = second[...]


def choose(flag, first, second):
    rows, width = first.shape
    steps = steps_for(rows)
    spec = tiled(width, rows // steps)
    return pl.pallas_call(
        choose_kernel,
        grid_spec=pltpu.PrefetchScalarGridSpec(
            num_scalar_prefetch=1, grid=(steps,), in_specs=[spec] * 2, out_specs=spec
        ),
        out_shape=float_shape(rows, width),
        compiler_params=PARAMS,
    )(scalars(flag), first, second)


def add_parts_kernel(first, second, *outs):
    total = first[...] + second[...]
    for number, out in enumerate(outs):

        @pl.when(pl.program_id(0) == number)
        def _(out=out):
            out[...] = total


def add_parts(first, second, parts):
    rows, width = first.shape
    outs = (float_shape(rows // parts, width),) * parts
    spec = tiled(width, rows // parts)
    return pl.pallas_call(
        add_parts_kernel,
        grid=(parts,),
        in_specs=[spec] * 2,
        out_specs=tuple(whole(out) for out in outs),
        out_shape=outs,
        compiler_params=PARAMS,
    )(first, second)


def add_split_kernel(mine, first, second, away, keep):
    total = first[...] + second[...]

    @pl.when(pl.program_id(0) == 0)
    def _():
        away[...] = total

    @pl.when(pl.program_id(0) == 1)
    def _():
        keep[...] = total


def add_split(mine, first, second):
    rows, width = first.shape
    outs = (float_shape(rows // 2, width),) * 2
    spec = tiled(width, rows // 2, lambda i, mine: (i + 1 + mine[0]) % 2)
    return pl.pallas_call(
        add_split_kernel,
        grid_spec=pltpu.PrefetchScalarGridSpec(
            num_scalar_prefetch=1,
            grid=(2,),
            in_specs=[spec] * 2,
            out_specs=tuple(whole(out) for out in outs),
        ),
        out_shape=outs,
        compiler_params=PARAMS,
    )(scalars(mine), first, second)


def norm_back_kernel(at, first, second, tokens, cotangent, out):
    rows = first[...] + second[...]
    normed, scale_inv = normed_rows(tokens[...])
    out[...] = cotangent[...].astype(jnp.float32) + scale_inv * (
        rows
        - jnp.mean(rows, axis=-1, keepdims=True)
        - normed * jnp.mean(rows * normed, axis=-1, keepdims=True)
    )


def norm_back(first, second, at, tokens, cotangent):
    rows, width = first.shape
    spec = pl.BlockSpec((rows, width), lambda i, at: (0, 0))
    moved = pl.BlockSpec((rows, width), lambda i, at: (at[0], 0))
    return pl.pallas_call(
        norm_back_kernel,
        grid_spec=pltpu.PrefetchScalarGridSpec(
            num_scalar_prefetch=1,
            grid=(1,),
            in_specs=[spec, spec, moved, moved],
            out_specs=spec,
        ),
        out_shape=float_shape(rows, width),
        compiler_params=PARAMS,
    )(scalars(at // rows), first, second, tokens, cotangent)


def join_kernel(mine, own, other, out):
    @pl.when(pl.program_id(0) == mine[0])
    def _():
        out[...] = own[...]

    @pl.when(pl.program_id(0) != mine[0])
    def _():
        out[...] = other[...]


def join(mine, own, other):
    rows, width = own.shape
    return pl.pallas_call(
        join_kernel,
        grid_spec=pltpu.PrefetchScalarGridSpec(
            num_scalar_prefetch=1,
            grid=(2,),
            in_specs=[pl.BlockSpec((rows, width), lambda i, mine: (0, 0))] * 2,
            out_specs=tiled(width, rows, lambda i, mine: i),
        ),
        out_shape=float_shape(2 * rows, width),
        compiler_params=PARAMS,
    )(scalars(mine), own, other)


def collect_kernel(order, *refs):
    parts, out = refs[:4], refs[-1]
    extra = refs[4:-1]
    for number, part in enumerate(parts):

        @pl.when(order[pl.program_id(0)] == number)
        def _(part=part):
            if extra:
                tokens, bias = extra
                total = tokens[...].astype(jnp.float32) + part[...] + bias[...]
                out[...] = total.astype(out.dtype)
            else:
                out[...] = part[...]


def collect(order, parts, *extra):
    rows, width = parts[0].shape
    specs = [pl.BlockSpec((rows, width), lambda i, order: (0, 0))] * 4
    if extra:
        specs = specs + [tiled(width, rows, lambda i, order: i), whole(extra[1])]
    return pl.pallas_call(
        collect_kernel,
        grid_spec=pltpu.PrefetchScalarGridSpec(
            num_scalar_prefetch=1,
            grid=(4,),
            in_specs=specs,
            out_specs=tiled(width, rows, lambda i, order: i),
        ),
        out_shape=jax.ShapeDtypeStruct(
            (4 * rows, width), extra[0].dtype if extra else jnp.float32
        ),
        compiler_params=PARAMS,
    )(order, *parts, *extra)


class Order:
    def __init__(self, token):
        self.token = token

    def tie(self, *arrays):
        tied = lax.optimization_barrier((self.token, *arrays))
        self.token = tied[0]
        return tied[1] if len(arrays) == 1 else tied[1:]

    def run(self, step, *arrays):
        tied = lax.optimization_barrier((self.token, *arrays))
        out = step(*tied[1:])
        out = tuple(out) if isinstance(out, list) else out
        if isinstance(out, tuple):
            return self.tie(*out)
        return self.tie(out)


class Chain:
    def __init__(self, order, steps):
        self.order, self.steps, self.out, self.held = order, steps, None, None
        self._go(None)

    def _go(self, arrived):
        try:
            array, axis, pairs = self.steps.send(arrived)
        except StopIteration as stop:
            self.held, self.out = None, stop.value
            return
        array = self.order.tie(array)
        self.held = lax.ppermute(array, axis, pairs)

    def on(self):
        if self.held is not None:
            self._go(self.order.tie(self.held))
        return self

    def end(self):
        while self.held is not None:
            self.on()
        return self.out


def swap_pairs(size, bit):
    return [(i, i ^ bit) for i in range(size)]


def tensor_steps(away, keep, size, order, finish):
    place = lax.axis_index("tensor")
    first = 0
    rows = away.shape[0]
    for number, bit in enumerate(order):
        got = yield away, "tensor", swap_pairs(size, bit)
        first = first + (place // bit) % 2 * rows
        if number + 1 < len(order):
            away, keep = add_split((place // order[number + 1]) % 2, keep, got)
            rows = rows // 2
    array = finish(keep, got, first)
    for number, bit in enumerate(reversed(order)):
        got = yield array, "tensor", swap_pairs(size, bit)
        if number + 1 < len(order):
            array = join((place // bit) % 2, array, got)
    return array, got


def core_steps(parts, size, chunks):
    away, keep = parts
    got = yield away, "dp", swap_pairs(size, 1)
    return add_parts(keep, got, chunks)


def line_steps(array, size):
    chips = size // 2
    place = lax.axis_index("dp") // 2

    def pairs(moves):
        return [(2 * a + c, 2 * b + c) for a, b in moves for c in range(2)]

    if chips > 1:
        steps = range(chips // 2 - 1)
        for s in steps:
            got = yield array, "dp", pairs([(s, s + 1), (chips - 1 - s, chips - 2 - s)])
            array = add(array, got)
        middle = chips // 2
        got = yield array, "dp", pairs([(middle - 1, middle), (middle, middle - 1)])
        array = add(array, got)
        for s in reversed(steps):
            got = yield array, "dp", pairs([(s + 1, s), (chips - 2 - s, chips - 1 - s)])
            array = choose((place == s) | (place == chips - 1 - s), got, array)
    got = yield array, "dp", swap_pairs(size, 1)
    return array, got


def small_steps(stats, size):
    for bit in (1 << k for k in range(size.bit_length() - 1)):
        got = yield stats, "tensor", swap_pairs(size, bit)
        stats = stats + got
    return stats


def assemble(core, parts):
    low = [jnp.where(core == 0, mine, other) for mine, other in parts]
    high = [jnp.where(core == 0, other, mine) for mine, other in parts]
    return jnp.concatenate(low + high, axis=0)


def shards(
    dp_size,
    tensor_size,
    tokens,
    segment,
    attn_gain,
    attn_shift,
    mlp_gain,
    mlp_shift,
    w_qkv,
    b_qkv,
    w_out,
    w_up,
    b_up,
    w_down,
    b_branch,
    cotangent,
):
    rows_here, width = tokens.shape
    heads = w_qkv.shape[1] // (3 * HD)
    group = 2 if heads % 2 == 0 else heads
    wide = 3 * HD * group
    lanes = -(-wide // 128) * 128
    groups = heads // group
    bits = [1 << k for k in range(tensor_size.bit_length() - 1)]
    orders = (bits, bits[::-1])
    split = rows_here // 2
    core = lax.axis_index("dp") % 2
    place = lax.axis_index("tensor")
    order = Order(core)
    run = order.run
    mine = [(place // its[0]) % 2 for its in orders]
    tiles = jnp.stack([1 - mine[0], 3 - mine[1], mine[0], 2 + mine[1]]).astype(jnp.int32)

    def chain(steps):
        return Chain(order, steps)

    def lines(core_chain):
        return [line_steps(part, dp_size) for part in core_chain.end()]

    def grads(chunks, first_mat, *parts, wide=None, begin=0, rows=None):
        def step(first_mat, *parts):
            return gradient(1 - core, first_mat, parts, wide or parts[0].shape[1], begin, rows)

        return chain(core_steps(run(step, first_mat, *parts), dp_size, chunks))

    vectors = [v[None, :] for v in (attn_gain, attn_shift, mlp_gain, mlp_shift)]
    attn_low, mlp_low, projected, d_attended, hidden, slope = run(
        lambda *a: forward(a[0], a[1], vectors, *a[2:], lanes=lanes * groups),
        tokens,
        cotangent,
        w_qkv,
        b_qkv[None, :],
        w_out,
        w_up,
        b_up[None, :],
    )
    inner = hidden.shape[1]
    core_down = grads(1, hidden, cotangent, begin=inner // 2, rows=inner // 2)
    top = run(
        lambda h, dy: gradient(0, h, [dy], width, 0, inner // 2), hidden, cotangent
    )
    top = lax.psum(top, "dp")
    angles = run(turn_angles, segment[0])
    down = chain(lines(core_down)[0])
    d_pre, scaled_mlp, sums_mlp, up_bias = run(
        feed_back, tokens, cotangent, slope, w_down, w_up, mlp_gain[None, :]
    )
    core_up = grads(2, mlp_low, d_pre)
    kept = run(functools.partial(attend, heads=heads), angles, projected)
    attended = kept[0]
    up = lines(core_up)
    down.on()
    up[0] = chain(up[0])
    partial = run(branches, tiles, attended, hidden, w_out, w_down)
    result = [
        chain(
            tensor_steps(
                partial[p],
                partial[2 + p],
                tensor_size,
                orders[p],
                lambda keep, got, first: add(keep, got),
            )
        )
        for p in range(2)
    ]
    back = []
    for begin in range(0, heads, group):
        def step(angles, d_attended, *kept, begin=begin):
            return attend_back(angles, kept, d_attended, begin, group, lanes)

        back.append(run(step, angles, d_attended, *kept))
    down.on()
    up[0].on()
    up[1] = chain(up[1])
    *scaled, sums_attn, qkv_bias, branch_sum = run(
        lambda tiles, *a: input_back(tiles, a[:-5], wide, *a[-5:]),
        tiles,
        *back,
        tokens,
        cotangent,
        scaled_mlp,
        w_qkv,
        attn_gain[None, :],
    )
    top = order.tie(*top)
    for part in result:
        part.on()
    small = chain(small_steps(jnp.concatenate([sums_attn, sums_mlp], axis=0), tensor_size))
    core_qkv = grads(2, attn_low, *back, wide=wide)
    small.on()
    grad_out = run(inner_rows, attended, cotangent)
    qkv = lines(core_qkv)
    stats = small.end()
    for part in result:
        part.on()
    for part in (down, up[0], up[1]):
        part.on()
    qkv[0] = chain(qkv[0])

    sizes = (width,) * 4 + (w_qkv.shape[1], w_up.shape[1], width)
    ends = [sum(sizes[: k + 1]) for k in range(len(sizes))]
    flat = jnp.concatenate([stats.reshape(-1), qkv_bias[0], up_bias[0], branch_sum[0]])
    spare = -(-flat.shape[0] // width // 16) * 16
    flat = jnp.pad(flat, (0, spare * width - flat.shape[0])).reshape(spare, width)

    def pack(grad_out, flat):
        packed = jnp.concatenate([grad_out, flat], axis=0)
        rows = packed.shape[0] // 2
        return tuple(
            lax.dynamic_slice_in_dim(packed, side * rows, rows, 0) for side in (1 - core, core)
        )

    core_out = chain(core_steps(run(pack, grad_out, flat), dp_size, 1))

    def back_end(part):
        def finish(keep, got, first):
            return norm_back(keep, got, first + part * split, tokens, cotangent)

        return finish

    out = lines(core_out)[0]
    for part in result:
        part.on()
    down.end()
    d_tokens = [
        chain(tensor_steps(scaled[p], scaled[2 + p], tensor_size, orders[p], back_end(p)))
        for p in range(2)
    ]
    for part in (up[0], up[1], qkv[0]):
        part.on()
    qkv[1] = chain(qkv[1])
    grad_down = run(collect, scalars(0, 1, 2 + core, 3 - core), [*top, *down.end()])
    spots = scalars(mine[0], 1 - mine[0], 2 + mine[1], 3 - mine[1])
    up[0].end()
    ended = [part.end() for part in result]
    for part in d_tokens:
        part.on()
    result = run(collect, spots, [*ended[0], *ended[1]], tokens, b_branch[None, :])
    for part in (up[1], qkv[0], qkv[1]):
        part.on()
    out = chain(out)
    up[1].end()
    for part in d_tokens:
        part.on()
    core_spots = jnp.where(core == 0, scalars(0, 2, 1, 3), scalars(1, 3, 0, 2))
    grad_up = run(collect, core_spots, [*up[0].end(), *up[1].end()])
    for part in (qkv[0], qkv[1], out):
        part.on()
    for part in d_tokens:
        part.on()
    qkv[0].end()
    for part in (qkv[1], out):
        part.on()
    qkv[1].end()
    grad_qkv = run(collect, core_spots, [*qkv[0].end(), *qkv[1].end()])
    ended = [part.end() for part in d_tokens]
    out.on()
    d_tokens = run(collect, spots, [*ended[0], *ended[1]])
    packed = order.tie(assemble(core, (out.end(),)))
    grad_out = packed[: w_out.shape[0]]
    vectors = packed[w_out.shape[0] :].reshape(-1)
    a_gain, a_shift, m_gain, m_shift, qkv_bias, up_bias, branch = (
        vectors[end - size : end] for end, size in zip(ends, sizes, strict=True)
    )
    return (
        result,
        d_tokens,
        grad_qkv,
        qkv_bias,
        grad_out,
        grad_up,
        up_bias,
        grad_down,
        branch,
        a_gain,
        a_shift,
        m_gain,
        m_shift,
    )


def solution(mesh):
    placed = (
        P("dp", None),
        P("dp", None),
        P(),
        P(),
        P(),
        P(),
        P(None, "tensor"),
        P("tensor"),
        P("tensor", None),
        P(None, "tensor"),
        P("tensor"),
        P("tensor", None),
        P(),
        P("dp", None),
    )

    def body(*arrays):
        return shards(mesh.shape["dp"], mesh.shape["tensor"], *arrays)

    return jax.shard_map(
        body,
        mesh=mesh,
        in_specs=placed,
        out_specs=(
            P("dp", None),
            P("dp", None),
            P(None, "tensor"),
            P("tensor"),
            P("tensor", None),
            P(None, "tensor"),
            P("tensor"),
            P("tensor", None),
            P(),
            P(),
            P(),
            P(),
            P(),
        ),
        check_vma=False,
    )
```

```python
import functools
import math

import jax
import jax.numpy as jnp
from jax import lax
from jax.experimental import pallas as pl
from jax.experimental.pallas import tpu as pltpu
from jax.sharding import PartitionSpec as P

HD = 64
ROT = 16
MOST = 512

EPS = 1e-05
NEG = -1e30


def inner_rows(first_mat, second_mat):
    return lax.dot_general(
        first_mat, second_mat, (((0,), (0,)), ((), ())), preferred_element_type=jnp.float32
    )


def times_trans(first_mat, second_mat):
    return lax.dot_general(
        first_mat, second_mat, (((1,), (1,)), ((), ())), preferred_element_type=jnp.float32
    )


def product(first_mat, second_mat):
    return jnp.dot(first_mat, second_mat, preferred_element_type=jnp.float32)


def turn_angles(segment):
    spots = lax.broadcasted_iota(jnp.int32, segment.shape, 0)
    starts = jnp.zeros_like(segment)
    for number in range(3):
        count = jnp.sum((segment == number).astype(jnp.int32))
        starts = starts + jnp.where(segment > number, count, 0)
    offsets = (spots - starts).astype(jnp.float32)
    frequency = 10000.0 ** (-2.0 * jnp.arange(ROT // 2, dtype=jnp.float32) / ROT)
    angles = frequency[:, None] * offsets[None, :]
    number = jnp.broadcast_to(segment.astype(jnp.float32), (8, segment.shape[0]))
    return jnp.concatenate([jnp.cos(angles), jnp.sin(angles), number], axis=0)


def spread(angles, rows, take):
    return lax.dot_general(
        angles[0 : take.shape[0], rows],
        take,
        (((0,), (0,)), ((), ())),
        precision=lax.Precision.HIGHEST,
        preferred_element_type=jnp.float32,
    )


def turn_tables(angles, rows):
    tile, half = 2 * HD, ROT // 2
    source = lax.broadcasted_iota(jnp.int32, (ROT, tile), 0)
    column = lax.broadcasted_iota(jnp.int32, (ROT, tile), 1) % HD
    take_cos = ((source == column % half) & (column < ROT)).astype(jnp.float32)
    take_sin = source == column % half + half
    take_low = -(take_sin & (column < half)).astype(jnp.float32)
    take_high = (take_sin & (column >= half) & (column < ROT)).astype(jnp.float32)
    lane = lax.broadcasted_iota(jnp.int32, (rows.stop - rows.start, tile), 1)
    still = (lane % HD >= ROT).astype(jnp.float32)
    return (
        spread(angles, rows, take_cos) + still,
        spread(angles, rows, take_low),
        spread(angles, rows, take_high),
    )


def turn(wide, number, turned, low, high):
    tile, half = 2 * HD, ROT // 2
    lane = lax.broadcasted_iota(jnp.int32, wide.shape, 1)
    moved = (
        wide * turned
        + pltpu.roll(wide, tile - half, 1) * low
        + pltpu.roll(wide, half, 1) * high
    )
    if 2 * number % 3 == 2:
        return jnp.where(lane < HD, wide, moved)
    if (2 * number + 1) % 3 == 2:
        return jnp.where(lane >= HD, wide, moved)
    return moved


def key_range(start, block):
    return max(0, start - -(-MOST // block) * block), start + block


def fill_bias(bias, angles, start, block):
    first, until = key_range(start, block)
    count = until - first
    source = lax.broadcasted_iota(jnp.int32, (ROT + 8, 2 * HD), 0)
    own = spread(angles, slice(start, until), (source == ROT).astype(jnp.float32))[:, :1]
    other = angles[ROT : ROT + 1, first:until]
    query_spot = lax.broadcasted_iota(jnp.int32, (block, count), 0) + start
    key_spot = lax.broadcasted_iota(jnp.int32, (block, count), 1) + first
    bias[:, :count] = jnp.where((own == other) & (key_spot <= query_spot), 0.0, NEG)


def attend_kernel(heads, angles, projected, attended, sums, q_s, k_s, v_s, bias):
    seq_len, lanes = projected.shape
    block = min(256, seq_len)
    tile = 2 * HD
    for start in range(0, seq_len, block):
        rows = slice(start, start + block)
        turned, low, high = turn_tables(angles, rows)
        for number in range(lanes // tile):
            wide = turn(
                projected[rows, number * tile : (number + 1) * tile], number, turned, low, high
            )
            for side in range(2):
                head, kind = divmod(2 * number + side, 3)
                if head < heads:
                    part = wide[:, side * HD : (side + 1) * HD].astype(jnp.bfloat16)
                    (q_s, k_s, v_s)[kind][head, rows, :] = (
                        part * HD ** (-0.5) if kind == 0 else part
                    )
    for start in range(0, seq_len, block):
        first, until = key_range(start, block)
        count = until - first
        rows, keys = slice(start, until), slice(first, until)
        fill_bias(bias, angles, start, block)
        outs = []
        for h in range(heads):
            scores = times_trans(q_s[h, rows, :], k_s[h, keys, :]) + bias[:, :count]
            most = jnp.max(scores, axis=-1, keepdims=True)
            exponent = jnp.exp(scores - most)
            total = jnp.sum(exponent, axis=-1, keepdims=True)
            probs = (exponent * (1.0 / total)).astype(jnp.bfloat16)
            sums[rows, h : h + 1] = most + jnp.log(total)
            outs.append(product(probs, v_s[h, keys, :]))
        attended[rows, :] = jnp.concatenate(outs, axis=1).astype(jnp.bfloat16)


def attend_back_kernel(
    begin, heads, angles, q_s, k_s, v_s, sums, attended, d_attended, d_projected, dq_s, dk_s, dv_s, bias
):
    seq_len, lanes = d_projected.shape
    block = min(256, seq_len)
    tile = 2 * HD
    for start in range(0, seq_len, block):
        first, until = key_range(start, block)
        count = until - first
        rows, keys = slice(start, until), slice(first, until)
        fill_bias(bias, angles, start, block)
        for h in range(heads):
            g = begin + h
            q, k, v = q_s[g, rows, :], k_s[g, keys, :], v_s[g, keys, :]
            d_out = d_attended[rows, g * HD : (g + 1) * HD]
            out = attended[rows, g * HD : (g + 1) * HD]
            probs = jnp.exp(times_trans(q, k) + (bias[:, :count] - sums[rows, g : g + 1]))
            row_dot = jnp.sum(
                out.astype(jnp.float32) * d_out.astype(jnp.float32), axis=-1, keepdims=True
            )
            d_scores = (probs * (times_trans(d_out, v) - row_dot)).astype(jnp.bfloat16)
            dq_s[h, rows, :] = product(d_scores, k) * HD ** (-0.5)
            d_k = inner_rows(q, d_scores)
            d_v = inner_rows(d_out, probs.astype(jnp.bfloat16))
            old = count - block
            if old:
                dk_s[h, :, first:start] += d_k[:, :old]
                dv_s[h, :, first:start] += d_v[:, :old]
            dk_s[h, :, rows] = d_k[:, old:]
            dv_s[h, :, rows] = d_v[:, old:]
    for start in range(0, seq_len, block):
        rows = slice(start, start + block)
        turned, low, high = turn_tables(angles, rows)

        def section(at, rows=rows):
            head, kind = divmod(at, 3)
            if head >= heads:
                return jnp.zeros((block, HD), jnp.float32)
            return dq_s[head, rows, :] if kind == 0 else (dk_s, dv_s)[kind - 1][head, :, rows].T

        for number in range(lanes // tile):
            wide = jnp.concatenate([section(2 * number), section(2 * number + 1)], axis=1)
            d_projected[rows, number * tile : (number + 1) * tile] = turn(
                wide, number, turned, -low, -high
            ).astype(jnp.bfloat16)


VMEM = pl.BlockSpec(memory_space=pltpu.VMEM)


def bias_held(block):
    return pltpu.VMEM((block, -(-MOST // block) * block + block), jnp.float32)


def attend(angles, projected, heads):
    seq_len = projected.shape[0]
    shape = jax.ShapeDtypeStruct
    return pl.pallas_call(
        functools.partial(attend_kernel, heads),
        out_shape=(
            shape((seq_len, heads * HD), jnp.bfloat16),
            shape((seq_len, 2 * HD), jnp.float32),
        )
        + (shape((heads, seq_len, HD), jnp.bfloat16),) * 3,
        in_specs=[VMEM] * 2,
        out_specs=(VMEM,) * 5,
        scratch_shapes=[bias_held(min(256, seq_len))],
        compiler_params=pltpu.CompilerParams(vmem_limit_bytes=24 * 2**20),
    )(angles, projected)


def attend_back(angles, kept, d_attended, begin, heads, lanes):
    attended, sums, queries, keys, values = kept
    seq_len = attended.shape[0]
    cross = pltpu.VMEM((heads, HD, seq_len), jnp.float32)
    return pl.pallas_call(
        functools.partial(attend_back_kernel, begin, heads),
        out_shape=jax.ShapeDtypeStruct((seq_len, lanes), jnp.bfloat16),
        in_specs=[VMEM] * 7,
        out_specs=VMEM,
        scratch_shapes=[
            pltpu.VMEM((heads, seq_len, HD), jnp.float32),
            cross,
            cross,
            bias_held(min(256, seq_len)),
        ],
        compiler_params=pltpu.CompilerParams(vmem_limit_bytes=24 * 2**20),
    )(angles, queries, keys, values, sums, attended, d_attended)


def normed_rows(tokens):
    rows = tokens.astype(jnp.float32)
    centred = rows - jnp.mean(rows, axis=-1, keepdims=True)
    scale_inv = lax.rsqrt(jnp.mean(centred * centred, axis=-1, keepdims=True) + EPS)
    return centred * scale_inv, scale_inv


def tiled(width, tile, at=lambda i, *order: i):
    return pl.BlockSpec((tile, width), lambda i, *order: (at(i, *order), 0))


def whole(array):
    return pl.BlockSpec(array.shape, lambda i, *order: (0,) * array.ndim)


PARAMS = pltpu.CompilerParams(vmem_limit_bytes=32 * 2**20)


def forward_kernel(
    tokens,
    cotangent,
    attn_gain,
    attn_shift,
    mlp_gain,
    mlp_shift,
    w_qkv,
    b_qkv,
    w_out,
    w_up,
    b_up,
    attn_low,
    mlp_low,
    projected,
    d_attended,
    hidden,
    slope,
):
    normed, _ = normed_rows(tokens[...])
    attn_in = (normed * attn_gain[...] + attn_shift[...]).astype(jnp.bfloat16)
    mlp_in = (normed * mlp_gain[...] + mlp_shift[...]).astype(jnp.bfloat16)
    attn_low[...] = attn_in
    mlp_low[...] = mlp_in
    count, lanes = w_qkv.shape[1], projected.shape[1]
    if lanes > count:
        projected[...] = jnp.zeros(projected.shape, jnp.float32)
    projected[:, :count] = product(attn_in, w_qkv[...]) + b_qkv[...]
    d_attended[...] = times_trans(cotangent[...], w_out[...]).astype(jnp.bfloat16)
    pre_act = product(mlp_in, w_up[...]) + b_up[...]
    below = 0.5 * (1.0 + lax.erf(pre_act * (0.5**0.5)))
    bell = jnp.exp(-0.5 * pre_act * pre_act) * ((2.0 * math.pi) ** -0.5)
    hidden[...] = (pre_act * below).astype(jnp.bfloat16)
    slope[...] = (below + pre_act * bell).astype(slope.dtype)


def forward(tokens, cotangent, vectors, w_qkv, b_qkv, w_out, w_up, b_up, lanes):
    rows, width = tokens.shape
    tile = rows // 4
    fixed = (*vectors, w_qkv, b_qkv, w_out, w_up, b_up)
    outs = (
        (width, jnp.bfloat16),
        (width, jnp.bfloat16),
        (lanes, jnp.float32),
        (w_out.shape[0], jnp.bfloat16),
        (w_up.shape[1], jnp.bfloat16),
        (w_up.shape[1], jnp.float32),
    )
    return pl.pallas_call(
        forward_kernel,
        grid=(4,),
        in_specs=[tiled(width, tile)] * 2 + [whole(array) for array in fixed],
        out_specs=tuple(tiled(wide, tile) for wide, _ in outs),
        out_shape=tuple(jax.ShapeDtypeStruct((rows, wide), kind) for wide, kind in outs),
        compiler_params=PARAMS,
    )(tokens, cotangent, *fixed)


def feed_back_kernel(
    tokens, cotangent, slope, w_down, w_up, mlp_gain, d_pre, scaled, sums, bias_sum
):
    @pl.when(pl.program_id(0) == 0)
    def _():
        sums[...] = jnp.zeros(sums.shape, jnp.float32)
        bias_sum[...] = jnp.zeros(bias_sum.shape, jnp.float32)

    d_low = (times_trans(cotangent[...], w_down[...]) * slope[...]).astype(jnp.bfloat16)
    d_pre[...] = d_low
    d_in = times_trans(d_low, w_up[...])
    scaled[...] = d_in * mlp_gain[...]
    normed, _ = normed_rows(tokens[...])
    sums[0:1, :] += jnp.sum(d_in * normed, axis=0, keepdims=True)
    sums[1:2, :] += jnp.sum(d_in, axis=0, keepdims=True)
    bias_sum[...] += jnp.sum(d_low.astype(jnp.float32), axis=0, keepdims=True)


def feed_back(tokens, cotangent, slope, w_down, w_up, mlp_gain):
    rows, width = tokens.shape
    inner = w_up.shape[1]
    tile = rows // 4
    fixed = (w_down, w_up, mlp_gain)
    shape = jax.ShapeDtypeStruct
    out_shape = (
        shape((rows, inner), jnp.bfloat16),
        shape((rows, width), jnp.float32),
        shape((2, width), jnp.float32),
        shape((1, inner), jnp.float32),
    )
    return pl.pallas_call(
        feed_back_kernel,
        grid=(4,),
        in_specs=[tiled(width, tile)] * 2 + [tiled(inner, tile)] + [whole(a) for a in fixed],
        out_specs=(tiled(inner, tile), tiled(width, tile)) + tuple(whole(a) for a in out_shape[2:]),
        out_shape=out_shape,
        compiler_params=PARAMS,
    )(tokens, cotangent, slope, *fixed)


def quarter_outs(rows, width):
    shape = jax.ShapeDtypeStruct((rows // 4, width), jnp.float32)
    return (shape,) * 4


def branches_kernel(tiles, attended, hidden, w_out, w_down, *outs):
    total = product(attended[...], w_out[...]) + product(hidden[...], w_down[...])
    for number, out in enumerate(outs):

        @pl.when(pl.program_id(0) == number)
        def _(out=out):
            out[...] = total


def picked(i, tiles):
    return tiles[i]


def branches(tiles, attended, hidden, w_out, w_down):
    rows, width = hidden.shape[0], w_down.shape[1]
    outs = quarter_outs(rows, width)
    return pl.pallas_call(
        branches_kernel,
        grid_spec=pltpu.PrefetchScalarGridSpec(
            num_scalar_prefetch=1,
            grid=(4,),
            in_specs=[
                tiled(attended.shape[1], rows // 4, picked),
                tiled(hidden.shape[1], rows // 4, picked),
                whole(w_out),
                whole(w_down),
            ],
            out_specs=tuple(whole(out) for out in outs),
        ),
        out_shape=outs,
        compiler_params=PARAMS,
    )(tiles, attended, hidden, w_out, w_down)


def input_back_kernel(count, heads_wide, tiles, *refs):
    d_heads, rest = refs[:count], refs[count:]
    tokens, cotangent, before, w_qkv, attn_gain = rest[:5]
    outs, (sums, bias_sum, branch_sum) = rest[5:9], rest[9:]

    @pl.when(pl.program_id(0) == 0)
    def _():
        for held in (sums, bias_sum, branch_sum):
            held[...] = jnp.zeros(held.shape, jnp.float32)

    d_in = None
    for number, part in enumerate(d_heads):
        columns = slice(number * heads_wide, (number + 1) * heads_wide)
        low = part[:, :heads_wide]
        term = times_trans(low, w_qkv[:, columns])
        d_in = term if d_in is None else d_in + term
        bias_sum[:, columns] += jnp.sum(low.astype(jnp.float32), axis=0, keepdims=True)
    normed, _ = normed_rows(tokens[...])
    sums[0:1, :] += jnp.sum(d_in * normed, axis=0, keepdims=True)
    sums[1:2, :] += jnp.sum(d_in, axis=0, keepdims=True)
    branch_sum[...] += jnp.sum(cotangent[...].astype(jnp.float32), axis=0, keepdims=True)
    total = d_in * attn_gain[...] + before[...]
    for number, out in enumerate(outs):

        @pl.when(pl.program_id(0) == number)
        def _(out=out):
            out[...] = total


def input_back(tiles, d_heads, heads_wide, tokens, cotangent, before, w_qkv, attn_gain):
    rows, width = tokens.shape
    tile = rows // 4
    shape = jax.ShapeDtypeStruct
    outs = quarter_outs(rows, width) + (
        shape((2, width), jnp.float32),
        shape((1, w_qkv.shape[1]), jnp.float32),
        shape((1, width), jnp.float32),
    )
    return pl.pallas_call(
        functools.partial(input_back_kernel, len(d_heads), heads_wide),
        grid_spec=pltpu.PrefetchScalarGridSpec(
            num_scalar_prefetch=1,
            grid=(4,),
            in_specs=[tiled(part.shape[1], tile, picked) for part in d_heads]
            + [tiled(width, tile, picked)] * 3
            + [whole(w_qkv), whole(attn_gain)],
            out_specs=tuple(whole(out) for out in outs),
        ),
        out_shape=outs,
        compiler_params=PARAMS,
    )(tiles, *d_heads, tokens, cotangent, before, w_qkv, attn_gain)


def plain_gradient_kernel(first_mat, second_mat, out):
    out[...] = inner_rows(first_mat[...], second_mat[...])


def plain_gradient(first_mat, second_mat):
    count, rows = first_mat.shape
    steps = 4 if rows % 512 == 0 else 2
    tile = rows // steps
    if tile % 128:
        return inner_rows(first_mat, second_mat)
    return pl.pallas_call(
        plain_gradient_kernel,
        grid=(steps,),
        in_specs=[pl.BlockSpec((count, tile), lambda i: (0, i)), whole(second_mat)],
        out_specs=tiled(second_mat.shape[1], tile),
        out_shape=jax.ShapeDtypeStruct((rows, second_mat.shape[1]), jnp.float32),
        compiler_params=PARAMS,
    )(first_mat, second_mat)


def gradient_kernel(wide, tiles, first_mat, *refs):
    parts, outs = refs[:-2], refs[-2:]
    for number, part in enumerate(parts):
        block = inner_rows(first_mat[...], part[:, :wide])
        columns = slice(number * wide, (number + 1) * wide)
        for side, out in enumerate(outs):

            @pl.when(pl.program_id(0) // (pl.num_programs(0) // 2) == side)
            def _(out=out, block=block, columns=columns):
                out[:, columns] = block


def gradient(swapped, first_mat, parts, wide, begin=0, rows=None):
    count = first_mat.shape[0]
    rows = rows or first_mat.shape[1]
    steps = 4 if rows >= 1024 else 2
    tile = rows // steps
    half = steps // 2
    columns = wide * len(parts)
    if tile % 128:
        full = inner_rows(
            first_mat[:, begin : begin + rows],
            jnp.concatenate([part[:, :wide] for part in parts], axis=1),
        )
        return tuple(
            lax.dynamic_slice_in_dim(full, side * (rows // 2), rows // 2, 0)
            for side in (swapped, 1 - swapped)
        )
    tiles = (jnp.arange(steps, dtype=jnp.int32) + swapped * half) % steps + begin // tile
    out = jax.ShapeDtypeStruct((rows // 2, columns), jnp.float32)
    return pl.pallas_call(
        functools.partial(gradient_kernel, wide),
        grid_spec=pltpu.PrefetchScalarGridSpec(
            num_scalar_prefetch=1,
            grid=(steps,),
            in_specs=[pl.BlockSpec((count, tile), lambda i, tiles: (0, tiles[i]))]
            + [whole(part) for part in parts],
            out_specs=(
                tiled(columns, tile, lambda i, tiles: jnp.minimum(i, half - 1)),
                tiled(columns, tile, lambda i, tiles: jnp.maximum(i - half, 0)),
            ),
        ),
        out_shape=(out, out),
        compiler_params=PARAMS,
    )(tiles, first_mat, *parts)


def float_shape(rows, width):
    return jax.ShapeDtypeStruct((rows, width), jnp.float32)


def steps_for(rows):
    return 2 if rows % 16 == 0 else 1


def scalars(*values):
    return jnp.stack([jnp.asarray(value, jnp.int32) for value in values])


def add_kernel(first, second, out):
    out[...] = first[...] + second[...]


def add(first, second):
    rows, width = first.shape
    steps = steps_for(rows)
    spec = tiled(width, rows // steps)
    return pl.pallas_call(
        add_kernel,
        grid=(steps,),
        in_specs=[spec] * 2,
        out_specs=spec,
        out_shape=float_shape(rows, width),
        compiler_params=PARAMS,
    )(first, second)


def choose_kernel(flag, first, second, out):
    @pl.when(flag[0] == 1)
    def _():
        out[...] = first[...]

    @pl.when(flag[0] == 0)
    def _():
        out[...] = second[...]


def choose(flag, first, second):
    rows, width = first.shape
    steps = steps_for(rows)
    spec = tiled(width, rows // steps)
    return pl.pallas_call(
        choose_kernel,
        grid_spec=pltpu.PrefetchScalarGridSpec(
            num_scalar_prefetch=1, grid=(steps,), in_specs=[spec] * 2, out_specs=spec
        ),
        out_shape=float_shape(rows, width),
        compiler_params=PARAMS,
    )(scalars(flag), first, second)


def add_parts_kernel(first, second, *outs):
    total = first[...] + second[...]
    for number, out in enumerate(outs):

        @pl.when(pl.program_id(0) == number)
        def _(out=out):
            out[...] = total


def add_parts(first, second, parts):
    rows, width = first.shape
    outs = (float_shape(rows // parts, width),) * parts
    spec = tiled(width, rows // parts)
    return pl.pallas_call(
        add_parts_kernel,
        grid=(parts,),
        in_specs=[spec] * 2,
        out_specs=tuple(whole(out) for out in outs),
        out_shape=outs,
        compiler_params=PARAMS,
    )(first, second)


def add_split_kernel(mine, first, second, away, keep):
    total = first[...] + second[...]

    @pl.when(pl.program_id(0) == 0)
    def _():
        away[...] = total

    @pl.when(pl.program_id(0) == 1)
    def _():
        keep[...] = total


def add_split(mine, first, second):
    rows, width = first.shape
    outs = (float_shape(rows // 2, width),) * 2
    spec = tiled(width, rows // 2, lambda i, mine: (i + 1 + mine[0]) % 2)
    return pl.pallas_call(
        add_split_kernel,
        grid_spec=pltpu.PrefetchScalarGridSpec(
            num_scalar_prefetch=1,
            grid=(2,),
            in_specs=[spec] * 2,
            out_specs=tuple(whole(out) for out in outs),
        ),
        out_shape=outs,
        compiler_params=PARAMS,
    )(scalars(mine), first, second)


def norm_back_kernel(at, first, second, tokens, cotangent, out):
    rows = first[...] + second[...]
    normed, scale_inv = normed_rows(tokens[...])
    out[...] = cotangent[...].astype(jnp.float32) + scale_inv * (
        rows
        - jnp.mean(rows, axis=-1, keepdims=True)
        - normed * jnp.mean(rows * normed, axis=-1, keepdims=True)
    )


def norm_back(first, second, at, tokens, cotangent):
    rows, width = first.shape
    spec = pl.BlockSpec((rows, width), lambda i, at: (0, 0))
    moved = pl.BlockSpec((rows, width), lambda i, at: (at[0], 0))
    return pl.pallas_call(
        norm_back_kernel,
        grid_spec=pltpu.PrefetchScalarGridSpec(
            num_scalar_prefetch=1,
            grid=(1,),
            in_specs=[spec, spec, moved, moved],
            out_specs=spec,
        ),
        out_shape=float_shape(rows, width),
        compiler_params=PARAMS,
    )(scalars(at // rows), first, second, tokens, cotangent)


def join_kernel(mine, own, other, out):
    @pl.when(pl.program_id(0) == mine[0])
    def _():
        out[...] = own[...]

    @pl.when(pl.program_id(0) != mine[0])
    def _():
        out[...] = other[...]


def join(mine, own, other):
    rows, width = own.shape
    return pl.pallas_call(
        join_kernel,
        grid_spec=pltpu.PrefetchScalarGridSpec(
            num_scalar_prefetch=1,
            grid=(2,),
            in_specs=[pl.BlockSpec((rows, width), lambda i, mine: (0, 0))] * 2,
            out_specs=tiled(width, rows, lambda i, mine: i),
        ),
        out_shape=float_shape(2 * rows, width),
        compiler_params=PARAMS,
    )(scalars(mine), own, other)


def collect_kernel(order, *refs):
    parts, out = refs[:4], refs[-1]
    extra = refs[4:-1]
    for number, part in enumerate(parts):

        @pl.when(order[pl.program_id(0)] == number)
        def _(part=part):
            if extra:
                tokens, bias = extra
                total = tokens[...].astype(jnp.float32) + part[...] + bias[...]
                out[...] = total.astype(out.dtype)
            else:
                out[...] = part[...]


def collect(order, parts, *extra):
    rows, width = parts[0].shape
    specs = [pl.BlockSpec((rows, width), lambda i, order: (0, 0))] * 4
    if extra:
        specs = specs + [tiled(width, rows, lambda i, order: i), whole(extra[1])]
    return pl.pallas_call(
        collect_kernel,
        grid_spec=pltpu.PrefetchScalarGridSpec(
            num_scalar_prefetch=1,
            grid=(4,),
            in_specs=specs,
            out_specs=tiled(width, rows, lambda i, order: i),
        ),
        out_shape=jax.ShapeDtypeStruct(
            (4 * rows, width), extra[0].dtype if extra else jnp.float32
        ),
        compiler_params=PARAMS,
    )(order, *parts, *extra)


class Order:
    def __init__(self, token):
        self.token = token

    def tie(self, *arrays):
        tied = lax.optimization_barrier((self.token, *arrays))
        self.token = tied[0]
        return tied[1] if len(arrays) == 1 else tied[1:]

    def run(self, step, *arrays):
        tied = lax.optimization_barrier((self.token, *arrays))
        out = step(*tied[1:])
        out = tuple(out) if isinstance(out, list) else out
        if isinstance(out, tuple):
            return self.tie(*out)
        return self.tie(out)


class Chain:
    def __init__(self, order, steps):
        self.order, self.steps, self.out, self.held = order, steps, None, None
        self._go(None)

    def _go(self, arrived):
        try:
            array, axis, pairs = self.steps.send(arrived)
        except StopIteration as stop:
            self.held, self.out = None, stop.value
            return
        array = self.order.tie(array)
        self.held = lax.ppermute(array, axis, pairs)

    def on(self):
        if self.held is not None:
            self._go(self.order.tie(self.held))
        return self

    def end(self):
        while self.held is not None:
            self.on()
        return self.out


def swap_pairs(size, bit):
    return [(i, i ^ bit) for i in range(size)]


def tensor_steps(away, keep, size, order, finish):
    place = lax.axis_index("tensor")
    first = 0
    rows = away.shape[0]
    for number, bit in enumerate(order):
        got = yield away, "tensor", swap_pairs(size, bit)
        first = first + (place // bit) % 2 * rows
        if number + 1 < len(order):
            away, keep = add_split((place // order[number + 1]) % 2, keep, got)
            rows = rows // 2
    array = finish(keep, got, first)
    for number, bit in enumerate(reversed(order)):
        got = yield array, "tensor", swap_pairs(size, bit)
        if number + 1 < len(order):
            array = join((place // bit) % 2, array, got)
    return array, got


def core_steps(parts, size, chunks):
    away, keep = parts
    got = yield away, "dp", swap_pairs(size, 1)
    return add_parts(keep, got, chunks)


def line_steps(array, size):
    chips = size // 2
    place = lax.axis_index("dp") // 2

    def pairs(moves):
        return [(2 * a + c, 2 * b + c) for a, b in moves for c in range(2)]

    if chips > 1:
        steps = range(chips // 2 - 1)
        for s in steps:
            got = yield array, "dp", pairs([(s, s + 1), (chips - 1 - s, chips - 2 - s)])
            array = add(array, got)
        middle = chips // 2
        got = yield array, "dp", pairs([(middle - 1, middle), (middle, middle - 1)])
        array = add(array, got)
        for s in reversed(steps):
            got = yield array, "dp", pairs([(s + 1, s), (chips - 2 - s, chips - 1 - s)])
            array = choose((place == s) | (place == chips - 1 - s), got, array)
    got = yield array, "dp", swap_pairs(size, 1)
    return array, got


def add_end(keep, got, first):
    return add(keep, got)


def small_steps(stats, size):
    for bit in (1 << k for k in range(size.bit_length() - 1)):
        got = yield stats, "tensor", swap_pairs(size, bit)
        stats = stats + got
    return stats


def assemble(core, parts):
    low = [jnp.where(core == 0, mine, other) for mine, other in parts]
    high = [jnp.where(core == 0, other, mine) for mine, other in parts]
    return jnp.concatenate(low + high, axis=0)


def shards(
    dp_size,
    tensor_size,
    tokens,
    segment,
    attn_gain,
    attn_shift,
    mlp_gain,
    mlp_shift,
    w_qkv,
    b_qkv,
    w_out,
    w_up,
    b_up,
    w_down,
    b_branch,
    cotangent,
):
    rows_here, width = tokens.shape
    heads = w_qkv.shape[1] // (3 * HD)
    group = 2 if heads % 2 == 0 else heads
    wide = 3 * HD * group
    lanes = -(-wide // 128) * 128
    groups = heads // group
    bits = [1 << k for k in range(tensor_size.bit_length() - 1)]
    orders = (bits, bits[::-1])
    split = rows_here // 2
    core = lax.axis_index("dp") % 2
    place = lax.axis_index("tensor")
    order = Order(core)
    run = order.run
    mine = [(place // its[0]) % 2 for its in orders]
    tiles = jnp.stack([1 - mine[0], 3 - mine[1], mine[0], 2 + mine[1]]).astype(jnp.int32)

    def chain(steps):
        return Chain(order, steps)

    def lines(core_chain):
        return [line_steps(part, dp_size) for part in core_chain.end()]

    def grads(chunks, first_mat, *parts, wide=None, begin=0, rows=None):
        def step(first_mat, *parts):
            return gradient(1 - core, first_mat, parts, wide or parts[0].shape[1], begin, rows)

        return chain(core_steps(run(step, first_mat, *parts), dp_size, chunks))

    vectors = [v[None, :] for v in (attn_gain, attn_shift, mlp_gain, mlp_shift)]
    angles = run(turn_angles, segment[0])
    attn_low, mlp_low, projected, d_attended, hidden, slope = run(
        lambda *a: forward(a[0], a[1], vectors, *a[2:], lanes=lanes * groups),
        tokens,
        cotangent,
        w_qkv,
        b_qkv[None, :],
        w_out,
        w_up,
        b_up[None, :],
    )
    kept = run(functools.partial(attend, heads=heads), angles, projected)
    attended = kept[0]
    partial = run(branches, tiles, attended, hidden, w_out, w_down)
    result = [
        chain(tensor_steps(partial[p], partial[2 + p], tensor_size, orders[p], add_end))
        for p in range(2)
    ]
    grad_down = run(plain_gradient, hidden, cotangent)
    d_pre, scaled_mlp, sums_mlp, up_bias = run(
        feed_back, tokens, cotangent, slope, w_down, w_up, mlp_gain[None, :]
    )
    summed = lax.psum((grad_down, run(plain_gradient, mlp_low, d_pre)), "dp")
    back = []
    for begin in range(0, heads, group):
        def step(angles, d_attended, *kept, begin=begin):
            return attend_back(angles, kept, d_attended, begin, group, lanes)

        back.append(run(step, angles, d_attended, *kept))
    for part in result:
        part.on()
    *scaled, sums_attn, qkv_bias, branch_sum = run(
        lambda tiles, *a: input_back(tiles, a[:-5], wide, *a[-5:]),
        tiles,
        *back,
        tokens,
        cotangent,
        scaled_mlp,
        w_qkv,
        attn_gain[None, :],
    )
    small = chain(small_steps(jnp.concatenate([sums_attn, sums_mlp], axis=0), tensor_size))
    core_qkv = grads(2, attn_low, *back, wide=wide)
    for part in result:
        part.on()
    small.on()
    grad_out = run(inner_rows, attended, cotangent)
    qkv = lines(core_qkv)
    qkv[0] = chain(qkv[0])
    for part in result:
        part.on()

    def back_end(part):
        def finish(keep, got, first):
            return norm_back(keep, got, first + part * split, tokens, cotangent)

        return finish

    d_tokens = [
        chain(tensor_steps(scaled[p], scaled[2 + p], tensor_size, orders[p], back_end(p)))
        for p in range(2)
    ]
    stats = small.end()

    sizes = (width,) * 4 + (w_qkv.shape[1], w_up.shape[1], width)
    ends = [sum(sizes[: k + 1]) for k in range(len(sizes))]
    flat = jnp.concatenate([stats.reshape(-1), qkv_bias[0], up_bias[0], branch_sum[0]])
    spare = -(-flat.shape[0] // width // 16) * 16
    flat = jnp.pad(flat, (0, spare * width - flat.shape[0])).reshape(spare, width)

    def pack(grad_out, flat):
        packed = jnp.concatenate([grad_out, flat], axis=0)
        rows = packed.shape[0] // 2
        return tuple(
            lax.dynamic_slice_in_dim(packed, side * rows, rows, 0) for side in (1 - core, core)
        )

    core_out = chain(core_steps(run(pack, grad_out, flat), dp_size, 1))
    qkv[0].on()
    qkv[1] = chain(qkv[1])
    spots = scalars(mine[0], 1 - mine[0], 2 + mine[1], 3 - mine[1])
    out = lines(core_out)[0]
    ended = [part.end() for part in result]
    for part in (qkv[0], qkv[1]):
        part.on()
    out = chain(out)
    for part in d_tokens:
        part.on()
    result = run(collect, spots, [*ended[0], *ended[1]], tokens, b_branch[None, :])
    for part in d_tokens:
        part.on()
    for part in (qkv[0], qkv[1], out):
        part.on()
    core_spots = jnp.where(core == 0, scalars(0, 2, 1, 3), scalars(1, 3, 0, 2))
    summed = order.tie(*summed)
    for part in d_tokens:
        part.on()
    qkv[0].end()
    for part in (qkv[1], out):
        part.on()
    qkv[1].end()
    out.on()
    grad_qkv = run(collect, core_spots, [*qkv[0].end(), *qkv[1].end()])
    packed = order.tie(assemble(core, (out.end(),)))
    ended = [part.end() for part in d_tokens]
    d_tokens = run(collect, spots, [*ended[0], *ended[1]])
    grad_down, grad_up = summed
    grad_out = packed[: w_out.shape[0]]
    vectors = packed[w_out.shape[0] :].reshape(-1)
    a_gain, a_shift, m_gain, m_shift, qkv_bias, up_bias, branch = (
        vectors[end - size : end] for end, size in zip(ends, sizes, strict=True)
    )
    return (
        result,
        d_tokens,
        grad_qkv,
        qkv_bias,
        grad_out,
        grad_up,
        up_bias,
        grad_down,
        branch,
        a_gain,
        a_shift,
        m_gain,
        m_shift,
    )


def solution(mesh):
    placed = (
        P("dp", None),
        P("dp", None),
        P(),
        P(),
        P(),
        P(),
        P(None, "tensor"),
        P("tensor"),
        P("tensor", None),
        P(None, "tensor"),
        P("tensor"),
        P("tensor", None),
        P(),
        P("dp", None),
    )

    def body(*arrays):
        return shards(mesh.shape["dp"], mesh.shape["tensor"], *arrays)

    return jax.shard_map(
        body,
        mesh=mesh,
        in_specs=placed,
        out_specs=(
            P("dp", None),
            P("dp", None),
            P(None, "tensor"),
            P("tensor"),
            P("tensor", None),
            P(None, "tensor"),
            P("tensor"),
            P("tensor", None),
            P(),
            P(),
            P(),
            P(),
            P(),
        ),
        check_vma=False,
    )
```

```python
import functools
import math

import jax
import jax.numpy as jnp
from jax import lax
from jax.experimental import pallas as pl
from jax.experimental.pallas import tpu as pltpu
from jax.sharding import PartitionSpec as P

HD = 64
ROT = 16
MOST = 512

EPS = 1e-05
NEG = -1e30


def inner_rows(first_mat, second_mat):
    return lax.dot_general(
        first_mat, second_mat, (((0,), (0,)), ((), ())), preferred_element_type=jnp.float32
    )


def times_trans(first_mat, second_mat):
    return lax.dot_general(
        first_mat, second_mat, (((1,), (1,)), ((), ())), preferred_element_type=jnp.float32
    )


def product(first_mat, second_mat):
    return jnp.dot(first_mat, second_mat, preferred_element_type=jnp.float32)


def turn_angles(segment):
    spots = lax.broadcasted_iota(jnp.int32, segment.shape, 0)
    starts = jnp.zeros_like(segment)
    for number in range(3):
        count = jnp.sum((segment == number).astype(jnp.int32))
        starts = starts + jnp.where(segment > number, count, 0)
    offsets = (spots - starts).astype(jnp.float32)
    frequency = 10000.0 ** (-2.0 * jnp.arange(ROT // 2, dtype=jnp.float32) / ROT)
    angles = frequency[:, None] * offsets[None, :]
    number = jnp.broadcast_to(segment.astype(jnp.float32), (8, segment.shape[0]))
    return jnp.concatenate([jnp.cos(angles), jnp.sin(angles), number], axis=0)


def spread(angles, rows, take):
    return lax.dot_general(
        angles[0 : take.shape[0], rows],
        take,
        (((0,), (0,)), ((), ())),
        precision=lax.Precision.HIGHEST,
        preferred_element_type=jnp.float32,
    )


def turn_tables(angles, rows):
    tile, half = 2 * HD, ROT // 2
    source = lax.broadcasted_iota(jnp.int32, (ROT, tile), 0)
    column = lax.broadcasted_iota(jnp.int32, (ROT, tile), 1) % HD
    take_cos = ((source == column % half) & (column < ROT)).astype(jnp.float32)
    take_sin = source == column % half + half
    take_low = -(take_sin & (column < half)).astype(jnp.float32)
    take_high = (take_sin & (column >= half) & (column < ROT)).astype(jnp.float32)
    lane = lax.broadcasted_iota(jnp.int32, (rows.stop - rows.start, tile), 1)
    still = (lane % HD >= ROT).astype(jnp.float32)
    return (
        spread(angles, rows, take_cos) + still,
        spread(angles, rows, take_low),
        spread(angles, rows, take_high),
    )


def turn(wide, number, turned, low, high):
    tile, half = 2 * HD, ROT // 2
    lane = lax.broadcasted_iota(jnp.int32, wide.shape, 1)
    moved = (
        wide * turned
        + pltpu.roll(wide, tile - half, 1) * low
        + pltpu.roll(wide, half, 1) * high
    )
    if 2 * number % 3 == 2:
        return jnp.where(lane < HD, wide, moved)
    if (2 * number + 1) % 3 == 2:
        return jnp.where(lane >= HD, wide, moved)
    return moved


def key_range(start, block):
    return max(0, start - -(-MOST // block) * block), start + block


def fill_bias(bias, angles, start, block):
    first, until = key_range(start, block)
    count = until - first
    source = lax.broadcasted_iota(jnp.int32, (ROT + 8, 2 * HD), 0)
    own = spread(angles, slice(start, until), (source == ROT).astype(jnp.float32))[:, :1]
    other = angles[ROT : ROT + 1, first:until]
    query_spot = lax.broadcasted_iota(jnp.int32, (block, count), 0) + start
    key_spot = lax.broadcasted_iota(jnp.int32, (block, count), 1) + first
    bias[:, :count] = jnp.where((own == other) & (key_spot <= query_spot), 0.0, NEG)


def attend_kernel(heads, angles, projected, attended, sums, q_s, k_s, v_s, bias):
    seq_len, lanes = projected.shape
    block = min(256, seq_len)
    tile = 2 * HD
    for start in range(0, seq_len, block):
        rows = slice(start, start + block)
        turned, low, high = turn_tables(angles, rows)
        for number in range(lanes // tile):
            wide = turn(
                projected[rows, number * tile : (number + 1) * tile], number, turned, low, high
            )
            for side in range(2):
                head, kind = divmod(2 * number + side, 3)
                if head < heads:
                    part = wide[:, side * HD : (side + 1) * HD].astype(jnp.bfloat16)
                    (q_s, k_s, v_s)[kind][head, rows, :] = (
                        part * HD ** (-0.5) if kind == 0 else part
                    )
    for start in range(0, seq_len, block):
        first, until = key_range(start, block)
        count = until - first
        rows, keys = slice(start, until), slice(first, until)
        fill_bias(bias, angles, start, block)
        outs = []
        for h in range(heads):
            scores = times_trans(q_s[h, rows, :], k_s[h, keys, :]) + bias[:, :count]
            most = jnp.max(scores, axis=-1, keepdims=True)
            exponent = jnp.exp(scores - most)
            total = jnp.sum(exponent, axis=-1, keepdims=True)
            probs = (exponent * (1.0 / total)).astype(jnp.bfloat16)
            sums[rows, h : h + 1] = most + jnp.log(total)
            outs.append(product(probs, v_s[h, keys, :]))
        attended[rows, :] = jnp.concatenate(outs, axis=1).astype(jnp.bfloat16)


def attend_back_kernel(
    begin, heads, angles, q_s, k_s, v_s, sums, attended, d_attended, d_projected, dq_s, dk_s, dv_s, bias
):
    seq_len, lanes = d_projected.shape
    block = min(256, seq_len)
    tile = 2 * HD
    for start in range(0, seq_len, block):
        first, until = key_range(start, block)
        count = until - first
        rows, keys = slice(start, until), slice(first, until)
        fill_bias(bias, angles, start, block)
        for h in range(heads):
            g = begin + h
            q, k, v = q_s[g, rows, :], k_s[g, keys, :], v_s[g, keys, :]
            d_out = d_attended[rows, g * HD : (g + 1) * HD]
            out = attended[rows, g * HD : (g + 1) * HD]
            probs = jnp.exp(times_trans(q, k) + (bias[:, :count] - sums[rows, g : g + 1]))
            row_dot = jnp.sum(
                out.astype(jnp.float32) * d_out.astype(jnp.float32), axis=-1, keepdims=True
            )
            d_scores = (probs * (times_trans(d_out, v) - row_dot)).astype(jnp.bfloat16)
            dq_s[h, rows, :] = product(d_scores, k) * HD ** (-0.5)
            d_k = inner_rows(q, d_scores)
            d_v = inner_rows(d_out, probs.astype(jnp.bfloat16))
            old = count - block
            if old:
                dk_s[h, :, first:start] += d_k[:, :old]
                dv_s[h, :, first:start] += d_v[:, :old]
            dk_s[h, :, rows] = d_k[:, old:]
            dv_s[h, :, rows] = d_v[:, old:]
    for start in range(0, seq_len, block):
        rows = slice(start, start + block)
        turned, low, high = turn_tables(angles, rows)

        def section(at, rows=rows):
            head, kind = divmod(at, 3)
            if head >= heads:
                return jnp.zeros((block, HD), jnp.float32)
            return dq_s[head, rows, :] if kind == 0 else (dk_s, dv_s)[kind - 1][head, :, rows].T

        for number in range(lanes // tile):
            wide = jnp.concatenate([section(2 * number), section(2 * number + 1)], axis=1)
            d_projected[rows, number * tile : (number + 1) * tile] = turn(
                wide, number, turned, -low, -high
            ).astype(jnp.bfloat16)


VMEM = pl.BlockSpec(memory_space=pltpu.VMEM)


def bias_held(block):
    return pltpu.VMEM((block, -(-MOST // block) * block + block), jnp.float32)


def attend(angles, projected, heads):
    seq_len = projected.shape[0]
    shape = jax.ShapeDtypeStruct
    return pl.pallas_call(
        functools.partial(attend_kernel, heads),
        out_shape=(
            shape((seq_len, heads * HD), jnp.bfloat16),
            shape((seq_len, 2 * HD), jnp.float32),
        )
        + (shape((heads, seq_len, HD), jnp.bfloat16),) * 3,
        in_specs=[VMEM] * 2,
        out_specs=(VMEM,) * 5,
        scratch_shapes=[bias_held(min(256, seq_len))],
        compiler_params=pltpu.CompilerParams(vmem_limit_bytes=24 * 2**20),
    )(angles, projected)


def attend_back(angles, kept, d_attended, begin, heads, lanes):
    attended, sums, queries, keys, values = kept
    seq_len = attended.shape[0]
    cross = pltpu.VMEM((heads, HD, seq_len), jnp.float32)
    return pl.pallas_call(
        functools.partial(attend_back_kernel, begin, heads),
        out_shape=jax.ShapeDtypeStruct((seq_len, lanes), jnp.bfloat16),
        in_specs=[VMEM] * 7,
        out_specs=VMEM,
        scratch_shapes=[
            pltpu.VMEM((heads, seq_len, HD), jnp.float32),
            cross,
            cross,
            bias_held(min(256, seq_len)),
        ],
        compiler_params=pltpu.CompilerParams(vmem_limit_bytes=24 * 2**20),
    )(angles, queries, keys, values, sums, attended, d_attended)


def normed_rows(tokens):
    rows = tokens.astype(jnp.float32)
    centred = rows - jnp.mean(rows, axis=-1, keepdims=True)
    scale_inv = lax.rsqrt(jnp.mean(centred * centred, axis=-1, keepdims=True) + EPS)
    return centred * scale_inv, scale_inv


def tiled(width, tile, at=lambda i, *order: i):
    return pl.BlockSpec((tile, width), lambda i, *order: (at(i, *order), 0))


def whole(array):
    return pl.BlockSpec(array.shape, lambda i, *order: (0,) * array.ndim)


PARAMS = pltpu.CompilerParams(vmem_limit_bytes=40 * 2**20)
SMALL = pltpu.CompilerParams(vmem_limit_bytes=56 * 2**20)


def forward_kernel(
    tokens,
    cotangent,
    attn_gain,
    attn_shift,
    mlp_gain,
    mlp_shift,
    w_qkv,
    b_qkv,
    w_out,
    w_up,
    b_up,
    attn_low,
    mlp_low,
    projected,
    d_attended,
    hidden,
    slope,
):
    normed, _ = normed_rows(tokens[...])
    attn_in = (normed * attn_gain[...] + attn_shift[...]).astype(jnp.bfloat16)
    mlp_in = (normed * mlp_gain[...] + mlp_shift[...]).astype(jnp.bfloat16)
    attn_low[...] = attn_in
    mlp_low[...] = mlp_in
    count, lanes = w_qkv.shape[1], projected.shape[1]
    if lanes > count:
        projected[...] = jnp.zeros(projected.shape, jnp.float32)
    projected[:, :count] = product(attn_in, w_qkv[...]) + b_qkv[...]
    d_attended[...] = times_trans(cotangent[...], w_out[...]).astype(jnp.bfloat16)
    pre_act = product(mlp_in, w_up[...]) + b_up[...]
    below = 0.5 * (1.0 + lax.erf(pre_act * (0.5**0.5)))
    bell = jnp.exp(-0.5 * pre_act * pre_act) * ((2.0 * math.pi) ** -0.5)
    hidden[...] = (pre_act * below).astype(jnp.bfloat16)
    slope[...] = (below + pre_act * bell).astype(slope.dtype)


def forward(tokens, cotangent, vectors, w_qkv, b_qkv, w_out, w_up, b_up, lanes):
    rows, width = tokens.shape
    tile = rows // 4
    fixed = (*vectors, w_qkv, b_qkv, w_out, w_up, b_up)
    outs = (
        (width, jnp.bfloat16),
        (width, jnp.bfloat16),
        (lanes, jnp.float32),
        (w_out.shape[0], jnp.bfloat16),
        (w_up.shape[1], jnp.bfloat16),
        (w_up.shape[1], jnp.float32),
    )
    return pl.pallas_call(
        forward_kernel,
        grid=(4,),
        in_specs=[tiled(width, tile)] * 2 + [whole(array) for array in fixed],
        out_specs=tuple(tiled(wide, tile) for wide, _ in outs),
        out_shape=tuple(jax.ShapeDtypeStruct((rows, wide), kind) for wide, kind in outs),
        compiler_params=PARAMS,
    )(tokens, cotangent, *fixed)


def feed_back_kernel(
    tokens, cotangent, slope, w_down, w_up, mlp_gain, d_pre, scaled, sums, bias_sum
):
    @pl.when(pl.program_id(0) == 0)
    def _():
        sums[...] = jnp.zeros(sums.shape, jnp.float32)
        bias_sum[...] = jnp.zeros(bias_sum.shape, jnp.float32)

    d_low = (times_trans(cotangent[...], w_down[...]) * slope[...]).astype(jnp.bfloat16)
    d_pre[...] = d_low
    d_in = times_trans(d_low, w_up[...])
    scaled[...] = d_in * mlp_gain[...]
    normed, _ = normed_rows(tokens[...])
    sums[0:1, :] += jnp.sum(d_in * normed, axis=0, keepdims=True)
    sums[1:2, :] += jnp.sum(d_in, axis=0, keepdims=True)
    bias_sum[...] += jnp.sum(d_low.astype(jnp.float32), axis=0, keepdims=True)


def feed_back(tokens, cotangent, slope, w_down, w_up, mlp_gain):
    rows, width = tokens.shape
    inner = w_up.shape[1]
    tile = rows // 4
    fixed = (w_down, w_up, mlp_gain)
    shape = jax.ShapeDtypeStruct
    out_shape = (
        shape((rows, inner), jnp.bfloat16),
        shape((rows, width), jnp.float32),
        shape((2, width), jnp.float32),
        shape((1, inner), jnp.float32),
    )
    return pl.pallas_call(
        feed_back_kernel,
        grid=(4,),
        in_specs=[tiled(width, tile)] * 2 + [tiled(inner, tile)] + [whole(a) for a in fixed],
        out_specs=(tiled(inner, tile), tiled(width, tile)) + tuple(whole(a) for a in out_shape[2:]),
        out_shape=out_shape,
        compiler_params=PARAMS,
    )(tokens, cotangent, slope, *fixed)


def quarter_outs(rows, width):
    shape = jax.ShapeDtypeStruct((rows // 4, width), jnp.float32)
    return (shape,) * 4


def branches_kernel(tiles, attended, hidden, w_out, w_down, *outs):
    total = product(attended[...], w_out[...]) + product(hidden[...], w_down[...])
    for number, out in enumerate(outs):

        @pl.when(pl.program_id(0) == number)
        def _(out=out):
            out[...] = total


def picked(i, tiles):
    return tiles[i]


def branches(tiles, attended, hidden, w_out, w_down):
    rows, width = hidden.shape[0], w_down.shape[1]
    outs = quarter_outs(rows, width)
    return pl.pallas_call(
        branches_kernel,
        grid_spec=pltpu.PrefetchScalarGridSpec(
            num_scalar_prefetch=1,
            grid=(4,),
            in_specs=[
                tiled(attended.shape[1], rows // 4, picked),
                tiled(hidden.shape[1], rows // 4, picked),
                whole(w_out),
                whole(w_down),
            ],
            out_specs=tuple(whole(out) for out in outs),
        ),
        out_shape=outs,
        compiler_params=PARAMS,
    )(tiles, attended, hidden, w_out, w_down)


def input_back_kernel(count, heads_wide, tiles, *refs):
    d_heads, rest = refs[:count], refs[count:]
    tokens, cotangent, before, w_qkv, attn_gain = rest[:5]
    outs, (sums, bias_sum, branch_sum) = rest[5:9], rest[9:]

    @pl.when(pl.program_id(0) == 0)
    def _():
        for held in (sums, bias_sum, branch_sum):
            held[...] = jnp.zeros(held.shape, jnp.float32)

    d_in = None
    for number, part in enumerate(d_heads):
        columns = slice(number * heads_wide, (number + 1) * heads_wide)
        low = part[:, :heads_wide]
        term = times_trans(low, w_qkv[:, columns])
        d_in = term if d_in is None else d_in + term
        bias_sum[:, columns] += jnp.sum(low.astype(jnp.float32), axis=0, keepdims=True)
    normed, _ = normed_rows(tokens[...])
    sums[0:1, :] += jnp.sum(d_in * normed, axis=0, keepdims=True)
    sums[1:2, :] += jnp.sum(d_in, axis=0, keepdims=True)
    branch_sum[...] += jnp.sum(cotangent[...].astype(jnp.float32), axis=0, keepdims=True)
    total = d_in * attn_gain[...] + before[...]
    for number, out in enumerate(outs):

        @pl.when(pl.program_id(0) == number)
        def _(out=out):
            out[...] = total


def input_back(tiles, d_heads, heads_wide, tokens, cotangent, before, w_qkv, attn_gain):
    rows, width = tokens.shape
    tile = rows // 4
    shape = jax.ShapeDtypeStruct
    outs = quarter_outs(rows, width) + (
        shape((2, width), jnp.float32),
        shape((1, w_qkv.shape[1]), jnp.float32),
        shape((1, width), jnp.float32),
    )
    return pl.pallas_call(
        functools.partial(input_back_kernel, len(d_heads), heads_wide),
        grid_spec=pltpu.PrefetchScalarGridSpec(
            num_scalar_prefetch=1,
            grid=(4,),
            in_specs=[tiled(part.shape[1], tile, picked) for part in d_heads]
            + [tiled(width, tile, picked)] * 3
            + [whole(w_qkv), whole(attn_gain)],
            out_specs=tuple(whole(out) for out in outs),
        ),
        out_shape=outs,
        compiler_params=PARAMS,
    )(tiles, *d_heads, tokens, cotangent, before, w_qkv, attn_gain)


def gradient_kernel(wide, first_mat, *refs):
    for number, part in enumerate(refs[:-1]):
        columns = slice(number * wide, (number + 1) * wide)
        refs[-1][:, columns] = inner_rows(first_mat[...], part[:, :wide])


def gradient(first_mat, parts, wide):
    count, rows = first_mat.shape
    steps = 4 if rows % 512 == 0 else 2
    tile = rows // steps
    columns = wide * len(parts)
    if tile % 128:
        return inner_rows(
            first_mat, jnp.concatenate([part[:, :wide] for part in parts], axis=1)
        )
    return pl.pallas_call(
        functools.partial(gradient_kernel, wide),
        grid=(steps,),
        in_specs=[pl.BlockSpec((count, tile), lambda i: (0, i))] + [whole(p) for p in parts],
        out_specs=tiled(columns, tile),
        out_shape=jax.ShapeDtypeStruct((rows, columns), jnp.float32),
        compiler_params=PARAMS,
    )(first_mat, *parts)


def float_shape(rows, width):
    return jax.ShapeDtypeStruct((rows, width), jnp.float32)


def steps_for(rows):
    return 2 if rows % 16 == 0 else 1


def scalars(*values):
    return jnp.stack([jnp.asarray(value, jnp.int32) for value in values])


def add_kernel(first, second, out):
    out[...] = first[...] + second[...]


def add(first, second):
    rows, width = first.shape
    steps = steps_for(rows)
    spec = tiled(width, rows // steps)
    return pl.pallas_call(
        add_kernel,
        grid=(steps,),
        in_specs=[spec] * 2,
        out_specs=spec,
        out_shape=float_shape(rows, width),
        compiler_params=SMALL,
    )(first, second)


def add_split_kernel(mine, first, second, away, keep):
    total = first[...] + second[...]

    @pl.when(pl.program_id(0) == 0)
    def _():
        away[...] = total

    @pl.when(pl.program_id(0) == 1)
    def _():
        keep[...] = total


def add_split(mine, first, second):
    rows, width = first.shape
    outs = (float_shape(rows // 2, width),) * 2
    spec = tiled(width, rows // 2, lambda i, mine: (i + 1 + mine[0]) % 2)
    return pl.pallas_call(
        add_split_kernel,
        grid_spec=pltpu.PrefetchScalarGridSpec(
            num_scalar_prefetch=1,
            grid=(2,),
            in_specs=[spec] * 2,
            out_specs=tuple(whole(out) for out in outs),
        ),
        out_shape=outs,
        compiler_params=SMALL,
    )(scalars(mine), first, second)


def norm_back_kernel(at, first, second, tokens, cotangent, out):
    rows = first[...] + second[...]
    normed, scale_inv = normed_rows(tokens[...])
    out[...] = cotangent[...].astype(jnp.float32) + scale_inv * (
        rows
        - jnp.mean(rows, axis=-1, keepdims=True)
        - normed * jnp.mean(rows * normed, axis=-1, keepdims=True)
    )


def norm_back(first, second, at, tokens, cotangent):
    rows, width = first.shape
    spec = pl.BlockSpec((rows, width), lambda i, at: (0, 0))
    moved = pl.BlockSpec((rows, width), lambda i, at: (at[0], 0))
    return pl.pallas_call(
        norm_back_kernel,
        grid_spec=pltpu.PrefetchScalarGridSpec(
            num_scalar_prefetch=1,
            grid=(1,),
            in_specs=[spec, spec, moved, moved],
            out_specs=spec,
        ),
        out_shape=float_shape(rows, width),
        compiler_params=SMALL,
    )(scalars(at // rows), first, second, tokens, cotangent)


def join_kernel(mine, own, other, out):
    @pl.when(pl.program_id(0) == mine[0])
    def _():
        out[...] = own[...]

    @pl.when(pl.program_id(0) != mine[0])
    def _():
        out[...] = other[...]


def join(mine, own, other):
    rows, width = own.shape
    return pl.pallas_call(
        join_kernel,
        grid_spec=pltpu.PrefetchScalarGridSpec(
            num_scalar_prefetch=1,
            grid=(2,),
            in_specs=[pl.BlockSpec((rows, width), lambda i, mine: (0, 0))] * 2,
            out_specs=tiled(width, rows, lambda i, mine: i),
        ),
        out_shape=float_shape(2 * rows, width),
        compiler_params=SMALL,
    )(scalars(mine), own, other)


def collect_kernel(order, *refs):
    parts, out = refs[:4], refs[-1]
    extra = refs[4:-1]
    for number, part in enumerate(parts):

        @pl.when(order[pl.program_id(0)] == number)
        def _(part=part):
            if extra:
                tokens, bias = extra
                total = tokens[...].astype(jnp.float32) + part[...] + bias[...]
                out[...] = total.astype(out.dtype)
            else:
                out[...] = part[...]


def collect(order, parts, *extra):
    rows, width = parts[0].shape
    specs = [pl.BlockSpec((rows, width), lambda i, order: (0, 0))] * 4
    if extra:
        specs = specs + [tiled(width, rows, lambda i, order: i), whole(extra[1])]
    return pl.pallas_call(
        collect_kernel,
        grid_spec=pltpu.PrefetchScalarGridSpec(
            num_scalar_prefetch=1,
            grid=(4,),
            in_specs=specs,
            out_specs=tiled(width, rows, lambda i, order: i),
        ),
        out_shape=jax.ShapeDtypeStruct(
            (4 * rows, width), extra[0].dtype if extra else jnp.float32
        ),
        compiler_params=SMALL,
    )(order, *parts, *extra)


class Order:
    def __init__(self, token):
        self.token = token

    def tie(self, *arrays):
        tied = lax.optimization_barrier((self.token, *arrays))
        self.token = tied[0]
        return tied[1] if len(arrays) == 1 else tied[1:]

    def run(self, step, *arrays):
        tied = lax.optimization_barrier((self.token, *arrays))
        out = step(*tied[1:])
        out = tuple(out) if isinstance(out, list) else out
        if isinstance(out, tuple):
            return self.tie(*out)
        return self.tie(out)


class Chain:
    def __init__(self, order, steps):
        self.order, self.steps, self.out, self.held = order, steps, None, None
        self._go(None)

    def _go(self, arrived):
        try:
            array, axis, pairs = self.steps.send(arrived)
        except StopIteration as stop:
            self.held, self.out = None, stop.value
            return
        array = self.order.tie(array)
        self.held = lax.ppermute(array, axis, pairs)

    def on(self):
        if self.held is not None:
            self._go(self.order.tie(self.held))
        return self

    def end(self):
        while self.held is not None:
            self.on()
        return self.out


def swap_pairs(size, bit):
    return [(i, i ^ bit) for i in range(size)]


def tensor_steps(away, keep, size, order, finish):
    place = lax.axis_index("tensor")
    first = 0
    rows = away.shape[0]
    for number, bit in enumerate(order):
        got = yield away, "tensor", swap_pairs(size, bit)
        first = first + (place // bit) % 2 * rows
        if number + 1 < len(order):
            away, keep = add_split((place // order[number + 1]) % 2, keep, got)
            rows = rows // 2
    array = finish(keep, got, first)
    for number, bit in enumerate(reversed(order)):
        got = yield array, "tensor", swap_pairs(size, bit)
        if number + 1 < len(order):
            array = join((place // bit) % 2, array, got)
    return array, got


def line_steps(array, size):
    chips = size // 2
    place = lax.axis_index("dp") // 2

    def pairs(moves):
        return [(2 * a + c, 2 * b + c) for a, b in moves for c in range(2)]

    if chips > 1:
        steps = range(chips // 2 - 1)
        for s in steps:
            got = yield array, "dp", pairs([(s, s + 1), (chips - 1 - s, chips - 2 - s)])
            array = array + got
        middle = chips // 2
        got = yield array, "dp", pairs([(middle - 1, middle), (middle, middle - 1)])
        array = array + got
        for s in reversed(steps):
            got = yield array, "dp", pairs([(s + 1, s), (chips - 2 - s, chips - 1 - s)])
            array = jnp.where((place == s) | (place == chips - 1 - s), got, array)
    return array


def add_end(keep, got, first):
    return add(keep, got)


def small_steps(stats, rest, tensor_size, dp_size):
    for bit in (1 << k for k in range(tensor_size.bit_length() - 1)):
        got = yield stats, "tensor", swap_pairs(tensor_size, bit)
        stats = stats + got
    vectors = jnp.concatenate([stats.reshape(-1), *rest])
    got = yield vectors, "dp", swap_pairs(dp_size, 1)
    return (yield from line_steps(vectors + got, dp_size))


def shards(
    dp_size,
    tensor_size,
    tokens,
    segment,
    attn_gain,
    attn_shift,
    mlp_gain,
    mlp_shift,
    w_qkv,
    b_qkv,
    w_out,
    w_up,
    b_up,
    w_down,
    b_branch,
    cotangent,
):
    rows_here, width = tokens.shape
    heads = w_qkv.shape[1] // (3 * HD)
    group = 2 if heads % 2 == 0 else heads
    wide = 3 * HD * group
    lanes = -(-wide // 128) * 128
    groups = heads // group
    bits = [1 << k for k in range(tensor_size.bit_length() - 1)]
    orders = (bits, bits[::-1])
    split = rows_here // 2
    core = lax.axis_index("dp") % 2
    place = lax.axis_index("tensor")
    order = Order(core)
    run = order.run
    mine = [(place // its[0]) % 2 for its in orders]
    tiles = jnp.stack([1 - mine[0], 3 - mine[1], mine[0], 2 + mine[1]]).astype(jnp.int32)

    def chain(steps):
        return Chain(order, steps)

    vectors = [v[None, :] for v in (attn_gain, attn_shift, mlp_gain, mlp_shift)]
    angles = run(turn_angles, segment[0])
    attn_low, mlp_low, projected, d_attended, hidden, slope = run(
        lambda *a: forward(a[0], a[1], vectors, *a[2:], lanes=lanes * groups),
        tokens,
        cotangent,
        w_qkv,
        b_qkv[None, :],
        w_out,
        w_up,
        b_up[None, :],
    )
    kept = run(functools.partial(attend, heads=heads), angles, projected)
    attended = kept[0]
    partial = run(branches, tiles, attended, hidden, w_out, w_down)
    result = [
        chain(tensor_steps(partial[p], partial[2 + p], tensor_size, orders[p], add_end))
        for p in range(2)
    ]
    back = []
    for begin in range(0, heads, group):
        def step(angles, d_attended, *kept, begin=begin):
            return attend_back(angles, kept, d_attended, begin, group, lanes)

        back.append(run(step, angles, d_attended, *kept))
    d_pre, scaled_mlp, sums_mlp, up_bias = run(
        feed_back, tokens, cotangent, slope, w_down, w_up, mlp_gain[None, :]
    )
    grad_down = run(lambda a, b: gradient(a, [b], width), hidden, cotangent)
    grad_up = run(lambda a, b: gradient(a, [b], w_up.shape[1]), mlp_low, d_pre)
    grad_qkv = run(lambda a, *b: gradient(a, b, wide), attn_low, *back)
    grad_out = run(inner_rows, attended, cotangent)
    summed = lax.psum((grad_down, grad_up, grad_qkv, grad_out), "dp")
    for part in result:
        part.on()
    *scaled, sums_attn, qkv_bias, branch_sum = run(
        lambda tiles, *a: input_back(tiles, a[:-5], wide, *a[-5:]),
        tiles,
        *back,
        tokens,
        cotangent,
        scaled_mlp,
        w_qkv,
        attn_gain[None, :],
    )

    def back_end(part):
        def finish(keep, got, first):
            return norm_back(keep, got, first + part * split, tokens, cotangent)

        return finish

    small = chain(
        small_steps(
            jnp.concatenate([sums_attn, sums_mlp], axis=0),
            [qkv_bias[0], up_bias[0], branch_sum[0]],
            tensor_size,
            dp_size,
        )
    )
    for part in result:
        part.on()
    small.on()
    d_tokens = [
        chain(tensor_steps(scaled[p], scaled[2 + p], tensor_size, orders[p], back_end(p)))
        for p in range(2)
    ]
    for part in result:
        part.on()
    small.on()
    spots = scalars(mine[0], 1 - mine[0], 2 + mine[1], 3 - mine[1])
    ended = [part.end() for part in result]
    for part in d_tokens:
        part.on()
    small.on()
    result = run(collect, spots, [*ended[0], *ended[1]], tokens, b_branch[None, :])
    for part in d_tokens:
        part.on()
    small.on()
    for part in d_tokens:
        part.on()
    vectors = small.end()
    ended = [part.end() for part in d_tokens]
    d_tokens = run(collect, spots, [*ended[0], *ended[1]])
    grad_down, grad_up, grad_qkv, grad_out = order.tie(*summed)
    sizes = (width,) * 4 + (w_qkv.shape[1], w_up.shape[1], width)
    ends = [sum(sizes[: k + 1]) for k in range(len(sizes))]
    a_gain, a_shift, m_gain, m_shift, qkv_bias, up_bias, branch = (
        vectors[end - size : end] for end, size in zip(ends, sizes, strict=True)
    )
    return (
        result,
        d_tokens,
        grad_qkv,
        qkv_bias,
        grad_out,
        grad_up,
        up_bias,
        grad_down,
        branch,
        a_gain,
        a_shift,
        m_gain,
        m_shift,
    )


def solution(mesh):
    placed = (
        P("dp", None),
        P("dp", None),
        P(),
        P(),
        P(),
        P(),
        P(None, "tensor"),
        P("tensor"),
        P("tensor", None),
        P(None, "tensor"),
        P("tensor"),
        P("tensor", None),
        P(),
        P("dp", None),
    )

    def body(*arrays):
        return shards(mesh.shape["dp"], mesh.shape["tensor"], *arrays)

    return jax.shard_map(
        body,
        mesh=mesh,
        in_specs=placed,
        out_specs=(
            P("dp", None),
            P("dp", None),
            P(None, "tensor"),
            P("tensor"),
            P("tensor", None),
            P(None, "tensor"),
            P("tensor"),
            P("tensor", None),
            P(),
            P(),
            P(),
            P(),
            P(),
        ),
        check_vma=False,
    )
```

```python
import functools
import math

import jax
import jax.numpy as jnp
from jax import lax
from jax.experimental import pallas as pl
from jax.experimental.pallas import tpu as pltpu
from jax.sharding import PartitionSpec as P

HD = 64
ROT = 16
MOST = 512

EPS = 1e-05
NEG = -1e30


def inner_rows(first_mat, second_mat):
    return lax.dot_general(
        first_mat, second_mat, (((0,), (0,)), ((), ())), preferred_element_type=jnp.float32
    )


def times_trans(first_mat, second_mat):
    return lax.dot_general(
        first_mat, second_mat, (((1,), (1,)), ((), ())), preferred_element_type=jnp.float32
    )


def product(first_mat, second_mat):
    return jnp.dot(first_mat, second_mat, preferred_element_type=jnp.float32)


def turn_angles(segment):
    spots = lax.broadcasted_iota(jnp.int32, segment.shape, 0)
    starts = jnp.zeros_like(segment)
    for number in range(3):
        count = jnp.sum((segment == number).astype(jnp.int32))
        starts = starts + jnp.where(segment > number, count, 0)
    offsets = (spots - starts).astype(jnp.float32)
    frequency = 10000.0 ** (-2.0 * jnp.arange(ROT // 2, dtype=jnp.float32) / ROT)
    angles = frequency[:, None] * offsets[None, :]
    number = jnp.broadcast_to(segment.astype(jnp.float32), (8, segment.shape[0]))
    return jnp.concatenate([jnp.cos(angles), jnp.sin(angles), number], axis=0)


def spread(angles, rows, take):
    return lax.dot_general(
        angles[0 : take.shape[0], rows],
        take,
        (((0,), (0,)), ((), ())),
        precision=lax.Precision.HIGHEST,
        preferred_element_type=jnp.float32,
    )


def turn_tables(angles, rows):
    tile, half = 2 * HD, ROT // 2
    source = lax.broadcasted_iota(jnp.int32, (ROT, tile), 0)
    column = lax.broadcasted_iota(jnp.int32, (ROT, tile), 1) % HD
    take_cos = ((source == column % half) & (column < ROT)).astype(jnp.float32)
    take_sin = source == column % half + half
    take_low = -(take_sin & (column < half)).astype(jnp.float32)
    take_high = (take_sin & (column >= half) & (column < ROT)).astype(jnp.float32)
    lane = lax.broadcasted_iota(jnp.int32, (rows.stop - rows.start, tile), 1)
    still = (lane % HD >= ROT).astype(jnp.float32)
    return (
        spread(angles, rows, take_cos) + still,
        spread(angles, rows, take_low),
        spread(angles, rows, take_high),
    )


def turn(wide, number, turned, low, high):
    tile, half = 2 * HD, ROT // 2
    lane = lax.broadcasted_iota(jnp.int32, wide.shape, 1)
    moved = (
        wide * turned
        + pltpu.roll(wide, tile - half, 1) * low
        + pltpu.roll(wide, half, 1) * high
    )
    if 2 * number % 3 == 2:
        return jnp.where(lane < HD, wide, moved)
    if (2 * number + 1) % 3 == 2:
        return jnp.where(lane >= HD, wide, moved)
    return moved


def key_range(start, block):
    return max(0, start - -(-MOST // block) * block), start + block


def fill_bias(bias, angles, start, block):
    first, until = key_range(start, block)
    count = until - first
    source = lax.broadcasted_iota(jnp.int32, (ROT + 8, 2 * HD), 0)
    own = spread(angles, slice(start, until), (source == ROT).astype(jnp.float32))[:, :1]
    other = angles[ROT : ROT + 1, first:until]
    query_spot = lax.broadcasted_iota(jnp.int32, (block, count), 0) + start
    key_spot = lax.broadcasted_iota(jnp.int32, (block, count), 1) + first
    bias[:, :count] = jnp.where((own == other) & (key_spot <= query_spot), 0.0, NEG)


def attend_kernel(heads, angles, projected, attended, sums, q_s, k_s, v_s, bias):
    seq_len, lanes = projected.shape
    block = min(256, seq_len)
    tile = 2 * HD
    for start in range(0, seq_len, block):
        rows = slice(start, start + block)
        turned, low, high = turn_tables(angles, rows)
        for number in range(lanes // tile):
            wide = turn(
                projected[rows, number * tile : (number + 1) * tile], number, turned, low, high
            )
            for side in range(2):
                head, kind = divmod(2 * number + side, 3)
                if head < heads:
                    part = wide[:, side * HD : (side + 1) * HD].astype(jnp.bfloat16)
                    (q_s, k_s, v_s)[kind][head, rows, :] = (
                        part * HD ** (-0.5) if kind == 0 else part
                    )
    for start in range(0, seq_len, block):
        first, until = key_range(start, block)
        count = until - first
        rows, keys = slice(start, until), slice(first, until)
        fill_bias(bias, angles, start, block)
        outs = []
        for h in range(heads):
            scores = times_trans(q_s[h, rows, :], k_s[h, keys, :]) + bias[:, :count]
            most = jnp.max(scores, axis=-1, keepdims=True)
            exponent = jnp.exp(scores - most)
            total = jnp.sum(exponent, axis=-1, keepdims=True)
            probs = (exponent * (1.0 / total)).astype(jnp.bfloat16)
            sums[rows, h : h + 1] = most + jnp.log(total)
            outs.append(product(probs, v_s[h, keys, :]))
        attended[rows, :] = jnp.concatenate(outs, axis=1).astype(jnp.bfloat16)


def attend_back_kernel(
    begin, heads, angles, q_s, k_s, v_s, sums, attended, d_attended, d_projected, dq_s, dk_s, dv_s, bias
):
    seq_len, lanes = d_projected.shape
    block = min(256, seq_len)
    tile = 2 * HD
    for start in range(0, seq_len, block):
        first, until = key_range(start, block)
        count = until - first
        rows, keys = slice(start, until), slice(first, until)
        fill_bias(bias, angles, start, block)
        for h in range(heads):
            g = begin + h
            q, k, v = q_s[g, rows, :], k_s[g, keys, :], v_s[g, keys, :]
            d_out = d_attended[rows, g * HD : (g + 1) * HD]
            out = attended[rows, g * HD : (g + 1) * HD]
            probs = jnp.exp(times_trans(q, k) + (bias[:, :count] - sums[rows, g : g + 1]))
            row_dot = jnp.sum(
                out.astype(jnp.float32) * d_out.astype(jnp.float32), axis=-1, keepdims=True
            )
            d_scores = (probs * (times_trans(d_out, v) - row_dot)).astype(jnp.bfloat16)
            dq_s[h, rows, :] = product(d_scores, k) * HD ** (-0.5)
            d_k = inner_rows(q, d_scores)
            d_v = inner_rows(d_out, probs.astype(jnp.bfloat16))
            old = count - block
            if old:
                dk_s[h, :, first:start] += d_k[:, :old]
                dv_s[h, :, first:start] += d_v[:, :old]
            dk_s[h, :, rows] = d_k[:, old:]
            dv_s[h, :, rows] = d_v[:, old:]
    for start in range(0, seq_len, block):
        rows = slice(start, start + block)
        turned, low, high = turn_tables(angles, rows)

        def section(at, rows=rows):
            head, kind = divmod(at, 3)
            if head >= heads:
                return jnp.zeros((block, HD), jnp.float32)
            return dq_s[head, rows, :] if kind == 0 else (dk_s, dv_s)[kind - 1][head, :, rows].T

        for number in range(lanes // tile):
            wide = jnp.concatenate([section(2 * number), section(2 * number + 1)], axis=1)
            d_projected[rows, number * tile : (number + 1) * tile] = turn(
                wide, number, turned, -low, -high
            ).astype(jnp.bfloat16)


VMEM = pl.BlockSpec(memory_space=pltpu.VMEM)


def bias_held(block):
    return pltpu.VMEM((block, -(-MOST // block) * block + block), jnp.float32)


def attend(angles, projected, heads):
    seq_len = projected.shape[0]
    shape = jax.ShapeDtypeStruct
    return pl.pallas_call(
        functools.partial(attend_kernel, heads),
        out_shape=(
            shape((seq_len, heads * HD), jnp.bfloat16),
            shape((seq_len, 2 * HD), jnp.float32),
        )
        + (shape((heads, seq_len, HD), jnp.bfloat16),) * 3,
        in_specs=[VMEM] * 2,
        out_specs=(VMEM,) * 5,
        scratch_shapes=[bias_held(min(256, seq_len))],
        compiler_params=pltpu.CompilerParams(vmem_limit_bytes=24 * 2**20),
    )(angles, projected)


def attend_back(angles, kept, d_attended, begin, heads, lanes):
    attended, sums, queries, keys, values = kept
    seq_len = attended.shape[0]
    cross = pltpu.VMEM((heads, HD, seq_len), jnp.float32)
    return pl.pallas_call(
        functools.partial(attend_back_kernel, begin, heads),
        out_shape=jax.ShapeDtypeStruct((seq_len, lanes), jnp.bfloat16),
        in_specs=[VMEM] * 7,
        out_specs=VMEM,
        scratch_shapes=[
            pltpu.VMEM((heads, seq_len, HD), jnp.float32),
            cross,
            cross,
            bias_held(min(256, seq_len)),
        ],
        compiler_params=pltpu.CompilerParams(vmem_limit_bytes=24 * 2**20),
    )(angles, queries, keys, values, sums, attended, d_attended)


def normed_rows(tokens):
    rows = tokens.astype(jnp.float32)
    centred = rows - jnp.mean(rows, axis=-1, keepdims=True)
    scale_inv = lax.rsqrt(jnp.mean(centred * centred, axis=-1, keepdims=True) + EPS)
    return centred * scale_inv, scale_inv


def tiled(width, tile, at=lambda i, *order: i):
    return pl.BlockSpec((tile, width), lambda i, *order: (at(i, *order), 0))


def whole(array):
    return pl.BlockSpec(array.shape, lambda i, *order: (0,) * array.ndim)


PARAMS = pltpu.CompilerParams(vmem_limit_bytes=40 * 2**20)
SMALL = pltpu.CompilerParams(vmem_limit_bytes=48 * 2**20)


def forward_kernel(
    tokens,
    cotangent,
    attn_gain,
    attn_shift,
    mlp_gain,
    mlp_shift,
    w_qkv,
    b_qkv,
    w_out,
    w_up,
    b_up,
    attn_low,
    mlp_low,
    projected,
    d_attended,
    hidden,
    slope,
):
    normed, _ = normed_rows(tokens[...])
    attn_in = (normed * attn_gain[...] + attn_shift[...]).astype(jnp.bfloat16)
    mlp_in = (normed * mlp_gain[...] + mlp_shift[...]).astype(jnp.bfloat16)
    attn_low[...] = attn_in
    mlp_low[...] = mlp_in
    count, lanes = w_qkv.shape[1], projected.shape[1]
    if lanes > count:
        projected[...] = jnp.zeros(projected.shape, jnp.float32)
    projected[:, :count] = product(attn_in, w_qkv[...]) + b_qkv[...]
    d_attended[...] = times_trans(cotangent[...], w_out[...]).astype(jnp.bfloat16)
    pre_act = product(mlp_in, w_up[...]) + b_up[...]
    below = 0.5 * (1.0 + lax.erf(pre_act * (0.5**0.5)))
    bell = jnp.exp(-0.5 * pre_act * pre_act) * ((2.0 * math.pi) ** -0.5)
    hidden[...] = (pre_act * below).astype(jnp.bfloat16)
    slope[...] = (below + pre_act * bell).astype(slope.dtype)


def forward(tokens, cotangent, vectors, w_qkv, b_qkv, w_out, w_up, b_up, lanes):
    rows, width = tokens.shape
    tile = rows // 4
    fixed = (*vectors, w_qkv, b_qkv, w_out, w_up, b_up)
    outs = (
        (width, jnp.bfloat16),
        (width, jnp.bfloat16),
        (lanes, jnp.float32),
        (w_out.shape[0], jnp.bfloat16),
        (w_up.shape[1], jnp.bfloat16),
        (w_up.shape[1], jnp.float32),
    )
    return pl.pallas_call(
        forward_kernel,
        grid=(4,),
        in_specs=[tiled(width, tile)] * 2 + [whole(array) for array in fixed],
        out_specs=tuple(tiled(wide, tile) for wide, _ in outs),
        out_shape=tuple(jax.ShapeDtypeStruct((rows, wide), kind) for wide, kind in outs),
        compiler_params=PARAMS,
    )(tokens, cotangent, *fixed)


def feed_back_kernel(
    tokens, cotangent, slope, w_down, w_up, mlp_gain, d_pre, scaled, sums, bias_sum
):
    @pl.when(pl.program_id(0) == 0)
    def _():
        sums[...] = jnp.zeros(sums.shape, jnp.float32)
        bias_sum[...] = jnp.zeros(bias_sum.shape, jnp.float32)

    d_low = (times_trans(cotangent[...], w_down[...]) * slope[...]).astype(jnp.bfloat16)
    d_pre[...] = d_low
    d_in = times_trans(d_low, w_up[...])
    scaled[...] = d_in * mlp_gain[...]
    normed, _ = normed_rows(tokens[...])
    sums[0:1, :] += jnp.sum(d_in * normed, axis=0, keepdims=True)
    sums[1:2, :] += jnp.sum(d_in, axis=0, keepdims=True)
    bias_sum[...] += jnp.sum(d_low.astype(jnp.float32), axis=0, keepdims=True)


def feed_back(tokens, cotangent, slope, w_down, w_up, mlp_gain):
    rows, width = tokens.shape
    inner = w_up.shape[1]
    tile = rows // 4
    fixed = (w_down, w_up, mlp_gain)
    shape = jax.ShapeDtypeStruct
    out_shape = (
        shape((rows, inner), jnp.bfloat16),
        shape((rows, width), jnp.float32),
        shape((2, width), jnp.float32),
        shape((1, inner), jnp.float32),
    )
    return pl.pallas_call(
        feed_back_kernel,
        grid=(4,),
        in_specs=[tiled(width, tile)] * 2 + [tiled(inner, tile)] + [whole(a) for a in fixed],
        out_specs=(tiled(inner, tile), tiled(width, tile)) + tuple(whole(a) for a in out_shape[2:]),
        out_shape=out_shape,
        compiler_params=PARAMS,
    )(tokens, cotangent, slope, *fixed)


def quarter_outs(rows, width):
    shape = jax.ShapeDtypeStruct((rows // 4, width), jnp.float32)
    return (shape,) * 4


def branches_kernel(tiles, attended, hidden, w_out, w_down, *outs):
    total = product(attended[...], w_out[...]) + product(hidden[...], w_down[...])
    for number, out in enumerate(outs):

        @pl.when(pl.program_id(0) == number)
        def _(out=out):
            out[...] = total


def picked(i, tiles):
    return tiles[i]


def branches(tiles, attended, hidden, w_out, w_down):
    rows, width = hidden.shape[0], w_down.shape[1]
    outs = quarter_outs(rows, width)
    return pl.pallas_call(
        branches_kernel,
        grid_spec=pltpu.PrefetchScalarGridSpec(
            num_scalar_prefetch=1,
            grid=(4,),
            in_specs=[
                tiled(attended.shape[1], rows // 4, picked),
                tiled(hidden.shape[1], rows // 4, picked),
                whole(w_out),
                whole(w_down),
            ],
            out_specs=tuple(whole(out) for out in outs),
        ),
        out_shape=outs,
        compiler_params=PARAMS,
    )(tiles, attended, hidden, w_out, w_down)


def input_back_kernel(count, heads_wide, tiles, *refs):
    d_heads, rest = refs[:count], refs[count:]
    tokens, cotangent, before, w_qkv, attn_gain = rest[:5]
    outs, (sums, bias_sum, branch_sum) = rest[5:9], rest[9:]

    @pl.when(pl.program_id(0) == 0)
    def _():
        for held in (sums, bias_sum, branch_sum):
            held[...] = jnp.zeros(held.shape, jnp.float32)

    d_in = None
    for number, part in enumerate(d_heads):
        columns = slice(number * heads_wide, (number + 1) * heads_wide)
        low = part[:, :heads_wide]
        term = times_trans(low, w_qkv[:, columns])
        d_in = term if d_in is None else d_in + term
        bias_sum[:, columns] += jnp.sum(low.astype(jnp.float32), axis=0, keepdims=True)
    normed, _ = normed_rows(tokens[...])
    sums[0:1, :] += jnp.sum(d_in * normed, axis=0, keepdims=True)
    sums[1:2, :] += jnp.sum(d_in, axis=0, keepdims=True)
    branch_sum[...] += jnp.sum(cotangent[...].astype(jnp.float32), axis=0, keepdims=True)
    total = d_in * attn_gain[...] + before[...]
    for number, out in enumerate(outs):

        @pl.when(pl.program_id(0) == number)
        def _(out=out):
            out[...] = total


def input_back(tiles, d_heads, heads_wide, tokens, cotangent, before, w_qkv, attn_gain):
    rows, width = tokens.shape
    tile = rows // 4
    shape = jax.ShapeDtypeStruct
    outs = quarter_outs(rows, width) + (
        shape((2, width), jnp.float32),
        shape((1, w_qkv.shape[1]), jnp.float32),
        shape((1, width), jnp.float32),
    )
    return pl.pallas_call(
        functools.partial(input_back_kernel, len(d_heads), heads_wide),
        grid_spec=pltpu.PrefetchScalarGridSpec(
            num_scalar_prefetch=1,
            grid=(4,),
            in_specs=[tiled(part.shape[1], tile, picked) for part in d_heads]
            + [tiled(width, tile, picked)] * 3
            + [whole(w_qkv), whole(attn_gain)],
            out_specs=tuple(whole(out) for out in outs),
        ),
        out_shape=outs,
        compiler_params=PARAMS,
    )(tiles, *d_heads, tokens, cotangent, before, w_qkv, attn_gain)


def gradient_kernel(wide, tiles, first_mat, *refs):
    parts, outs = refs[:-2], refs[-2:]
    for number, part in enumerate(parts):
        block = inner_rows(first_mat[...], part[:, :wide])
        columns = slice(number * wide, (number + 1) * wide)
        for side, out in enumerate(outs):

            @pl.when(pl.program_id(0) // (pl.num_programs(0) // 2) == side)
            def _(out=out, block=block, columns=columns):
                out[:, columns] = block


def gradient(swapped, first_mat, parts, wide, begin=0, rows=None):
    count = first_mat.shape[0]
    rows = rows or first_mat.shape[1]
    steps = 4 if rows >= 1024 else 2
    tile = rows // steps
    half = steps // 2
    columns = wide * len(parts)
    if tile % 128:
        full = inner_rows(
            first_mat[:, begin : begin + rows],
            jnp.concatenate([part[:, :wide] for part in parts], axis=1),
        )
        return tuple(
            lax.dynamic_slice_in_dim(full, side * (rows // 2), rows // 2, 0)
            for side in (swapped, 1 - swapped)
        )
    tiles = (jnp.arange(steps, dtype=jnp.int32) + swapped * half) % steps + begin // tile
    out = jax.ShapeDtypeStruct((rows // 2, columns), jnp.float32)
    return pl.pallas_call(
        functools.partial(gradient_kernel, wide),
        grid_spec=pltpu.PrefetchScalarGridSpec(
            num_scalar_prefetch=1,
            grid=(steps,),
            in_specs=[pl.BlockSpec((count, tile), lambda i, tiles: (0, tiles[i]))]
            + [whole(part) for part in parts],
            out_specs=(
                tiled(columns, tile, lambda i, tiles: jnp.minimum(i, half - 1)),
                tiled(columns, tile, lambda i, tiles: jnp.maximum(i - half, 0)),
            ),
        ),
        out_shape=(out, out),
        compiler_params=PARAMS,
    )(tiles, first_mat, *parts)


def float_shape(rows, width):
    return jax.ShapeDtypeStruct((rows, width), jnp.float32)


def steps_for(rows):
    return 4 if rows % 512 == 0 else 2 if rows % 16 == 0 else 1


def scalars(*values):
    return jnp.stack([jnp.asarray(value, jnp.int32) for value in values])


def add_kernel(first, second, out):
    out[...] = first[...] + second[...]


def add(first, second):
    rows, width = first.shape
    steps = steps_for(rows)
    spec = tiled(width, rows // steps)
    return pl.pallas_call(
        add_kernel,
        grid=(steps,),
        in_specs=[spec] * 2,
        out_specs=spec,
        out_shape=float_shape(rows, width),
        compiler_params=SMALL,
    )(first, second)


def choose_kernel(flag, first, second, out):
    @pl.when(flag[0] == 1)
    def _():
        out[...] = first[...]

    @pl.when(flag[0] == 0)
    def _():
        out[...] = second[...]


def choose(flag, first, second):
    rows, width = first.shape
    steps = steps_for(rows)
    spec = tiled(width, rows // steps)
    return pl.pallas_call(
        choose_kernel,
        grid_spec=pltpu.PrefetchScalarGridSpec(
            num_scalar_prefetch=1, grid=(steps,), in_specs=[spec] * 2, out_specs=spec
        ),
        out_shape=float_shape(rows, width),
        compiler_params=SMALL,
    )(scalars(flag), first, second)


def add_parts_kernel(first, second, *outs):
    total = first[...] + second[...]
    for number, out in enumerate(outs):

        @pl.when(pl.program_id(0) == number)
        def _(out=out):
            out[...] = total


def add_parts(first, second, parts):
    rows, width = first.shape
    outs = (float_shape(rows // parts, width),) * parts
    spec = tiled(width, rows // parts)
    return pl.pallas_call(
        add_parts_kernel,
        grid=(parts,),
        in_specs=[spec] * 2,
        out_specs=tuple(whole(out) for out in outs),
        out_shape=outs,
        compiler_params=SMALL,
    )(first, second)


def add_split_kernel(mine, first, second, away, keep):
    total = first[...] + second[...]

    @pl.when(pl.program_id(0) == 0)
    def _():
        away[...] = total

    @pl.when(pl.program_id(0) == 1)
    def _():
        keep[...] = total


def add_split(mine, first, second):
    rows, width = first.shape
    outs = (float_shape(rows // 2, width),) * 2
    spec = tiled(width, rows // 2, lambda i, mine: (i + 1 + mine[0]) % 2)
    return pl.pallas_call(
        add_split_kernel,
        grid_spec=pltpu.PrefetchScalarGridSpec(
            num_scalar_prefetch=1,
            grid=(2,),
            in_specs=[spec] * 2,
            out_specs=tuple(whole(out) for out in outs),
        ),
        out_shape=outs,
        compiler_params=SMALL,
    )(scalars(mine), first, second)


def norm_back_kernel(at, first, second, tokens, cotangent, out):
    rows = first[...] + second[...]
    normed, scale_inv = normed_rows(tokens[...])
    out[...] = cotangent[...].astype(jnp.float32) + scale_inv * (
        rows
        - jnp.mean(rows, axis=-1, keepdims=True)
        - normed * jnp.mean(rows * normed, axis=-1, keepdims=True)
    )


def norm_back(first, second, at, tokens, cotangent):
    rows, width = first.shape
    spec = pl.BlockSpec((rows, width), lambda i, at: (0, 0))
    moved = pl.BlockSpec((rows, width), lambda i, at: (at[0], 0))
    return pl.pallas_call(
        norm_back_kernel,
        grid_spec=pltpu.PrefetchScalarGridSpec(
            num_scalar_prefetch=1,
            grid=(1,),
            in_specs=[spec, spec, moved, moved],
            out_specs=spec,
        ),
        out_shape=float_shape(rows, width),
        compiler_params=SMALL,
    )(scalars(at // rows), first, second, tokens, cotangent)


def join_kernel(mine, own, other, out):
    @pl.when(pl.program_id(0) == mine[0])
    def _():
        out[...] = own[...]

    @pl.when(pl.program_id(0) != mine[0])
    def _():
        out[...] = other[...]


def join(mine, own, other):
    rows, width = own.shape
    return pl.pallas_call(
        join_kernel,
        grid_spec=pltpu.PrefetchScalarGridSpec(
            num_scalar_prefetch=1,
            grid=(2,),
            in_specs=[pl.BlockSpec((rows, width), lambda i, mine: (0, 0))] * 2,
            out_specs=tiled(width, rows, lambda i, mine: i),
        ),
        out_shape=float_shape(2 * rows, width),
        compiler_params=SMALL,
    )(scalars(mine), own, other)


def collect_kernel(count, order, *refs):
    parts, out = refs[:count], refs[-1]
    extra = refs[count:-1]
    for number, part in enumerate(parts):

        @pl.when(order[pl.program_id(0)] == number)
        def _(part=part):
            if extra:
                tokens, bias = extra
                total = tokens[...].astype(jnp.float32) + part[...] + bias[...]
                out[...] = total.astype(out.dtype)
            else:
                out[...] = part[...]


def collect(order, parts, *extra):
    rows, width = parts[0].shape
    count = len(parts)
    specs = [pl.BlockSpec((rows, width), lambda i, order: (0, 0))] * count
    if extra:
        specs = specs + [tiled(width, rows, lambda i, order: i), whole(extra[1])]
    return pl.pallas_call(
        functools.partial(collect_kernel, count),
        grid_spec=pltpu.PrefetchScalarGridSpec(
            num_scalar_prefetch=1,
            grid=(count,),
            in_specs=specs,
            out_specs=tiled(width, rows, lambda i, order: i),
        ),
        out_shape=jax.ShapeDtypeStruct(
            (count * rows, width), extra[0].dtype if extra else jnp.float32
        ),
        compiler_params=SMALL,
    )(order, *parts, *extra)


class Order:
    def __init__(self, token):
        self.token = token

    def tie(self, *arrays):
        tied = lax.optimization_barrier((self.token, *arrays))
        self.token = tied[0]
        return tied[1] if len(arrays) == 1 else tied[1:]

    def run(self, step, *arrays):
        tied = lax.optimization_barrier((self.token, *arrays))
        out = step(*tied[1:])
        out = tuple(out) if isinstance(out, list) else out
        if isinstance(out, tuple):
            return self.tie(*out)
        return self.tie(out)


class Chain:
    def __init__(self, order, steps):
        self.order, self.steps, self.out, self.held = order, steps, None, None
        self._go(None)

    def _go(self, arrived):
        try:
            array, axis, pairs = self.steps.send(arrived)
        except StopIteration as stop:
            self.held, self.out = None, stop.value
            return
        array = self.order.tie(array)
        self.held = lax.ppermute(array, axis, pairs)

    def on(self):
        if self.held is not None:
            self._go(self.order.tie(self.held))
        return self

    def end(self):
        while self.held is not None:
            self.on()
        return self.out


def swap_pairs(size, bit):
    return [(i, i ^ bit) for i in range(size)]


def tensor_steps(away, keep, size, order, finish):
    place = lax.axis_index("tensor")
    first = 0
    rows = away.shape[0]
    for number, bit in enumerate(order):
        got = yield away, "tensor", swap_pairs(size, bit)
        first = first + (place // bit) % 2 * rows
        if number + 1 < len(order):
            away, keep = add_split((place // order[number + 1]) % 2, keep, got)
            rows = rows // 2
    array = finish(keep, got, first)
    for number, bit in enumerate(reversed(order)):
        got = yield array, "tensor", swap_pairs(size, bit)
        if number + 1 < len(order):
            array = join((place // bit) % 2, array, got)
    return array, got


def core_steps(parts, size, chunks):
    away, keep = parts
    got = yield away, "dp", swap_pairs(size, 1)
    return add_parts(keep, got, chunks)


def line_steps(array, size):
    chips = size // 2
    place = lax.axis_index("dp") // 2

    def pairs(moves):
        return [(2 * a + c, 2 * b + c) for a, b in moves for c in range(2)]

    if chips > 1:
        steps = range(chips // 2 - 1)
        for s in steps:
            got = yield array, "dp", pairs([(s, s + 1), (chips - 1 - s, chips - 2 - s)])
            array = add(array, got)
        middle = chips // 2
        got = yield array, "dp", pairs([(middle - 1, middle), (middle, middle - 1)])
        array = add(array, got)
        for s in reversed(steps):
            got = yield array, "dp", pairs([(s + 1, s), (chips - 2 - s, chips - 1 - s)])
            array = choose((place == s) | (place == chips - 1 - s), got, array)
    got = yield array, "dp", swap_pairs(size, 1)
    return array, got


def add_end(keep, got, first):
    return add(keep, got)


def small_steps(stats, size):
    for bit in (1 << k for k in range(size.bit_length() - 1)):
        got = yield stats, "tensor", swap_pairs(size, bit)
        stats = stats + got
    return stats


def assemble(core, parts):
    low = [jnp.where(core == 0, mine, other) for mine, other in parts]
    high = [jnp.where(core == 0, other, mine) for mine, other in parts]
    return jnp.concatenate(low + high, axis=0)


def shards(
    dp_size,
    tensor_size,
    tokens,
    segment,
    attn_gain,
    attn_shift,
    mlp_gain,
    mlp_shift,
    w_qkv,
    b_qkv,
    w_out,
    w_up,
    b_up,
    w_down,
    b_branch,
    cotangent,
):
    rows_here, width = tokens.shape
    heads = w_qkv.shape[1] // (3 * HD)
    group = 2 if heads % 2 == 0 else heads
    wide = 3 * HD * group
    lanes = -(-wide // 128) * 128
    groups = heads // group
    bits = [1 << k for k in range(tensor_size.bit_length() - 1)]
    orders = (bits, bits[::-1])
    split = rows_here // 2
    core = lax.axis_index("dp") % 2
    place = lax.axis_index("tensor")
    order = Order(core)
    run = order.run
    mine = [(place // its[0]) % 2 for its in orders]
    tiles = jnp.stack([1 - mine[0], 3 - mine[1], mine[0], 2 + mine[1]]).astype(jnp.int32)

    def chain(steps):
        return Chain(order, steps)

    def lines(core_chain):
        return [line_steps(part, dp_size) for part in core_chain.end()]

    def grads(chunks, first_mat, *parts, wide=None, begin=0, rows=None):
        def step(first_mat, *parts):
            return gradient(1 - core, first_mat, parts, wide or parts[0].shape[1], begin, rows)

        return chain(core_steps(run(step, first_mat, *parts), dp_size, chunks))

    vectors = [v[None, :] for v in (attn_gain, attn_shift, mlp_gain, mlp_shift)]
    angles = run(turn_angles, segment[0])
    attn_low, mlp_low, projected, d_attended, hidden, slope = run(
        lambda *a: forward(a[0], a[1], vectors, *a[2:], lanes=lanes * groups),
        tokens,
        cotangent,
        w_qkv,
        b_qkv[None, :],
        w_out,
        w_up,
        b_up[None, :],
    )
    core_down = grads(1, hidden, cotangent)
    d_pre, scaled_mlp, sums_mlp, up_bias = run(
        feed_back, tokens, cotangent, slope, w_down, w_up, mlp_gain[None, :]
    )
    down = chain(lines(core_down)[0])
    core_up = grads(1, mlp_low, d_pre)
    kept = run(functools.partial(attend, heads=heads), angles, projected)
    attended = kept[0]
    partial = run(branches, tiles, attended, hidden, w_out, w_down)
    result = [
        chain(tensor_steps(partial[p], partial[2 + p], tensor_size, orders[p], add_end))
        for p in range(2)
    ]
    up = lines(core_up)[0]
    back = []
    for begin in range(0, heads, group):
        def step(angles, d_attended, *kept, begin=begin):
            return attend_back(angles, kept, d_attended, begin, group, lanes)

        back.append(run(step, angles, d_attended, *kept))
    down.on()
    up = chain(up)
    *scaled, sums_attn, qkv_bias, branch_sum = run(
        lambda tiles, *a: input_back(tiles, a[:-5], wide, *a[-5:]),
        tiles,
        *back,
        tokens,
        cotangent,
        scaled_mlp,
        w_qkv,
        attn_gain[None, :],
    )
    for part in result:
        part.on()
    small = chain(small_steps(jnp.concatenate([sums_attn, sums_mlp], axis=0), tensor_size))
    core_qkv = grads(1, attn_low, *back, wide=wide)
    small.on()
    for part in result:
        part.on()
    grad_out = run(inner_rows, attended, cotangent)
    qkv = lines(core_qkv)[0]
    stats = small.end()

    sizes = (width,) * 4 + (w_qkv.shape[1], w_up.shape[1], width)
    ends = [sum(sizes[: k + 1]) for k in range(len(sizes))]
    flat = jnp.concatenate([stats.reshape(-1), qkv_bias[0], up_bias[0], branch_sum[0]])
    spare = -(-flat.shape[0] // width // 16) * 16
    flat = jnp.pad(flat, (0, spare * width - flat.shape[0])).reshape(spare, width)

    def pack(grad_out, flat):
        packed = jnp.concatenate([grad_out, flat], axis=0)
        rows = packed.shape[0] // 2
        return tuple(
            lax.dynamic_slice_in_dim(packed, side * rows, rows, 0) for side in (1 - core, core)
        )

    core_out = chain(core_steps(run(pack, grad_out, flat), dp_size, 1))

    def back_end(part):
        def finish(keep, got, first):
            return norm_back(keep, got, first + part * split, tokens, cotangent)

        return finish

    for part in result:
        part.on()
    d_tokens = [
        chain(tensor_steps(scaled[p], scaled[2 + p], tensor_size, orders[p], back_end(p)))
        for p in range(2)
    ]
    out = lines(core_out)[0]
    down.on()
    up.on()
    qkv = chain(qkv)
    spots = scalars(mine[0], 1 - mine[0], 2 + mine[1], 3 - mine[1])
    ended = [part.end() for part in result]
    for part in d_tokens:
        part.on()
    result = run(collect, spots, [*ended[0], *ended[1]], tokens, b_branch[None, :])
    for part in d_tokens:
        part.on()
    for part in (down, up, qkv):
        part.on()
    out = chain(out)
    down.end()
    for part in d_tokens:
        part.on()
    core_spots = scalars(core, 1 - core)
    grad_down = run(collect, core_spots, [*down.end()])
    for part in (out, qkv, up):
        part.on()
    ended = [part.end() for part in d_tokens]
    d_tokens = run(collect, spots, [*ended[0], *ended[1]])
    up.end()
    grad_up = run(collect, core_spots, [*up.end()])
    out.on()
    qkv.on()
    out.on()
    qkv.end()
    grad_qkv = run(collect, core_spots, [*qkv.end()])
    packed = order.tie(assemble(core, (out.end(),)))
    grad_out = packed[: w_out.shape[0]]
    vectors = packed[w_out.shape[0] :].reshape(-1)
    a_gain, a_shift, m_gain, m_shift, qkv_bias, up_bias, branch = (
        vectors[end - size : end] for end, size in zip(ends, sizes, strict=True)
    )
    return (
        result,
        d_tokens,
        grad_qkv,
        qkv_bias,
        grad_out,
        grad_up,
        up_bias,
        grad_down,
        branch,
        a_gain,
        a_shift,
        m_gain,
        m_shift,
    )


def solution(mesh):
    placed = (
        P("dp", None),
        P("dp", None),
        P(),
        P(),
        P(),
        P(),
        P(None, "tensor"),
        P("tensor"),
        P("tensor", None),
        P(None, "tensor"),
        P("tensor"),
        P("tensor", None),
        P(),
        P("dp", None),
    )

    def body(*arrays):
        return shards(mesh.shape["dp"], mesh.shape["tensor"], *arrays)

    return jax.shard_map(
        body,
        mesh=mesh,
        in_specs=placed,
        out_specs=(
            P("dp", None),
            P("dp", None),
            P(None, "tensor"),
            P("tensor"),
            P("tensor", None),
            P(None, "tensor"),
            P("tensor"),
            P("tensor", None),
            P(),
            P(),
            P(),
            P(),
            P(),
        ),
        check_vma=False,
    )
```

```python
import functools
import math

import jax
import jax.numpy as jnp
from jax import lax
from jax.experimental import pallas as pl
from jax.experimental.pallas import tpu as pltpu
from jax.sharding import PartitionSpec as P

HD = 64
ROT = 16
MOST = 512

EPS = 1e-05
NEG = -1e30


def inner_rows(first_mat, second_mat):
    return lax.dot_general(
        first_mat, second_mat, (((0,), (0,)), ((), ())), preferred_element_type=jnp.float32
    )


def times_trans(first_mat, second_mat):
    return lax.dot_general(
        first_mat, second_mat, (((1,), (1,)), ((), ())), preferred_element_type=jnp.float32
    )


def product(first_mat, second_mat):
    return jnp.dot(first_mat, second_mat, preferred_element_type=jnp.float32)


def turn_angles(segment):
    spots = lax.broadcasted_iota(jnp.int32, segment.shape, 0)
    starts = jnp.zeros_like(segment)
    for number in range(3):
        count = jnp.sum((segment == number).astype(jnp.int32))
        starts = starts + jnp.where(segment > number, count, 0)
    offsets = (spots - starts).astype(jnp.float32)
    frequency = 10000.0 ** (-2.0 * jnp.arange(ROT // 2, dtype=jnp.float32) / ROT)
    angles = frequency[:, None] * offsets[None, :]
    number = jnp.broadcast_to(segment.astype(jnp.float32), (8, segment.shape[0]))
    return jnp.concatenate([jnp.cos(angles), jnp.sin(angles), number], axis=0)


def spread(angles, rows, take):
    return lax.dot_general(
        angles[0 : take.shape[0], rows],
        take,
        (((0,), (0,)), ((), ())),
        precision=lax.Precision.HIGHEST,
        preferred_element_type=jnp.float32,
    )


def turn_tables(angles, rows):
    tile, half = 2 * HD, ROT // 2
    source = lax.broadcasted_iota(jnp.int32, (ROT, tile), 0)
    column = lax.broadcasted_iota(jnp.int32, (ROT, tile), 1) % HD
    take_cos = ((source == column % half) & (column < ROT)).astype(jnp.float32)
    take_sin = source == column % half + half
    take_low = -(take_sin & (column < half)).astype(jnp.float32)
    take_high = (take_sin & (column >= half) & (column < ROT)).astype(jnp.float32)
    lane = lax.broadcasted_iota(jnp.int32, (rows.stop - rows.start, tile), 1)
    still = (lane % HD >= ROT).astype(jnp.float32)
    return (
        spread(angles, rows, take_cos) + still,
        spread(angles, rows, take_low),
        spread(angles, rows, take_high),
    )


def turn(wide, number, turned, low, high):
    tile, half = 2 * HD, ROT // 2
    lane = lax.broadcasted_iota(jnp.int32, wide.shape, 1)
    moved = (
        wide * turned
        + pltpu.roll(wide, tile - half, 1) * low
        + pltpu.roll(wide, half, 1) * high
    )
    if 2 * number % 3 == 2:
        return jnp.where(lane < HD, wide, moved)
    if (2 * number + 1) % 3 == 2:
        return jnp.where(lane >= HD, wide, moved)
    return moved


def key_range(start, block):
    return max(0, start - -(-MOST // block) * block), start + block


def fill_bias(bias, angles, start, block):
    first, until = key_range(start, block)
    count = until - first
    source = lax.broadcasted_iota(jnp.int32, (ROT + 8, 2 * HD), 0)
    own = spread(angles, slice(start, until), (source == ROT).astype(jnp.float32))[:, :1]
    other = angles[ROT : ROT + 1, first:until]
    query_spot = lax.broadcasted_iota(jnp.int32, (block, count), 0) + start
    key_spot = lax.broadcasted_iota(jnp.int32, (block, count), 1) + first
    bias[:, :count] = jnp.where((own == other) & (key_spot <= query_spot), 0.0, NEG)


def attend_kernel(heads, angles, projected, attended, sums, q_s, k_s, v_s, bias):
    seq_len, lanes = projected.shape
    block = min(256, seq_len)
    tile = 2 * HD
    for start in range(0, seq_len, block):
        rows = slice(start, start + block)
        turned, low, high = turn_tables(angles, rows)
        for number in range(lanes // tile):
            wide = turn(
                projected[rows, number * tile : (number + 1) * tile], number, turned, low, high
            )
            for side in range(2):
                head, kind = divmod(2 * number + side, 3)
                if head < heads:
                    part = wide[:, side * HD : (side + 1) * HD].astype(jnp.bfloat16)
                    (q_s, k_s, v_s)[kind][head, rows, :] = (
                        part * HD ** (-0.5) if kind == 0 else part
                    )
    for start in range(0, seq_len, block):
        first, until = key_range(start, block)
        count = until - first
        rows, keys = slice(start, until), slice(first, until)
        fill_bias(bias, angles, start, block)
        outs = []
        for h in range(heads):
            scores = times_trans(q_s[h, rows, :], k_s[h, keys, :]) + bias[:, :count]
            most = jnp.max(scores, axis=-1, keepdims=True)
            exponent = jnp.exp(scores - most)
            total = jnp.sum(exponent, axis=-1, keepdims=True)
            probs = (exponent * (1.0 / total)).astype(jnp.bfloat16)
            sums[rows, h : h + 1] = most + jnp.log(total)
            outs.append(product(probs, v_s[h, keys, :]))
        attended[rows, :] = jnp.concatenate(outs, axis=1).astype(jnp.bfloat16)


def attend_back_kernel(
    begin, heads, angles, q_s, k_s, v_s, sums, attended, d_attended, d_projected, dq_s, dk_s, dv_s, bias
):
    seq_len, lanes = d_projected.shape
    block = min(256, seq_len)
    tile = 2 * HD
    for start in range(0, seq_len, block):
        first, until = key_range(start, block)
        count = until - first
        rows, keys = slice(start, until), slice(first, until)
        fill_bias(bias, angles, start, block)
        for h in range(heads):
            g = begin + h
            q, k, v = q_s[g, rows, :], k_s[g, keys, :], v_s[g, keys, :]
            d_out = d_attended[rows, g * HD : (g + 1) * HD]
            out = attended[rows, g * HD : (g + 1) * HD]
            probs = jnp.exp(times_trans(q, k) + (bias[:, :count] - sums[rows, g : g + 1]))
            row_dot = jnp.sum(
                out.astype(jnp.float32) * d_out.astype(jnp.float32), axis=-1, keepdims=True
            )
            d_scores = (probs * (times_trans(d_out, v) - row_dot)).astype(jnp.bfloat16)
            dq_s[h, rows, :] = product(d_scores, k) * HD ** (-0.5)
            d_k = inner_rows(q, d_scores)
            d_v = inner_rows(d_out, probs.astype(jnp.bfloat16))
            old = count - block
            if old:
                dk_s[h, :, first:start] += d_k[:, :old]
                dv_s[h, :, first:start] += d_v[:, :old]
            dk_s[h, :, rows] = d_k[:, old:]
            dv_s[h, :, rows] = d_v[:, old:]
    for start in range(0, seq_len, block):
        rows = slice(start, start + block)
        turned, low, high = turn_tables(angles, rows)

        def section(at, rows=rows):
            head, kind = divmod(at, 3)
            if head >= heads:
                return jnp.zeros((block, HD), jnp.float32)
            return dq_s[head, rows, :] if kind == 0 else (dk_s, dv_s)[kind - 1][head, :, rows].T

        for number in range(lanes // tile):
            wide = jnp.concatenate([section(2 * number), section(2 * number + 1)], axis=1)
            d_projected[rows, number * tile : (number + 1) * tile] = turn(
                wide, number, turned, -low, -high
            ).astype(jnp.bfloat16)


VMEM = pl.BlockSpec(memory_space=pltpu.VMEM)


def bias_held(block):
    return pltpu.VMEM((block, -(-MOST // block) * block + block), jnp.float32)


def attend(angles, projected, heads):
    seq_len = projected.shape[0]
    shape = jax.ShapeDtypeStruct
    return pl.pallas_call(
        functools.partial(attend_kernel, heads),
        out_shape=(
            shape((seq_len, heads * HD), jnp.bfloat16),
            shape((seq_len, 2 * HD), jnp.float32),
        )
        + (shape((heads, seq_len, HD), jnp.bfloat16),) * 3,
        in_specs=[VMEM] * 2,
        out_specs=(VMEM,) * 5,
        scratch_shapes=[bias_held(min(256, seq_len))],
        compiler_params=pltpu.CompilerParams(vmem_limit_bytes=24 * 2**20),
    )(angles, projected)


def attend_back(angles, kept, d_attended, begin, heads, lanes):
    attended, sums, queries, keys, values = kept
    seq_len = attended.shape[0]
    cross = pltpu.VMEM((heads, HD, seq_len), jnp.float32)
    return pl.pallas_call(
        functools.partial(attend_back_kernel, begin, heads),
        out_shape=jax.ShapeDtypeStruct((seq_len, lanes), jnp.bfloat16),
        in_specs=[VMEM] * 7,
        out_specs=VMEM,
        scratch_shapes=[
            pltpu.VMEM((heads, seq_len, HD), jnp.float32),
            cross,
            cross,
            bias_held(min(256, seq_len)),
        ],
        compiler_params=pltpu.CompilerParams(vmem_limit_bytes=24 * 2**20),
    )(angles, queries, keys, values, sums, attended, d_attended)


def normed_rows(tokens):
    rows = tokens.astype(jnp.float32)
    centred = rows - jnp.mean(rows, axis=-1, keepdims=True)
    scale_inv = lax.rsqrt(jnp.mean(centred * centred, axis=-1, keepdims=True) + EPS)
    return centred * scale_inv, scale_inv


def tiled(width, tile, at=lambda i, *order: i):
    return pl.BlockSpec((tile, width), lambda i, *order: (at(i, *order), 0))


def whole(array):
    return pl.BlockSpec(array.shape, lambda i, *order: (0,) * array.ndim)


PARAMS = pltpu.CompilerParams(vmem_limit_bytes=40 * 2**20)
SMALL = pltpu.CompilerParams(vmem_limit_bytes=48 * 2**20)


def forward_kernel(
    tokens,
    cotangent,
    attn_gain,
    attn_shift,
    mlp_gain,
    mlp_shift,
    w_qkv,
    b_qkv,
    w_out,
    w_up,
    b_up,
    attn_low,
    mlp_low,
    projected,
    d_attended,
    hidden,
    slope,
):
    normed, _ = normed_rows(tokens[...])
    attn_in = (normed * attn_gain[...] + attn_shift[...]).astype(jnp.bfloat16)
    mlp_in = (normed * mlp_gain[...] + mlp_shift[...]).astype(jnp.bfloat16)
    attn_low[...] = attn_in
    mlp_low[...] = mlp_in
    count, lanes = w_qkv.shape[1], projected.shape[1]
    if lanes > count:
        projected[...] = jnp.zeros(projected.shape, jnp.float32)
    projected[:, :count] = product(attn_in, w_qkv[...]) + b_qkv[...]
    d_attended[...] = times_trans(cotangent[...], w_out[...]).astype(jnp.bfloat16)
    pre_act = product(mlp_in, w_up[...]) + b_up[...]
    below = 0.5 * (1.0 + lax.erf(pre_act * (0.5**0.5)))
    bell = jnp.exp(-0.5 * pre_act * pre_act) * ((2.0 * math.pi) ** -0.5)
    hidden[...] = (pre_act * below).astype(jnp.bfloat16)
    slope[...] = (below + pre_act * bell).astype(slope.dtype)


def forward(tokens, cotangent, vectors, w_qkv, b_qkv, w_out, w_up, b_up, lanes):
    rows, width = tokens.shape
    tile = rows // 4
    fixed = (*vectors, w_qkv, b_qkv, w_out, w_up, b_up)
    outs = (
        (width, jnp.bfloat16),
        (width, jnp.bfloat16),
        (lanes, jnp.float32),
        (w_out.shape[0], jnp.bfloat16),
        (w_up.shape[1], jnp.bfloat16),
        (w_up.shape[1], jnp.float32),
    )
    return pl.pallas_call(
        forward_kernel,
        grid=(4,),
        in_specs=[tiled(width, tile)] * 2 + [whole(array) for array in fixed],
        out_specs=tuple(tiled(wide, tile) for wide, _ in outs),
        out_shape=tuple(jax.ShapeDtypeStruct((rows, wide), kind) for wide, kind in outs),
        compiler_params=PARAMS,
    )(tokens, cotangent, *fixed)


def feed_back_kernel(
    tokens, cotangent, slope, w_down, w_up, mlp_gain, d_pre, scaled, sums, bias_sum
):
    @pl.when(pl.program_id(0) == 0)
    def _():
        sums[...] = jnp.zeros(sums.shape, jnp.float32)
        bias_sum[...] = jnp.zeros(bias_sum.shape, jnp.float32)

    d_low = (times_trans(cotangent[...], w_down[...]) * slope[...]).astype(jnp.bfloat16)
    d_pre[...] = d_low
    d_in = times_trans(d_low, w_up[...])
    scaled[...] = d_in * mlp_gain[...]
    normed, _ = normed_rows(tokens[...])
    sums[0:1, :] += jnp.sum(d_in * normed, axis=0, keepdims=True)
    sums[1:2, :] += jnp.sum(d_in, axis=0, keepdims=True)
    bias_sum[...] += jnp.sum(d_low.astype(jnp.float32), axis=0, keepdims=True)


def feed_back(tokens, cotangent, slope, w_down, w_up, mlp_gain):
    rows, width = tokens.shape
    inner = w_up.shape[1]
    tile = rows // 4
    fixed = (w_down, w_up, mlp_gain)
    shape = jax.ShapeDtypeStruct
    out_shape = (
        shape((rows, inner), jnp.bfloat16),
        shape((rows, width), jnp.float32),
        shape((2, width), jnp.float32),
        shape((1, inner), jnp.float32),
    )
    return pl.pallas_call(
        feed_back_kernel,
        grid=(4,),
        in_specs=[tiled(width, tile)] * 2 + [tiled(inner, tile)] + [whole(a) for a in fixed],
        out_specs=(tiled(inner, tile), tiled(width, tile)) + tuple(whole(a) for a in out_shape[2:]),
        out_shape=out_shape,
        compiler_params=PARAMS,
    )(tokens, cotangent, slope, *fixed)


def quarter_outs(rows, width):
    shape = jax.ShapeDtypeStruct((rows // 4, width), jnp.float32)
    return (shape,) * 4


def branches_kernel(tiles, attended, hidden, w_out, w_down, *outs):
    total = product(attended[...], w_out[...]) + product(hidden[...], w_down[...])
    for number, out in enumerate(outs):

        @pl.when(pl.program_id(0) == number)
        def _(out=out):
            out[...] = total


def picked(i, tiles):
    return tiles[i]


def branches(tiles, attended, hidden, w_out, w_down):
    rows, width = hidden.shape[0], w_down.shape[1]
    outs = quarter_outs(rows, width)
    return pl.pallas_call(
        branches_kernel,
        grid_spec=pltpu.PrefetchScalarGridSpec(
            num_scalar_prefetch=1,
            grid=(4,),
            in_specs=[
                tiled(attended.shape[1], rows // 4, picked),
                tiled(hidden.shape[1], rows // 4, picked),
                whole(w_out),
                whole(w_down),
            ],
            out_specs=tuple(whole(out) for out in outs),
        ),
        out_shape=outs,
        compiler_params=PARAMS,
    )(tiles, attended, hidden, w_out, w_down)


def input_back_kernel(count, heads_wide, tiles, *refs):
    d_heads, rest = refs[:count], refs[count:]
    tokens, cotangent, before, w_qkv, attn_gain = rest[:5]
    outs, (sums, bias_sum, branch_sum) = rest[5:9], rest[9:]

    @pl.when(pl.program_id(0) == 0)
    def _():
        for held in (sums, bias_sum, branch_sum):
            held[...] = jnp.zeros(held.shape, jnp.float32)

    d_in = None
    for number, part in enumerate(d_heads):
        columns = slice(number * heads_wide, (number + 1) * heads_wide)
        low = part[:, :heads_wide]
        term = times_trans(low, w_qkv[:, columns])
        d_in = term if d_in is None else d_in + term
        bias_sum[:, columns] += jnp.sum(low.astype(jnp.float32), axis=0, keepdims=True)
    normed, _ = normed_rows(tokens[...])
    sums[0:1, :] += jnp.sum(d_in * normed, axis=0, keepdims=True)
    sums[1:2, :] += jnp.sum(d_in, axis=0, keepdims=True)
    branch_sum[...] += jnp.sum(cotangent[...].astype(jnp.float32), axis=0, keepdims=True)
    total = d_in * attn_gain[...] + before[...]
    for number, out in enumerate(outs):

        @pl.when(pl.program_id(0) == number)
        def _(out=out):
            out[...] = total


def input_back(tiles, d_heads, heads_wide, tokens, cotangent, before, w_qkv, attn_gain):
    rows, width = tokens.shape
    tile = rows // 4
    shape = jax.ShapeDtypeStruct
    outs = quarter_outs(rows, width) + (
        shape((2, width), jnp.float32),
        shape((1, w_qkv.shape[1]), jnp.float32),
        shape((1, width), jnp.float32),
    )
    return pl.pallas_call(
        functools.partial(input_back_kernel, len(d_heads), heads_wide),
        grid_spec=pltpu.PrefetchScalarGridSpec(
            num_scalar_prefetch=1,
            grid=(4,),
            in_specs=[tiled(part.shape[1], tile, picked) for part in d_heads]
            + [tiled(width, tile, picked)] * 3
            + [whole(w_qkv), whole(attn_gain)],
            out_specs=tuple(whole(out) for out in outs),
        ),
        out_shape=outs,
        compiler_params=PARAMS,
    )(tiles, *d_heads, tokens, cotangent, before, w_qkv, attn_gain)


def gradient_kernel(wide, tiles, first_mat, *refs):
    parts, outs = refs[:-2], refs[-2:]
    for number, part in enumerate(parts):
        block = inner_rows(first_mat[...], part[:, :wide])
        columns = slice(number * wide, (number + 1) * wide)
        for side, out in enumerate(outs):

            @pl.when(pl.program_id(0) // (pl.num_programs(0) // 2) == side)
            def _(out=out, block=block, columns=columns):
                out[:, columns] = block


def gradient(swapped, first_mat, parts, wide, begin=0, rows=None):
    count = first_mat.shape[0]
    rows = rows or first_mat.shape[1]
    steps = 4 if rows >= 1024 else 2
    tile = rows // steps
    half = steps // 2
    columns = wide * len(parts)
    if tile % 128:
        full = inner_rows(
            first_mat[:, begin : begin + rows],
            jnp.concatenate([part[:, :wide] for part in parts], axis=1),
        )
        return tuple(
            lax.dynamic_slice_in_dim(full, side * (rows // 2), rows // 2, 0)
            for side in (swapped, 1 - swapped)
        )
    tiles = (jnp.arange(steps, dtype=jnp.int32) + swapped * half) % steps + begin // tile
    out = jax.ShapeDtypeStruct((rows // 2, columns), jnp.float32)
    return pl.pallas_call(
        functools.partial(gradient_kernel, wide),
        grid_spec=pltpu.PrefetchScalarGridSpec(
            num_scalar_prefetch=1,
            grid=(steps,),
            in_specs=[pl.BlockSpec((count, tile), lambda i, tiles: (0, tiles[i]))]
            + [whole(part) for part in parts],
            out_specs=(
                tiled(columns, tile, lambda i, tiles: jnp.minimum(i, half - 1)),
                tiled(columns, tile, lambda i, tiles: jnp.maximum(i - half, 0)),
            ),
        ),
        out_shape=(out, out),
        compiler_params=PARAMS,
    )(tiles, first_mat, *parts)


def float_shape(rows, width):
    return jax.ShapeDtypeStruct((rows, width), jnp.float32)


def steps_for(rows):
    return 4 if rows % 512 == 0 else 2 if rows % 16 == 0 else 1


def scalars(*values):
    return jnp.stack([jnp.asarray(value, jnp.int32) for value in values])


def add_kernel(first, second, out):
    out[...] = first[...] + second[...]


def add(first, second):
    rows, width = first.shape
    steps = steps_for(rows)
    spec = tiled(width, rows // steps)
    return pl.pallas_call(
        add_kernel,
        grid=(steps,),
        in_specs=[spec] * 2,
        out_specs=spec,
        out_shape=float_shape(rows, width),
        compiler_params=SMALL,
    )(first, second)


def choose_kernel(flag, first, second, out):
    @pl.when(flag[0] == 1)
    def _():
        out[...] = first[...]

    @pl.when(flag[0] == 0)
    def _():
        out[...] = second[...]


def choose(flag, first, second):
    rows, width = first.shape
    steps = steps_for(rows)
    spec = tiled(width, rows // steps)
    return pl.pallas_call(
        choose_kernel,
        grid_spec=pltpu.PrefetchScalarGridSpec(
            num_scalar_prefetch=1, grid=(steps,), in_specs=[spec] * 2, out_specs=spec
        ),
        out_shape=float_shape(rows, width),
        compiler_params=SMALL,
    )(scalars(flag), first, second)


def add_parts_kernel(first, second, *outs):
    total = first[...] + second[...]
    for number, out in enumerate(outs):

        @pl.when(pl.program_id(0) == number)
        def _(out=out):
            out[...] = total


def add_parts(first, second, parts):
    rows, width = first.shape
    outs = (float_shape(rows // parts, width),) * parts
    spec = tiled(width, rows // parts)
    return pl.pallas_call(
        add_parts_kernel,
        grid=(parts,),
        in_specs=[spec] * 2,
        out_specs=tuple(whole(out) for out in outs),
        out_shape=outs,
        compiler_params=SMALL,
    )(first, second)


def add_split_kernel(mine, first, second, away, keep):
    total = first[...] + second[...]

    @pl.when(pl.program_id(0) == 0)
    def _():
        away[...] = total

    @pl.when(pl.program_id(0) == 1)
    def _():
        keep[...] = total


def add_split(mine, first, second):
    rows, width = first.shape
    outs = (float_shape(rows // 2, width),) * 2
    spec = tiled(width, rows // 2, lambda i, mine: (i + 1 + mine[0]) % 2)
    return pl.pallas_call(
        add_split_kernel,
        grid_spec=pltpu.PrefetchScalarGridSpec(
            num_scalar_prefetch=1,
            grid=(2,),
            in_specs=[spec] * 2,
            out_specs=tuple(whole(out) for out in outs),
        ),
        out_shape=outs,
        compiler_params=SMALL,
    )(scalars(mine), first, second)


def norm_back_kernel(at, first, second, tokens, cotangent, out):
    rows = first[...] + second[...]
    normed, scale_inv = normed_rows(tokens[...])
    out[...] = cotangent[...].astype(jnp.float32) + scale_inv * (
        rows
        - jnp.mean(rows, axis=-1, keepdims=True)
        - normed * jnp.mean(rows * normed, axis=-1, keepdims=True)
    )


def norm_back(first, second, at, tokens, cotangent):
    rows, width = first.shape
    spec = pl.BlockSpec((rows, width), lambda i, at: (0, 0))
    moved = pl.BlockSpec((rows, width), lambda i, at: (at[0], 0))
    return pl.pallas_call(
        norm_back_kernel,
        grid_spec=pltpu.PrefetchScalarGridSpec(
            num_scalar_prefetch=1,
            grid=(1,),
            in_specs=[spec, spec, moved, moved],
            out_specs=spec,
        ),
        out_shape=float_shape(rows, width),
        compiler_params=SMALL,
    )(scalars(at // rows), first, second, tokens, cotangent)


def join_kernel(mine, own, other, out):
    @pl.when(pl.program_id(0) == mine[0])
    def _():
        out[...] = own[...]

    @pl.when(pl.program_id(0) != mine[0])
    def _():
        out[...] = other[...]


def join(mine, own, other):
    rows, width = own.shape
    return pl.pallas_call(
        join_kernel,
        grid_spec=pltpu.PrefetchScalarGridSpec(
            num_scalar_prefetch=1,
            grid=(2,),
            in_specs=[pl.BlockSpec((rows, width), lambda i, mine: (0, 0))] * 2,
            out_specs=tiled(width, rows, lambda i, mine: i),
        ),
        out_shape=float_shape(2 * rows, width),
        compiler_params=SMALL,
    )(scalars(mine), own, other)


def collect_kernel(count, order, *refs):
    parts, out = refs[:count], refs[-1]
    extra = refs[count:-1]
    for number, part in enumerate(parts):

        @pl.when(order[pl.program_id(0)] == number)
        def _(part=part):
            if extra:
                tokens, bias = extra
                total = tokens[...].astype(jnp.float32) + part[...] + bias[...]
                out[...] = total.astype(out.dtype)
            else:
                out[...] = part[...]


def collect(order, parts, *extra):
    rows, width = parts[0].shape
    count = len(parts)
    specs = [pl.BlockSpec((rows, width), lambda i, order: (0, 0))] * count
    if extra:
        specs = specs + [tiled(width, rows, lambda i, order: i), whole(extra[1])]
    return pl.pallas_call(
        functools.partial(collect_kernel, count),
        grid_spec=pltpu.PrefetchScalarGridSpec(
            num_scalar_prefetch=1,
            grid=(count,),
            in_specs=specs,
            out_specs=tiled(width, rows, lambda i, order: i),
        ),
        out_shape=jax.ShapeDtypeStruct(
            (count * rows, width), extra[0].dtype if extra else jnp.float32
        ),
        compiler_params=SMALL,
    )(order, *parts, *extra)


class Order:
    def __init__(self, token):
        self.token = token

    def tie(self, *arrays):
        tied = lax.optimization_barrier((self.token, *arrays))
        self.token = tied[0]
        return tied[1] if len(arrays) == 1 else tied[1:]

    def run(self, step, *arrays):
        tied = lax.optimization_barrier((self.token, *arrays))
        out = step(*tied[1:])
        out = tuple(out) if isinstance(out, list) else out
        if isinstance(out, tuple):
            return self.tie(*out)
        return self.tie(out)


class Chain:
    def __init__(self, order, steps):
        self.order, self.steps, self.out, self.held = order, steps, None, None
        self._go(None)

    def _go(self, arrived):
        try:
            array, axis, pairs = self.steps.send(arrived)
        except StopIteration as stop:
            self.held, self.out = None, stop.value
            return
        array = self.order.tie(array)
        self.held = lax.ppermute(array, axis, pairs)

    def on(self):
        if self.held is not None:
            self._go(self.order.tie(self.held))
        return self

    def end(self):
        while self.held is not None:
            self.on()
        return self.out


def swap_pairs(size, bit):
    return [(i, i ^ bit) for i in range(size)]


def tensor_steps(away, keep, size, order, finish):
    place = lax.axis_index("tensor")
    first = 0
    rows = away.shape[0]
    for number, bit in enumerate(order):
        got = yield away, "tensor", swap_pairs(size, bit)
        first = first + (place // bit) % 2 * rows
        if number + 1 < len(order):
            away, keep = add_split((place // order[number + 1]) % 2, keep, got)
            rows = rows // 2
    array = finish(keep, got, first)
    for number, bit in enumerate(reversed(order)):
        got = yield array, "tensor", swap_pairs(size, bit)
        if number + 1 < len(order):
            array = join((place // bit) % 2, array, got)
    return array, got


def core_steps(parts, size, chunks):
    away, keep = parts
    got = yield away, "dp", swap_pairs(size, 1)
    return add_parts(keep, got, chunks)


def line_steps(array, size):
    chips = size // 2
    place = lax.axis_index("dp") // 2

    def pairs(moves):
        return [(2 * a + c, 2 * b + c) for a, b in moves for c in range(2)]

    if chips > 1:
        steps = range(chips // 2 - 1)
        for s in steps:
            got = yield array, "dp", pairs([(s, s + 1), (chips - 1 - s, chips - 2 - s)])
            array = add(array, got)
        middle = chips // 2
        got = yield array, "dp", pairs([(middle - 1, middle), (middle, middle - 1)])
        array = add(array, got)
        for s in reversed(steps):
            got = yield array, "dp", pairs([(s + 1, s), (chips - 2 - s, chips - 1 - s)])
            array = choose((place == s) | (place == chips - 1 - s), got, array)
    got = yield array, "dp", swap_pairs(size, 1)
    return array, got


def add_end(keep, got, first):
    return add(keep, got)


def small_steps(stats, size):
    for bit in (1 << k for k in range(size.bit_length() - 1)):
        got = yield stats, "tensor", swap_pairs(size, bit)
        stats = stats + got
    return stats


def assemble(core, parts):
    low = [jnp.where(core == 0, mine, other) for mine, other in parts]
    high = [jnp.where(core == 0, other, mine) for mine, other in parts]
    return jnp.concatenate(low + high, axis=0)


def shards(
    dp_size,
    tensor_size,
    tokens,
    segment,
    attn_gain,
    attn_shift,
    mlp_gain,
    mlp_shift,
    w_qkv,
    b_qkv,
    w_out,
    w_up,
    b_up,
    w_down,
    b_branch,
    cotangent,
):
    rows_here, width = tokens.shape
    heads = w_qkv.shape[1] // (3 * HD)
    group = 2 if heads % 2 == 0 else heads
    wide = 3 * HD * group
    lanes = -(-wide // 128) * 128
    groups = heads // group
    bits = [1 << k for k in range(tensor_size.bit_length() - 1)]
    orders = (bits, bits[::-1])
    split = rows_here // 2
    core = lax.axis_index("dp") % 2
    place = lax.axis_index("tensor")
    order = Order(core)
    run = order.run
    mine = [(place // its[0]) % 2 for its in orders]
    tiles = jnp.stack([1 - mine[0], 3 - mine[1], mine[0], 2 + mine[1]]).astype(jnp.int32)

    def chain(steps):
        return Chain(order, steps)

    def lines(core_chain):
        return [line_steps(part, dp_size) for part in core_chain.end()]

    def grads(chunks, first_mat, *parts, wide=None, begin=0, rows=None):
        def step(first_mat, *parts):
            return gradient(1 - core, first_mat, parts, wide or parts[0].shape[1], begin, rows)

        return chain(core_steps(run(step, first_mat, *parts), dp_size, chunks))

    vectors = [v[None, :] for v in (attn_gain, attn_shift, mlp_gain, mlp_shift)]
    angles = run(turn_angles, segment[0])
    attn_low, mlp_low, projected, d_attended, hidden, slope = run(
        lambda *a: forward(a[0], a[1], vectors, *a[2:], lanes=lanes * groups),
        tokens,
        cotangent,
        w_qkv,
        b_qkv[None, :],
        w_out,
        w_up,
        b_up[None, :],
    )
    core_down = grads(1, hidden, cotangent)
    d_pre, scaled_mlp, sums_mlp, up_bias = run(
        feed_back, tokens, cotangent, slope, w_down, w_up, mlp_gain[None, :]
    )
    down = chain(lines(core_down)[0])
    core_up = grads(1, mlp_low, d_pre)
    kept = run(functools.partial(attend, heads=heads), angles, projected)
    attended = kept[0]
    partial = run(branches, tiles, attended, hidden, w_out, w_down)
    result = [
        chain(tensor_steps(partial[p], partial[2 + p], tensor_size, orders[p], add_end))
        for p in range(2)
    ]
    up = lines(core_up)[0]
    back = []
    for begin in range(0, heads, group):
        def step(angles, d_attended, *kept, begin=begin):
            return attend_back(angles, kept, d_attended, begin, group, lanes)

        back.append(run(step, angles, d_attended, *kept))
    for part in result:
        part.on()
    down.on()
    up = chain(up)
    *scaled, sums_attn, qkv_bias, branch_sum = run(
        lambda tiles, *a: input_back(tiles, a[:-5], wide, *a[-5:]),
        tiles,
        *back,
        tokens,
        cotangent,
        scaled_mlp,
        w_qkv,
        attn_gain[None, :],
    )
    core_qkv = grads(1, attn_low, *back, wide=wide)
    for part in result:
        part.on()
    grad_out = run(inner_rows, attended, cotangent)
    qkv = lines(core_qkv)[0]
    down.on()
    up.on()
    qkv = chain(qkv)
    for part in result:
        part.on()
    small = chain(small_steps(jnp.concatenate([sums_attn, sums_mlp], axis=0), tensor_size))
    small.on()
    stats = small.end()

    sizes = (width,) * 4 + (w_qkv.shape[1], w_up.shape[1], width)
    ends = [sum(sizes[: k + 1]) for k in range(len(sizes))]
    flat = jnp.concatenate([stats.reshape(-1), qkv_bias[0], up_bias[0], branch_sum[0]])
    spare = -(-flat.shape[0] // width // 16) * 16
    flat = jnp.pad(flat, (0, spare * width - flat.shape[0])).reshape(spare, width)

    def pack(grad_out, flat):
        packed = jnp.concatenate([grad_out, flat], axis=0)
        rows = packed.shape[0] // 2
        return tuple(
            lax.dynamic_slice_in_dim(packed, side * rows, rows, 0) for side in (1 - core, core)
        )

    core_out = chain(core_steps(run(pack, grad_out, flat), dp_size, 1))

    def back_end(part):
        def finish(keep, got, first):
            return norm_back(keep, got, first + part * split, tokens, cotangent)

        return finish

    out = lines(core_out)[0]
    spots = scalars(mine[0], 1 - mine[0], 2 + mine[1], 3 - mine[1])
    ended = [part.end() for part in result]
    d_tokens = [
        chain(tensor_steps(scaled[p], scaled[2 + p], tensor_size, orders[p], back_end(p)))
        for p in range(2)
    ]
    for part in d_tokens:
        part.on()
    result = run(collect, spots, [*ended[0], *ended[1]], tokens, b_branch[None, :])
    for part in d_tokens:
        part.on()
    for part in (down, up, qkv):
        part.on()
    out = chain(out)
    down.end()
    for part in d_tokens:
        part.on()
    core_spots = scalars(core, 1 - core)
    grad_down = run(collect, core_spots, [*down.end()])
    for part in (out, qkv, up):
        part.on()
    ended = [part.end() for part in d_tokens]
    d_tokens = run(collect, spots, [*ended[0], *ended[1]])
    up.end()
    grad_up = run(collect, core_spots, [*up.end()])
    out.on()
    qkv.on()
    out.on()
    qkv.end()
    grad_qkv = run(collect, core_spots, [*qkv.end()])
    packed = order.tie(assemble(core, (out.end(),)))
    grad_out = packed[: w_out.shape[0]]
    vectors = packed[w_out.shape[0] :].reshape(-1)
    a_gain, a_shift, m_gain, m_shift, qkv_bias, up_bias, branch = (
        vectors[end - size : end] for end, size in zip(ends, sizes, strict=True)
    )
    return (
        result,
        d_tokens,
        grad_qkv,
        qkv_bias,
        grad_out,
        grad_up,
        up_bias,
        grad_down,
        branch,
        a_gain,
        a_shift,
        m_gain,
        m_shift,
    )


def solution(mesh):
    placed = (
        P("dp", None),
        P("dp", None),
        P(),
        P(),
        P(),
        P(),
        P(None, "tensor"),
        P("tensor"),
        P("tensor", None),
        P(None, "tensor"),
        P("tensor"),
        P("tensor", None),
        P(),
        P("dp", None),
    )

    def body(*arrays):
        return shards(mesh.shape["dp"], mesh.shape["tensor"], *arrays)

    return jax.shard_map(
        body,
        mesh=mesh,
        in_specs=placed,
        out_specs=(
            P("dp", None),
            P("dp", None),
            P(None, "tensor"),
            P("tensor"),
            P("tensor", None),
            P(None, "tensor"),
            P("tensor"),
            P("tensor", None),
            P(),
            P(),
            P(),
            P(),
            P(),
        ),
        check_vma=False,
    )
```

```python
import functools
import math

import jax
import jax.numpy as jnp
from jax import lax
from jax.experimental import pallas as pl
from jax.experimental.pallas import tpu as pltpu
from jax.sharding import PartitionSpec as P

HD = 64
ROT = 16
MOST = 512

EPS = 1e-05
NEG = -1e30


def inner_rows(first_mat, second_mat):
    return lax.dot_general(
        first_mat, second_mat, (((0,), (0,)), ((), ())), preferred_element_type=jnp.float32
    )


def times_trans(first_mat, second_mat):
    return lax.dot_general(
        first_mat, second_mat, (((1,), (1,)), ((), ())), preferred_element_type=jnp.float32
    )


def product(first_mat, second_mat):
    return jnp.dot(first_mat, second_mat, preferred_element_type=jnp.float32)


def turn_angles(segment):
    spots = lax.broadcasted_iota(jnp.int32, segment.shape, 0)
    starts = jnp.zeros_like(segment)
    for number in range(3):
        count = jnp.sum((segment == number).astype(jnp.int32))
        starts = starts + jnp.where(segment > number, count, 0)
    offsets = (spots - starts).astype(jnp.float32)
    frequency = 10000.0 ** (-2.0 * jnp.arange(ROT // 2, dtype=jnp.float32) / ROT)
    angles = frequency[:, None] * offsets[None, :]
    number = jnp.broadcast_to(segment.astype(jnp.float32), (8, segment.shape[0]))
    return jnp.concatenate([jnp.cos(angles), jnp.sin(angles), number], axis=0)


def spread(angles, rows, take):
    return lax.dot_general(
        angles[0 : take.shape[0], rows],
        take,
        (((0,), (0,)), ((), ())),
        precision=lax.Precision.HIGHEST,
        preferred_element_type=jnp.float32,
    )


def turn_tables(angles, rows):
    tile, half = 2 * HD, ROT // 2
    source = lax.broadcasted_iota(jnp.int32, (ROT, tile), 0)
    column = lax.broadcasted_iota(jnp.int32, (ROT, tile), 1) % HD
    take_cos = ((source == column % half) & (column < ROT)).astype(jnp.float32)
    take_sin = source == column % half + half
    take_low = -(take_sin & (column < half)).astype(jnp.float32)
    take_high = (take_sin & (column >= half) & (column < ROT)).astype(jnp.float32)
    lane = lax.broadcasted_iota(jnp.int32, (rows.stop - rows.start, tile), 1)
    still = (lane % HD >= ROT).astype(jnp.float32)
    return (
        spread(angles, rows, take_cos) + still,
        spread(angles, rows, take_low),
        spread(angles, rows, take_high),
    )


def turn(wide, number, turned, low, high):
    tile, half = 2 * HD, ROT // 2
    lane = lax.broadcasted_iota(jnp.int32, wide.shape, 1)
    moved = (
        wide * turned
        + pltpu.roll(wide, tile - half, 1) * low
        + pltpu.roll(wide, half, 1) * high
    )
    if 2 * number % 3 == 2:
        return jnp.where(lane < HD, wide, moved)
    if (2 * number + 1) % 3 == 2:
        return jnp.where(lane >= HD, wide, moved)
    return moved


def key_range(start, block):
    return max(0, start - -(-MOST // block) * block), start + block


def fill_bias(bias, angles, start, block):
    first, until = key_range(start, block)
    count = until - first
    source = lax.broadcasted_iota(jnp.int32, (ROT + 8, 2 * HD), 0)
    own = spread(angles, slice(start, until), (source == ROT).astype(jnp.float32))[:, :1]
    other = angles[ROT : ROT + 1, first:until]
    query_spot = lax.broadcasted_iota(jnp.int32, (block, count), 0) + start
    key_spot = lax.broadcasted_iota(jnp.int32, (block, count), 1) + first
    bias[:, :count] = jnp.where((own == other) & (key_spot <= query_spot), 0.0, NEG)


def attend_kernel(heads, angles, projected, attended, sums, q_s, k_s, v_s, bias):
    seq_len, lanes = projected.shape
    block = min(256, seq_len)
    tile = 2 * HD
    for start in range(0, seq_len, block):
        rows = slice(start, start + block)
        turned, low, high = turn_tables(angles, rows)
        for number in range(lanes // tile):
            wide = turn(
                projected[rows, number * tile : (number + 1) * tile], number, turned, low, high
            )
            for side in range(2):
                head, kind = divmod(2 * number + side, 3)
                if head < heads:
                    part = wide[:, side * HD : (side + 1) * HD].astype(jnp.bfloat16)
                    (q_s, k_s, v_s)[kind][head, rows, :] = (
                        part * HD ** (-0.5) if kind == 0 else part
                    )
    for start in range(0, seq_len, block):
        first, until = key_range(start, block)
        count = until - first
        rows, keys = slice(start, until), slice(first, until)
        fill_bias(bias, angles, start, block)
        outs = []
        for h in range(heads):
            scores = times_trans(q_s[h, rows, :], k_s[h, keys, :]) + bias[:, :count]
            most = jnp.max(scores, axis=-1, keepdims=True)
            exponent = jnp.exp(scores - most)
            total = jnp.sum(exponent, axis=-1, keepdims=True)
            probs = (exponent * (1.0 / total)).astype(jnp.bfloat16)
            sums[rows, h : h + 1] = most + jnp.log(total)
            outs.append(product(probs, v_s[h, keys, :]))
        attended[rows, :] = jnp.concatenate(outs, axis=1).astype(jnp.bfloat16)


def attend_back_kernel(
    begin, heads, angles, q_s, k_s, v_s, sums, attended, d_attended, d_projected, dq_s, dk_s, dv_s, bias
):
    seq_len, lanes = d_projected.shape
    block = min(256, seq_len)
    tile = 2 * HD
    for start in range(0, seq_len, block):
        first, until = key_range(start, block)
        count = until - first
        rows, keys = slice(start, until), slice(first, until)
        fill_bias(bias, angles, start, block)
        for h in range(heads):
            g = begin + h
            q, k, v = q_s[g, rows, :], k_s[g, keys, :], v_s[g, keys, :]
            d_out = d_attended[rows, g * HD : (g + 1) * HD]
            out = attended[rows, g * HD : (g + 1) * HD]
            probs = jnp.exp(times_trans(q, k) + (bias[:, :count] - sums[rows, g : g + 1]))
            row_dot = jnp.sum(
                out.astype(jnp.float32) * d_out.astype(jnp.float32), axis=-1, keepdims=True
            )
            d_scores = (probs * (times_trans(d_out, v) - row_dot)).astype(jnp.bfloat16)
            dq_s[h, rows, :] = product(d_scores, k) * HD ** (-0.5)
            d_k = inner_rows(q, d_scores)
            d_v = inner_rows(d_out, probs.astype(jnp.bfloat16))
            old = count - block
            if old:
                dk_s[h, :, first:start] += d_k[:, :old]
                dv_s[h, :, first:start] += d_v[:, :old]
            dk_s[h, :, rows] = d_k[:, old:]
            dv_s[h, :, rows] = d_v[:, old:]
    for start in range(0, seq_len, block):
        rows = slice(start, start + block)
        turned, low, high = turn_tables(angles, rows)

        def section(at, rows=rows):
            head, kind = divmod(at, 3)
            if head >= heads:
                return jnp.zeros((block, HD), jnp.float32)
            return dq_s[head, rows, :] if kind == 0 else (dk_s, dv_s)[kind - 1][head, :, rows].T

        for number in range(lanes // tile):
            wide = jnp.concatenate([section(2 * number), section(2 * number + 1)], axis=1)
            d_projected[rows, number * tile : (number + 1) * tile] = turn(
                wide, number, turned, -low, -high
            ).astype(jnp.bfloat16)


VMEM = pl.BlockSpec(memory_space=pltpu.VMEM)


def bias_held(block):
    return pltpu.VMEM((block, -(-MOST // block) * block + block), jnp.float32)


def attend(angles, projected, heads):
    seq_len = projected.shape[0]
    shape = jax.ShapeDtypeStruct
    return pl.pallas_call(
        functools.partial(attend_kernel, heads),
        out_shape=(
            shape((seq_len, heads * HD), jnp.bfloat16),
            shape((seq_len, 2 * HD), jnp.float32),
        )
        + (shape((heads, seq_len, HD), jnp.bfloat16),) * 3,
        in_specs=[VMEM] * 2,
        out_specs=(VMEM,) * 5,
        scratch_shapes=[bias_held(min(256, seq_len))],
        compiler_params=pltpu.CompilerParams(vmem_limit_bytes=24 * 2**20),
    )(angles, projected)


def attend_back(angles, kept, d_attended, begin, heads, lanes):
    attended, sums, queries, keys, values = kept
    seq_len = attended.shape[0]
    cross = pltpu.VMEM((heads, HD, seq_len), jnp.float32)
    return pl.pallas_call(
        functools.partial(attend_back_kernel, begin, heads),
        out_shape=jax.ShapeDtypeStruct((seq_len, lanes), jnp.bfloat16),
        in_specs=[VMEM] * 7,
        out_specs=VMEM,
        scratch_shapes=[
            pltpu.VMEM((heads, seq_len, HD), jnp.float32),
            cross,
            cross,
            bias_held(min(256, seq_len)),
        ],
        compiler_params=pltpu.CompilerParams(vmem_limit_bytes=24 * 2**20),
    )(angles, queries, keys, values, sums, attended, d_attended)


def normed_rows(tokens):
    rows = tokens.astype(jnp.float32)
    centred = rows - jnp.mean(rows, axis=-1, keepdims=True)
    scale_inv = lax.rsqrt(jnp.mean(centred * centred, axis=-1, keepdims=True) + EPS)
    return centred * scale_inv, scale_inv


def tiled(width, tile, at=lambda i, *order: i):
    return pl.BlockSpec((tile, width), lambda i, *order: (at(i, *order), 0))


def whole(array):
    return pl.BlockSpec(array.shape, lambda i, *order: (0,) * array.ndim)


PARAMS = pltpu.CompilerParams(vmem_limit_bytes=40 * 2**20)
SMALL = pltpu.CompilerParams(vmem_limit_bytes=48 * 2**20)


def forward_kernel(
    tokens,
    cotangent,
    attn_gain,
    attn_shift,
    mlp_gain,
    mlp_shift,
    w_qkv,
    b_qkv,
    w_out,
    w_up,
    b_up,
    attn_low,
    mlp_low,
    projected,
    d_attended,
    hidden,
    slope,
):
    normed, _ = normed_rows(tokens[...])
    attn_in = (normed * attn_gain[...] + attn_shift[...]).astype(jnp.bfloat16)
    mlp_in = (normed * mlp_gain[...] + mlp_shift[...]).astype(jnp.bfloat16)
    attn_low[...] = attn_in
    mlp_low[...] = mlp_in
    count, lanes = w_qkv.shape[1], projected.shape[1]
    if lanes > count:
        projected[...] = jnp.zeros(projected.shape, jnp.float32)
    projected[:, :count] = product(attn_in, w_qkv[...]) + b_qkv[...]
    d_attended[...] = times_trans(cotangent[...], w_out[...]).astype(jnp.bfloat16)
    pre_act = product(mlp_in, w_up[...]) + b_up[...]
    below = 0.5 * (1.0 + lax.erf(pre_act * (0.5**0.5)))
    bell = jnp.exp(-0.5 * pre_act * pre_act) * ((2.0 * math.pi) ** -0.5)
    hidden[...] = (pre_act * below).astype(jnp.bfloat16)
    slope[...] = (below + pre_act * bell).astype(slope.dtype)


def forward(tokens, cotangent, vectors, w_qkv, b_qkv, w_out, w_up, b_up, lanes):
    rows, width = tokens.shape
    tile = rows // 4
    fixed = (*vectors, w_qkv, b_qkv, w_out, w_up, b_up)
    outs = (
        (width, jnp.bfloat16),
        (width, jnp.bfloat16),
        (lanes, jnp.float32),
        (w_out.shape[0], jnp.bfloat16),
        (w_up.shape[1], jnp.bfloat16),
        (w_up.shape[1], jnp.float32),
    )
    return pl.pallas_call(
        forward_kernel,
        grid=(4,),
        in_specs=[tiled(width, tile)] * 2 + [whole(array) for array in fixed],
        out_specs=tuple(tiled(wide, tile) for wide, _ in outs),
        out_shape=tuple(jax.ShapeDtypeStruct((rows, wide), kind) for wide, kind in outs),
        compiler_params=PARAMS,
    )(tokens, cotangent, *fixed)


def feed_back_kernel(
    tokens, cotangent, slope, w_down, w_up, mlp_gain, d_pre, scaled, sums, bias_sum
):
    @pl.when(pl.program_id(0) == 0)
    def _():
        sums[...] = jnp.zeros(sums.shape, jnp.float32)
        bias_sum[...] = jnp.zeros(bias_sum.shape, jnp.float32)

    d_low = (times_trans(cotangent[...], w_down[...]) * slope[...]).astype(jnp.bfloat16)
    d_pre[...] = d_low
    d_in = times_trans(d_low, w_up[...])
    scaled[...] = d_in * mlp_gain[...]
    normed, _ = normed_rows(tokens[...])
    sums[0:1, :] += jnp.sum(d_in * normed, axis=0, keepdims=True)
    sums[1:2, :] += jnp.sum(d_in, axis=0, keepdims=True)
    bias_sum[...] += jnp.sum(d_low.astype(jnp.float32), axis=0, keepdims=True)


def feed_back(tokens, cotangent, slope, w_down, w_up, mlp_gain):
    rows, width = tokens.shape
    inner = w_up.shape[1]
    tile = rows // 4
    fixed = (w_down, w_up, mlp_gain)
    shape = jax.ShapeDtypeStruct
    out_shape = (
        shape((rows, inner), jnp.bfloat16),
        shape((rows, width), jnp.float32),
        shape((2, width), jnp.float32),
        shape((1, inner), jnp.float32),
    )
    return pl.pallas_call(
        feed_back_kernel,
        grid=(4,),
        in_specs=[tiled(width, tile)] * 2 + [tiled(inner, tile)] + [whole(a) for a in fixed],
        out_specs=(tiled(inner, tile), tiled(width, tile)) + tuple(whole(a) for a in out_shape[2:]),
        out_shape=out_shape,
        compiler_params=PARAMS,
    )(tokens, cotangent, slope, *fixed)


def quarter_outs(rows, width):
    shape = jax.ShapeDtypeStruct((rows // 4, width), jnp.float32)
    return (shape,) * 4


def branches_kernel(tiles, attended, hidden, w_out, w_down, *outs):
    total = product(attended[...], w_out[...]) + product(hidden[...], w_down[...])
    for number, out in enumerate(outs):

        @pl.when(pl.program_id(0) == number)
        def _(out=out):
            out[...] = total


def picked(i, tiles):
    return tiles[i]


def branches(tiles, attended, hidden, w_out, w_down):
    rows, width = hidden.shape[0], w_down.shape[1]
    outs = quarter_outs(rows, width)
    return pl.pallas_call(
        branches_kernel,
        grid_spec=pltpu.PrefetchScalarGridSpec(
            num_scalar_prefetch=1,
            grid=(4,),
            in_specs=[
                tiled(attended.shape[1], rows // 4, picked),
                tiled(hidden.shape[1], rows // 4, picked),
                whole(w_out),
                whole(w_down),
            ],
            out_specs=tuple(whole(out) for out in outs),
        ),
        out_shape=outs,
        compiler_params=PARAMS,
    )(tiles, attended, hidden, w_out, w_down)


def input_back_kernel(count, heads_wide, tiles, *refs):
    d_heads, rest = refs[:count], refs[count:]
    tokens, cotangent, before, w_qkv, attn_gain = rest[:5]
    outs, (sums, bias_sum, branch_sum) = rest[5:9], rest[9:]

    @pl.when(pl.program_id(0) == 0)
    def _():
        for held in (sums, bias_sum, branch_sum):
            held[...] = jnp.zeros(held.shape, jnp.float32)

    d_in = None
    for number, part in enumerate(d_heads):
        columns = slice(number * heads_wide, (number + 1) * heads_wide)
        low = part[:, :heads_wide]
        term = times_trans(low, w_qkv[:, columns])
        d_in = term if d_in is None else d_in + term
        bias_sum[:, columns] += jnp.sum(low.astype(jnp.float32), axis=0, keepdims=True)
    normed, _ = normed_rows(tokens[...])
    sums[0:1, :] += jnp.sum(d_in * normed, axis=0, keepdims=True)
    sums[1:2, :] += jnp.sum(d_in, axis=0, keepdims=True)
    branch_sum[...] += jnp.sum(cotangent[...].astype(jnp.float32), axis=0, keepdims=True)
    total = d_in * attn_gain[...] + before[...]
    for number, out in enumerate(outs):

        @pl.when(pl.program_id(0) == number)
        def _(out=out):
            out[...] = total


def input_back(tiles, d_heads, heads_wide, tokens, cotangent, before, w_qkv, attn_gain):
    rows, width = tokens.shape
    tile = rows // 4
    shape = jax.ShapeDtypeStruct
    outs = quarter_outs(rows, width) + (
        shape((2, width), jnp.float32),
        shape((1, w_qkv.shape[1]), jnp.float32),
        shape((1, width), jnp.float32),
    )
    return pl.pallas_call(
        functools.partial(input_back_kernel, len(d_heads), heads_wide),
        grid_spec=pltpu.PrefetchScalarGridSpec(
            num_scalar_prefetch=1,
            grid=(4,),
            in_specs=[tiled(part.shape[1], tile, picked) for part in d_heads]
            + [tiled(width, tile, picked)] * 3
            + [whole(w_qkv), whole(attn_gain)],
            out_specs=tuple(whole(out) for out in outs),
        ),
        out_shape=outs,
        compiler_params=PARAMS,
    )(tiles, *d_heads, tokens, cotangent, before, w_qkv, attn_gain)


def gradient_kernel(wide, tiles, first_mat, *refs):
    parts, outs = refs[:-2], refs[-2:]
    for number, part in enumerate(parts):
        block = inner_rows(first_mat[...], part[:, :wide])
        columns = slice(number * wide, (number + 1) * wide)
        for side, out in enumerate(outs):

            @pl.when(pl.program_id(0) // (pl.num_programs(0) // 2) == side)
            def _(out=out, block=block, columns=columns):
                out[:, columns] = block


def gradient(swapped, first_mat, parts, wide, begin=0, rows=None):
    count = first_mat.shape[0]
    rows = rows or first_mat.shape[1]
    steps = 4 if rows >= 1024 else 2
    tile = rows // steps
    half = steps // 2
    columns = wide * len(parts)
    if tile % 128:
        full = inner_rows(
            first_mat[:, begin : begin + rows],
            jnp.concatenate([part[:, :wide] for part in parts], axis=1),
        )
        return tuple(
            lax.dynamic_slice_in_dim(full, side * (rows // 2), rows // 2, 0)
            for side in (swapped, 1 - swapped)
        )
    tiles = (jnp.arange(steps, dtype=jnp.int32) + swapped * half) % steps + begin // tile
    out = jax.ShapeDtypeStruct((rows // 2, columns), jnp.float32)
    return pl.pallas_call(
        functools.partial(gradient_kernel, wide),
        grid_spec=pltpu.PrefetchScalarGridSpec(
            num_scalar_prefetch=1,
            grid=(steps,),
            in_specs=[pl.BlockSpec((count, tile), lambda i, tiles: (0, tiles[i]))]
            + [whole(part) for part in parts],
            out_specs=(
                tiled(columns, tile, lambda i, tiles: jnp.minimum(i, half - 1)),
                tiled(columns, tile, lambda i, tiles: jnp.maximum(i - half, 0)),
            ),
        ),
        out_shape=(out, out),
        compiler_params=PARAMS,
    )(tiles, first_mat, *parts)


def float_shape(rows, width):
    return jax.ShapeDtypeStruct((rows, width), jnp.float32)


def steps_for(rows):
    return 4 if rows % 512 == 0 else 2 if rows % 16 == 0 else 1


def scalars(*values):
    return jnp.stack([jnp.asarray(value, jnp.int32) for value in values])


def add_kernel(first, second, out):
    out[...] = first[...] + second[...]


def add(first, second):
    rows, width = first.shape
    steps = steps_for(rows)
    spec = tiled(width, rows // steps)
    return pl.pallas_call(
        add_kernel,
        grid=(steps,),
        in_specs=[spec] * 2,
        out_specs=spec,
        out_shape=float_shape(rows, width),
        compiler_params=SMALL,
    )(first, second)


def choose_kernel(flag, first, second, out):
    @pl.when(flag[0] == 1)
    def _():
        out[...] = first[...]

    @pl.when(flag[0] == 0)
    def _():
        out[...] = second[...]


def choose(flag, first, second):
    rows, width = first.shape
    steps = steps_for(rows)
    spec = tiled(width, rows // steps)
    return pl.pallas_call(
        choose_kernel,
        grid_spec=pltpu.PrefetchScalarGridSpec(
            num_scalar_prefetch=1, grid=(steps,), in_specs=[spec] * 2, out_specs=spec
        ),
        out_shape=float_shape(rows, width),
        compiler_params=SMALL,
    )(scalars(flag), first, second)


def add_parts_kernel(first, second, *outs):
    total = first[...] + second[...]
    for number, out in enumerate(outs):

        @pl.when(pl.program_id(0) == number)
        def _(out=out):
            out[...] = total


def add_parts(first, second, parts):
    rows, width = first.shape
    outs = (float_shape(rows // parts, width),) * parts
    spec = tiled(width, rows // parts)
    return pl.pallas_call(
        add_parts_kernel,
        grid=(parts,),
        in_specs=[spec] * 2,
        out_specs=tuple(whole(out) for out in outs),
        out_shape=outs,
        compiler_params=SMALL,
    )(first, second)


def add_split_kernel(mine, first, second, away, keep):
    total = first[...] + second[...]

    @pl.when(pl.program_id(0) == 0)
    def _():
        away[...] = total

    @pl.when(pl.program_id(0) == 1)
    def _():
        keep[...] = total


def add_split(mine, first, second):
    rows, width = first.shape
    outs = (float_shape(rows // 2, width),) * 2
    spec = tiled(width, rows // 2, lambda i, mine: (i + 1 + mine[0]) % 2)
    return pl.pallas_call(
        add_split_kernel,
        grid_spec=pltpu.PrefetchScalarGridSpec(
            num_scalar_prefetch=1,
            grid=(2,),
            in_specs=[spec] * 2,
            out_specs=tuple(whole(out) for out in outs),
        ),
        out_shape=outs,
        compiler_params=SMALL,
    )(scalars(mine), first, second)


def norm_back_kernel(at, first, second, tokens, cotangent, out):
    rows = first[...] + second[...]
    normed, scale_inv = normed_rows(tokens[...])
    out[...] = cotangent[...].astype(jnp.float32) + scale_inv * (
        rows
        - jnp.mean(rows, axis=-1, keepdims=True)
        - normed * jnp.mean(rows * normed, axis=-1, keepdims=True)
    )


def norm_back(first, second, at, tokens, cotangent):
    rows, width = first.shape
    spec = pl.BlockSpec((rows, width), lambda i, at: (0, 0))
    moved = pl.BlockSpec((rows, width), lambda i, at: (at[0], 0))
    return pl.pallas_call(
        norm_back_kernel,
        grid_spec=pltpu.PrefetchScalarGridSpec(
            num_scalar_prefetch=1,
            grid=(1,),
            in_specs=[spec, spec, moved, moved],
            out_specs=spec,
        ),
        out_shape=float_shape(rows, width),
        compiler_params=SMALL,
    )(scalars(at // rows), first, second, tokens, cotangent)


def join_kernel(mine, own, other, out):
    @pl.when(pl.program_id(0) == mine[0])
    def _():
        out[...] = own[...]

    @pl.when(pl.program_id(0) != mine[0])
    def _():
        out[...] = other[...]


def join(mine, own, other):
    rows, width = own.shape
    return pl.pallas_call(
        join_kernel,
        grid_spec=pltpu.PrefetchScalarGridSpec(
            num_scalar_prefetch=1,
            grid=(2,),
            in_specs=[pl.BlockSpec((rows, width), lambda i, mine: (0, 0))] * 2,
            out_specs=tiled(width, rows, lambda i, mine: i),
        ),
        out_shape=float_shape(2 * rows, width),
        compiler_params=SMALL,
    )(scalars(mine), own, other)


def collect_kernel(count, order, *refs):
    parts, out = refs[:count], refs[-1]
    extra = refs[count:-1]
    for number, part in enumerate(parts):

        @pl.when(order[pl.program_id(0)] == number)
        def _(part=part):
            if extra:
                tokens, bias = extra
                total = tokens[...].astype(jnp.float32) + part[...] + bias[...]
                out[...] = total.astype(out.dtype)
            else:
                out[...] = part[...]


def collect(order, parts, *extra):
    rows, width = parts[0].shape
    count = len(parts)
    specs = [pl.BlockSpec((rows, width), lambda i, order: (0, 0))] * count
    if extra:
        specs = specs + [tiled(width, rows, lambda i, order: i), whole(extra[1])]
    return pl.pallas_call(
        functools.partial(collect_kernel, count),
        grid_spec=pltpu.PrefetchScalarGridSpec(
            num_scalar_prefetch=1,
            grid=(count,),
            in_specs=specs,
            out_specs=tiled(width, rows, lambda i, order: i),
        ),
        out_shape=jax.ShapeDtypeStruct(
            (count * rows, width), extra[0].dtype if extra else jnp.float32
        ),
        compiler_params=SMALL,
    )(order, *parts, *extra)


class Order:
    def __init__(self, token):
        self.token = token

    def tie(self, *arrays):
        tied = lax.optimization_barrier((self.token, *arrays))
        self.token = tied[0]
        return tied[1] if len(arrays) == 1 else tied[1:]

    def run(self, step, *arrays):
        tied = lax.optimization_barrier((self.token, *arrays))
        out = step(*tied[1:])
        out = tuple(out) if isinstance(out, list) else out
        if isinstance(out, tuple):
            return self.tie(*out)
        return self.tie(out)


class Chain:
    def __init__(self, order, steps):
        self.order, self.steps, self.out, self.held = order, steps, None, None
        self._go(None)

    def _go(self, arrived):
        try:
            array, axis, pairs = self.steps.send(arrived)
        except StopIteration as stop:
            self.held, self.out = None, stop.value
            return
        array = self.order.tie(array)
        self.held = lax.ppermute(array, axis, pairs)

    def on(self):
        if self.held is not None:
            self._go(self.order.tie(self.held))
        return self

    def end(self):
        while self.held is not None:
            self.on()
        return self.out


def swap_pairs(size, bit):
    return [(i, i ^ bit) for i in range(size)]


def tensor_steps(away, keep, size, order, finish):
    place = lax.axis_index("tensor")
    first = 0
    rows = away.shape[0]
    for number, bit in enumerate(order):
        got = yield away, "tensor", swap_pairs(size, bit)
        first = first + (place // bit) % 2 * rows
        if number + 1 < len(order):
            away, keep = add_split((place // order[number + 1]) % 2, keep, got)
            rows = rows // 2
    array = finish(keep, got, first)
    for number, bit in enumerate(reversed(order)):
        got = yield array, "tensor", swap_pairs(size, bit)
        if number + 1 < len(order):
            array = join((place // bit) % 2, array, got)
    return array, got


def core_steps(parts, size, chunks):
    away, keep = parts
    got = yield away, "dp", swap_pairs(size, 1)
    return add_parts(keep, got, chunks)


def line_steps(array, size):
    chips = size // 2
    place = lax.axis_index("dp") // 2

    def pairs(moves):
        return [(2 * a + c, 2 * b + c) for a, b in moves for c in range(2)]

    if chips > 1:
        steps = range(chips // 2 - 1)
        for s in steps:
            got = yield array, "dp", pairs([(s, s + 1), (chips - 1 - s, chips - 2 - s)])
            array = add(array, got)
        middle = chips // 2
        got = yield array, "dp", pairs([(middle - 1, middle), (middle, middle - 1)])
        array = add(array, got)
        for s in reversed(steps):
            got = yield array, "dp", pairs([(s + 1, s), (chips - 2 - s, chips - 1 - s)])
            array = choose((place == s) | (place == chips - 1 - s), got, array)
    got = yield array, "dp", swap_pairs(size, 1)
    return array, got


def add_end(keep, got, first):
    return add(keep, got)


def small_steps(stats, size):
    for bit in (1 << k for k in range(size.bit_length() - 1)):
        got = yield stats, "tensor", swap_pairs(size, bit)
        stats = stats + got
    return stats


def assemble(core, parts):
    low = [jnp.where(core == 0, mine, other) for mine, other in parts]
    high = [jnp.where(core == 0, other, mine) for mine, other in parts]
    return jnp.concatenate(low + high, axis=0)


def shards(
    dp_size,
    tensor_size,
    tokens,
    segment,
    attn_gain,
    attn_shift,
    mlp_gain,
    mlp_shift,
    w_qkv,
    b_qkv,
    w_out,
    w_up,
    b_up,
    w_down,
    b_branch,
    cotangent,
):
    rows_here, width = tokens.shape
    heads = w_qkv.shape[1] // (3 * HD)
    group = 2 if heads % 2 == 0 else heads
    wide = 3 * HD * group
    lanes = -(-wide // 128) * 128
    groups = heads // group
    bits = [1 << k for k in range(tensor_size.bit_length() - 1)]
    orders = (bits, bits[::-1])
    split = rows_here // 2
    core = lax.axis_index("dp") % 2
    place = lax.axis_index("tensor")
    order = Order(core)
    run = order.run
    mine = [(place // its[0]) % 2 for its in orders]
    tiles = jnp.stack([1 - mine[0], 3 - mine[1], mine[0], 2 + mine[1]]).astype(jnp.int32)

    def chain(steps):
        return Chain(order, steps)

    def lines(core_chain):
        return [line_steps(part, dp_size) for part in core_chain.end()]

    def grads(chunks, first_mat, *parts, wide=None, begin=0, rows=None):
        def step(first_mat, *parts):
            return gradient(1 - core, first_mat, parts, wide or parts[0].shape[1], begin, rows)

        return chain(core_steps(run(step, first_mat, *parts), dp_size, chunks))

    vectors = [v[None, :] for v in (attn_gain, attn_shift, mlp_gain, mlp_shift)]
    angles = run(turn_angles, segment[0])
    attn_low, mlp_low, projected, d_attended, hidden, slope = run(
        lambda *a: forward(a[0], a[1], vectors, *a[2:], lanes=lanes * groups),
        tokens,
        cotangent,
        w_qkv,
        b_qkv[None, :],
        w_out,
        w_up,
        b_up[None, :],
    )
    core_down = grads(1, hidden, cotangent)
    d_pre, scaled_mlp, sums_mlp, up_bias = run(
        feed_back, tokens, cotangent, slope, w_down, w_up, mlp_gain[None, :]
    )
    down = chain(lines(core_down)[0])
    core_up = grads(1, mlp_low, d_pre)
    kept = run(functools.partial(attend, heads=heads), angles, projected)
    attended = kept[0]
    partial = run(branches, tiles, attended, hidden, w_out, w_down)
    result = [
        chain(tensor_steps(partial[p], partial[2 + p], tensor_size, orders[p], add_end))
        for p in range(2)
    ]
    up = lines(core_up)[0]
    back = []
    for begin in range(0, heads, group):
        def step(angles, d_attended, *kept, begin=begin):
            return attend_back(angles, kept, d_attended, begin, group, lanes)

        back.append(run(step, angles, d_attended, *kept))
    for part in result:
        part.on()
    down.on()
    up = chain(up)
    *scaled, sums_attn, qkv_bias, branch_sum = run(
        lambda tiles, *a: input_back(tiles, a[:-5], wide, *a[-5:]),
        tiles,
        *back,
        tokens,
        cotangent,
        scaled_mlp,
        w_qkv,
        attn_gain[None, :],
    )
    core_qkv = grads(1, attn_low, *back, wide=wide)
    for part in result:
        part.on()
    grad_out = run(inner_rows, attended, cotangent)
    qkv = lines(core_qkv)[0]
    down.on()
    up.on()
    qkv = chain(qkv)
    for part in result:
        part.on()
    small = chain(small_steps(jnp.concatenate([sums_attn, sums_mlp], axis=0), tensor_size))
    small.on()
    stats = small.end()

    sizes = (width,) * 4 + (w_qkv.shape[1], w_up.shape[1], width)
    ends = [sum(sizes[: k + 1]) for k in range(len(sizes))]
    flat = jnp.concatenate([stats.reshape(-1), qkv_bias[0], up_bias[0], branch_sum[0]])
    spare = -(-flat.shape[0] // width // 16) * 16
    flat = jnp.pad(flat, (0, spare * width - flat.shape[0])).reshape(spare, width)

    def pack(grad_out, flat):
        packed = jnp.concatenate([grad_out, flat], axis=0)
        rows = packed.shape[0] // 2
        return tuple(
            lax.dynamic_slice_in_dim(packed, side * rows, rows, 0) for side in (1 - core, core)
        )

    core_out = chain(core_steps(run(pack, grad_out, flat), dp_size, 1))

    def back_end(part):
        def finish(keep, got, first):
            return norm_back(keep, got, first + part * split, tokens, cotangent)

        return finish

    out = lines(core_out)[0]
    spots = scalars(mine[0], 1 - mine[0], 2 + mine[1], 3 - mine[1])
    ended = [part.end() for part in result]
    d_tokens = [
        chain(tensor_steps(scaled[p], scaled[2 + p], tensor_size, orders[p], back_end(p)))
        for p in range(2)
    ]
    for part in d_tokens:
        part.on()
    result = run(collect, spots, [*ended[0], *ended[1]], tokens, b_branch[None, :])
    for part in (down, up, qkv):
        part.on()
    out = chain(out)
    for part in d_tokens:
        part.on()
    down.end()
    for part in d_tokens:
        part.on()
    core_spots = scalars(core, 1 - core)
    grad_down = run(collect, core_spots, [*down.end()])
    for part in (out, qkv, up):
        part.on()
    ended = [part.end() for part in d_tokens]
    d_tokens = run(collect, spots, [*ended[0], *ended[1]])
    up.end()
    grad_up = run(collect, core_spots, [*up.end()])
    out.on()
    qkv.on()
    out.on()
    qkv.end()
    grad_qkv = run(collect, core_spots, [*qkv.end()])
    packed = order.tie(assemble(core, (out.end(),)))
    grad_out = packed[: w_out.shape[0]]
    vectors = packed[w_out.shape[0] :].reshape(-1)
    a_gain, a_shift, m_gain, m_shift, qkv_bias, up_bias, branch = (
        vectors[end - size : end] for end, size in zip(ends, sizes, strict=True)
    )
    return (
        result,
        d_tokens,
        grad_qkv,
        qkv_bias,
        grad_out,
        grad_up,
        up_bias,
        grad_down,
        branch,
        a_gain,
        a_shift,
        m_gain,
        m_shift,
    )


def solution(mesh):
    placed = (
        P("dp", None),
        P("dp", None),
        P(),
        P(),
        P(),
        P(),
        P(None, "tensor"),
        P("tensor"),
        P("tensor", None),
        P(None, "tensor"),
        P("tensor"),
        P("tensor", None),
        P(),
        P("dp", None),
    )

    def body(*arrays):
        return shards(mesh.shape["dp"], mesh.shape["tensor"], *arrays)

    return jax.shard_map(
        body,
        mesh=mesh,
        in_specs=placed,
        out_specs=(
            P("dp", None),
            P("dp", None),
            P(None, "tensor"),
            P("tensor"),
            P("tensor", None),
            P(None, "tensor"),
            P("tensor"),
            P("tensor", None),
            P(),
            P(),
            P(),
            P(),
            P(),
        ),
        check_vma=False,
    )
```
